32 devices in a mesh: grp: 2 (over y), col: 4 (over z), freq: 2 (over x), rep: 2 (over core).
Axes of the slice: x: 2, y: 2, z: 4, core: 2. Of those that a mesh axis runs over, the one named last changes fastest.
Arguments:
- focusing: float32 [2, 2, 512, 16384], P('freq', None, ('grp', 'rep'), 'col'), parts along dimension 2, may hold values from -6 to 6
- v_factors: bfloat16 [2, 2, 384, 16384], P('freq', None, None, 'col'), may hold values from -0.1875 to 0.1875
- u_factors: bfloat16 [2, 2, 16, 384, 1024], P('freq', None, 'col'), may hold values from -0.3125 to 0.3125
- tile_ranks: int32 [16, 16], replicated, may hold values from 1 to 24
- owners: int32 [16], replicated, may hold values from 0 to 3, as said below
- onsets: int32 [16384], replicated, may hold values from 64 to 511
Outputs:
- update: float32 [2, 2, 512, 16384], P('freq', None, ('grp', 'rep'), 'col'), parts along dimension 2
The draws below stay inside these ranges and needn't reach their ends.
There are 2 independent parts, one for each index of `grp`. The reference program is written for one: setup_inputs(seed, part) draws one part's arguments, and reference() takes and returns one part's arrays. A program takes and returns all parts, laid end to end along the dimension named above; an argument that names none is the same for every part. Nothing has to cross between parts.
Inputs may be any that keep to these rules, and one draw needn't show every extreme that they name: `owners`: no owner holds more than 4 row tiles, and some owner holds exactly 4; the factors of row tile I stand in slot slot[I] of u_factors as the steps define it.
All inputs are finite; a program needn't handle non-finite values.
Results may differ from the reference program's by a relative error of at most 0.0062.
Values may be sent and summed in bfloat16 or wider, within the bound.
No kernel may reach another device: no remote copies, remote signals or barrier semaphores. Data moves between devices by JAX's collectives and lax.ppermute only.
A program may use at most 64 MiB of HBM per device.

```python
import jax
import jax.numpy as jnp
from jax import lax

TS = 1024
R = 24
NR = 16384
NS = 16384
NT = 512
KLO = 8
NF = 2
NV = 256
NRT = 16
NST = 16
BW = 1024
CAP = 4
SLOTS = 16


def draw_owners(key, part):
    key_order, key_rest, key_tiles = jax.random.split(jax.random.fold_in(key, 11), 3)
    owner_count = SLOTS // CAP
    order = jax.random.permutation(key_order, owner_count).astype(jnp.int32)
    others = jax.random.permutation(key_rest, SLOTS - CAP)[:NRT - CAP].astype(jnp.int32)
    first = jnp.full((CAP,), order[0], jnp.int32)
    remaining = order[1 + others // CAP]
    listed = jnp.concatenate([first, remaining]).astype(jnp.int32)
    tile_order = jax.random.permutation(key_tiles, NRT).astype(jnp.int32)
    return jnp.zeros((NRT,), jnp.int32).at[tile_order].set(listed)


def set_ends(array, key, least, largest):
    index_at = [jax.random.randint(jax.random.fold_in(key, axis), (), 0, length) for axis, length in enumerate(array.shape)]
    widest = array.shape.index(max(array.shape))
    neighbour = index_at[:widest] + [(index_at[widest] + 1) % array.shape[widest]] + index_at[widest + 1:]
    return array.at[tuple(index_at)].set(least).at[tuple(neighbour)].set(largest)


def block_scale(own_key, dims, cuts, least, largest):
    level = 1.0
    for dim, shards_of in cuts:
        steps = jax.random.uniform(jax.random.fold_in(jax.random.fold_in(own_key, 6), dim), (shards_of,), jnp.float32, least / len(cuts), largest / len(cuts))
        level = level * jnp.repeat(jnp.exp(steps), dims[dim] // shards_of).reshape((-1,) + (1,) * (len(dims) - 1 - dim))
    return level


def normal_values(stream_key, extent, scale, most, cuts=(), held_as=jnp.bfloat16):
    entries = jax.random.normal(stream_key, extent, jnp.float32) * scale
    if len(cuts) > 0:
        entries = block_scale(stream_key, extent, cuts, -0.22, 0.18) * entries
    return jnp.clip(entries, min=-most, max=most).astype(held_as)


def setup_inputs(seed: int = 0, part: int = 0) -> dict:
    key_list = jax.random.split(jax.random.key(seed), 7)
    part_splits = jax.random.split(jax.random.fold_in(key_list[6], part), 7)
    focusing = normal_values(part_splits[0], (NF, 2, NV, NS), 1.0, 6.0, ((0, 2), (2, 2), (3, 4)), jnp.float32)
    v_factors = normal_values(key_list[1], (NF, 2, NRT * R, NS), TS ** -0.5, 0.1875, ((0, 2), (3, 4)))
    u_factors = normal_values(key_list[2], (NF, 2, SLOTS, NST * R, TS), (NST * R) ** -0.5, 0.3125, ((0, 2), (2, 4)))
    tile_ranks = set_ends(jax.random.randint(key_list[3], (NRT, NST), 1, R + 1), jax.random.fold_in(key_list[3], 1), 1, R).astype(jnp.int32)
    owners = draw_owners(jax.random.fold_in(key_list[6], 71), part)
    onsets = set_ends(jax.random.randint(key_list[5], (NR,), NT // 8, NT), jax.random.fold_in(key_list[5], 1), NT // 8, NT - 1).astype(jnp.int32)
    return {"focusing": focusing, "v_factors": v_factors, "u_factors": u_factors, "tile_ranks": tile_ranks, "owners": owners, "onsets": onsets}


def window_tables(count_freq, onset_rows):
    time_steps = jnp.arange(NT, dtype=jnp.int32)
    freq_bins = KLO + jnp.arange(count_freq, dtype=jnp.int32)
    phases = 2.0 * jnp.pi * ((freq_bins[None, :] * time_steps[:, None]) % NT).astype(jnp.float32) / NT
    cosine = jnp.cos(phases)
    sines = jnp.sin(phases)
    analyse = jnp.stack([cosine, -sines], axis=2).reshape(NT, 2 * count_freq)
    synthesis = analyse * (2.0 / NT)
    product_table = (analyse[:, :, None] * synthesis[:, None, :]).reshape(NT, 4 * count_freq * count_freq)
    running_table = jnp.cumsum(product_table, axis=0)
    mixing = jnp.take(running_table, (onset_rows - 1).astype(jnp.int32), axis=0)
    return mixing.reshape(-1, 2 * count_freq, 2 * count_freq)


def settle(values):
    return lax.optimization_barrier(values.astype(jnp.bfloat16)).astype(jnp.float32)


def kernel_product(einsum_recipe, left_side, right_side):
    return jnp.einsum(einsum_recipe, left_side, right_side, precision=lax.Precision.HIGHEST)


def reference(focusing, v_factors, u_factors, tile_ranks, owners, onsets):
    row_tiles = NR // TS
    col_tiles = NS // TS
    all_blocks = NS // BW
    per_tile = TS // BW
    focus_low = settle(focusing).reshape(NF, 2, NV, all_blocks, BW)
    factors_v = v_factors.astype(jnp.float32).reshape(NF, 2, row_tiles, R, all_blocks, BW)
    einsum_recipe = "fikbs,fvbs->ifbkv"
    real_portion = kernel_product(einsum_recipe, factors_v[:, 0], focus_low[:, 0]) - kernel_product(einsum_recipe, factors_v[:, 1], focus_low[:, 1])
    part_imag = kernel_product(einsum_recipe, factors_v[:, 0], focus_low[:, 1]) + kernel_product(einsum_recipe, factors_v[:, 1], focus_low[:, 0])
    partial_sums = settle(jnp.stack([real_portion, part_imag], axis=3))
    coefficients = jnp.sum(partial_sums.reshape(row_tiles, NF, col_tiles, per_tile, 2, R, NV), axis=3)
    rank_mask = (jnp.arange(R, dtype=jnp.int32)[None, None, :] < tile_ranks[:, :, None]).astype(jnp.float32)
    coefficients = settle(coefficients * rank_mask[:, None, :, None, :, None])
    tile_ids = jnp.arange(row_tiles, dtype=jnp.int32)
    same_owner = owners[:, None] == owners[None, :]
    earlier = tile_ids[None, :] < tile_ids[:, None]
    slot_of = jnp.sum((same_owner & earlier).astype(jnp.int32), axis=1)
    destination = (owners * CAP + slot_of).astype(jnp.int32)
    chosen = jnp.take(u_factors, destination, axis=2).astype(jnp.float32)
    chosen = chosen.reshape(NF, 2, row_tiles, col_tiles, R, TS)
    uform = "fijka,ifjkv->ifav"
    field_real = kernel_product(uform, chosen[:, 0], coefficients[:, :, :, 0]) - kernel_product(uform, chosen[:, 1], coefficients[:, :, :, 1])
    field_imag = kernel_product(uform, chosen[:, 0], coefficients[:, :, :, 1]) + kernel_product(uform, chosen[:, 1], coefficients[:, :, :, 0])
    receiver_field = settle(jnp.stack([field_real, field_imag], axis=2))
    mixing = window_tables(NF, onsets).reshape(row_tiles, TS, 2 * NF, 2 * NF)
    flat_field = receiver_field.reshape(row_tiles, 2 * NF, TS, NV)
    windowed = settle(kernel_product("itpq,iqtv->iptv", mixing, flat_field)).reshape(row_tiles, NF, 2, TS, NV)
    aform = "fijka,ifav->ifjkv"
    back_real = kernel_product(aform, chosen[:, 0], windowed[:, :, 0]) + kernel_product(aform, chosen[:, 1], windowed[:, :, 1])
    back_imag = kernel_product(aform, chosen[:, 0], windowed[:, :, 1]) - kernel_product(aform, chosen[:, 1], windowed[:, :, 0])
    adjoint = jnp.stack([back_real, back_imag], axis=3) * rank_mask[:, None, :, None, :, None]
    adjoint = settle(adjoint)
    spread = jnp.broadcast_to(adjoint[:, :, :, None], (row_tiles, NF, col_tiles, per_tile, 2, R, NV))
    spread = spread.reshape(row_tiles, NF, all_blocks, 2, R, NV)
    wform = "fikbs,ifbkv->fvbs"
    wave_real = kernel_product(wform, factors_v[:, 0], spread[:, :, :, 0]) + kernel_product(wform, factors_v[:, 1], spread[:, :, :, 1])
    wave_imag = kernel_product(wform, factors_v[:, 0], spread[:, :, :, 1]) - kernel_product(wform, factors_v[:, 1], spread[:, :, :, 0])
    wave_field = jnp.stack([wave_real, wave_imag], axis=1).reshape(NF, 2, NV, NS)
    return focusing - wave_field
```

```python
import functools

import jax
import jax.numpy as jnp
import ml_dtypes
import numpy as np
from jax import lax
from jax.experimental import pallas as pl
from jax.experimental.pallas import tpu as pltpu
from jax.sharding import PartitionSpec as P

TS = 1024
R = 24
NR = 16384
NS = 16384
NT = 512
KLO = 8


def window_tables(count_freq, onset_rows):
    time_steps = jnp.arange(NT, dtype=jnp.int32)
    freq_bins = KLO + jnp.arange(count_freq, dtype=jnp.int32)
    phases = 2.0 * jnp.pi * (freq_bins[None, :] * time_steps[:, None] % NT).astype(jnp.float32) / NT
    cosine = jnp.cos(phases)
    sines = jnp.sin(phases)
    analyse = jnp.stack([cosine, -sines], axis=2).reshape(NT, 2 * count_freq)
    synthesis = analyse * (2.0 / NT)
    product_table = (analyse[:, :, None] * synthesis[:, None, :]).reshape(
        NT, 4 * count_freq * count_freq
    )
    running_table = jnp.cumsum(product_table, axis=0)
    mixing = jnp.take(running_table, onset_rows - 1, axis=0)
    return mixing.reshape(-1, 2 * count_freq, 2 * count_freq)


def kernel_product(einsum_recipe, left_side, right_side):
    return jnp.einsum(einsum_recipe, left_side, right_side, preferred_element_type=jnp.float32)


def per_device_general(focusing, v_factors, u_factors, tile_ranks, owners, onsets):
    count_col = lax.axis_size("col")
    my_column = lax.axis_index("col")
    count_freq = lax.axis_size("freq")
    my_freq = lax.axis_index("freq")
    freq_dev = focusing.shape[0]
    vis_dev = focusing.shape[2]
    sources_dev = focusing.shape[3]
    capacity = u_factors.shape[2]
    block_width = min(sources_dev, TS)
    blocks_dev = sources_dev // block_width
    per_tile = TS // block_width
    all_blocks = count_col * blocks_dev
    row_tiles = NR // TS
    col_tiles = NS // TS
    freq_all = freq_dev * count_freq
    quarter = TS // count_freq
    tile_ids = jnp.arange(row_tiles, dtype=jnp.int32)
    same_owner = owners[:, None] == owners[None, :]
    earlier = tile_ids[None, :] < tile_ids[:, None]
    slot_of = jnp.sum((same_owner & earlier).astype(jnp.int32), axis=1)
    slot_ids = jnp.arange(capacity, dtype=jnp.int32)
    routing = (owners[None, None, :] == jnp.arange(count_col, dtype=jnp.int32)[:, None, None]) & (
        slot_of[None, None, :] == slot_ids[None, :, None]
    )
    lower_routing = routing.astype(jnp.bfloat16)
    my_slots = ((owners[None, :] == my_column) & (slot_of[None, :] == slot_ids[:, None])).astype(
        jnp.int32
    )
    slot_ranks = jnp.sum(my_slots[:, :, None] * tile_ranks[None, :, :], axis=1)
    rank_mask = (jnp.arange(R, dtype=jnp.int32)[None, None, :] < slot_ranks[:, :, None]).astype(
        jnp.float32
    )
    slot_onsets = jnp.sum(my_slots[:, :, None] * onsets.reshape(row_tiles, TS)[None], axis=1)
    slot_onsets = jnp.maximum(slot_onsets, 1)
    focus_low = focusing.astype(jnp.bfloat16).reshape(freq_dev, 2, vis_dev, blocks_dev, block_width)
    factors_v = v_factors.reshape(freq_dev, 2, row_tiles, R, blocks_dev, block_width)
    einsum_recipe = "fikbs,fvbs->ifbkv"
    real_portion = kernel_product(einsum_recipe, factors_v[:, 0], focus_low[:, 0]) - kernel_product(
        einsum_recipe, factors_v[:, 1], focus_low[:, 1]
    )
    part_imag = kernel_product(einsum_recipe, factors_v[:, 0], focus_low[:, 1]) + kernel_product(
        einsum_recipe, factors_v[:, 1], focus_low[:, 0]
    )
    partial_sums = jnp.stack([real_portion, part_imag], axis=3).astype(jnp.bfloat16)
    outgoing_parts = kernel_product("way,ymleno->amwleno", lower_routing, partial_sums).astype(
        jnp.bfloat16
    )
    outgoing_parts = outgoing_parts.reshape(capacity, freq_dev, all_blocks, 2, R, vis_dev)
    arrived = lax.all_to_all(outgoing_parts, "col", split_axis=2, concat_axis=2, tiled=True)
    coefficients = jnp.sum(
        arrived.astype(jnp.float32).reshape(capacity, freq_dev, col_tiles, per_tile, 2, R, vis_dev),
        axis=3,
    )
    coefficients = (coefficients * rank_mask[:, None, :, None, :, None]).astype(jnp.bfloat16)
    factors_u = u_factors.reshape(freq_dev, 2, capacity, col_tiles, R, TS)
    uform = "fcjka,cfjkv->cfav"
    field_real = kernel_product(uform, factors_u[:, 0], coefficients[:, :, :, 0]) - kernel_product(
        uform, factors_u[:, 1], coefficients[:, :, :, 1]
    )
    field_imag = kernel_product(uform, factors_u[:, 0], coefficients[:, :, :, 1]) + kernel_product(
        uform, factors_u[:, 1], coefficients[:, :, :, 0]
    )
    receiver_field = jnp.stack([field_real, field_imag], axis=2).astype(jnp.bfloat16)
    turned = lax.all_to_all(receiver_field, "freq", split_axis=3, concat_axis=1, tiled=True)
    quarter_onsets = lax.dynamic_slice_in_dim(slot_onsets, my_freq * quarter, quarter, 1)
    mixing = window_tables(freq_all, quarter_onsets.reshape(-1)).reshape(
        capacity, quarter, 2 * freq_all, 2 * freq_all
    )
    flat_field = turned.reshape(capacity, 2 * freq_all, quarter, vis_dev).astype(jnp.float32)
    mixed_field = jnp.einsum("crpq,cqrv->cprv", mixing, flat_field, precision=lax.Precision.HIGHEST)
    mixed_field = mixed_field.astype(jnp.bfloat16).reshape(capacity, freq_all, 2, quarter, vis_dev)
    windowed = lax.all_to_all(mixed_field, "freq", split_axis=1, concat_axis=3, tiled=True)
    aform = "fcjka,cfav->cfjkv"
    back_real = kernel_product(aform, factors_u[:, 0], windowed[:, :, 0]) + kernel_product(
        aform, factors_u[:, 1], windowed[:, :, 1]
    )
    back_imag = kernel_product(aform, factors_u[:, 0], windowed[:, :, 1]) - kernel_product(
        aform, factors_u[:, 1], windowed[:, :, 0]
    )
    adjoint = jnp.stack([back_real, back_imag], axis=3) * rank_mask[:, None, :, None, :, None]
    adjoint = adjoint.astype(jnp.bfloat16)
    spread = jnp.broadcast_to(
        adjoint[:, :, :, None], (capacity, freq_dev, col_tiles, per_tile, 2, R, vis_dev)
    )
    spread = spread.reshape(capacity, freq_dev, all_blocks, 2, R, vis_dev)
    result_field = lax.all_to_all(spread, "col", split_axis=2, concat_axis=2, tiled=True)
    result_field = result_field.reshape(capacity, freq_dev, count_col, blocks_dev, 2, R, vis_dev)
    row_share = kernel_product("prq,rjpagwu->qjagwu", lower_routing, result_field).astype(
        jnp.bfloat16
    )
    wform = "fikbs,ifbkv->fvbs"
    wave_real = kernel_product(wform, factors_v[:, 0], row_share[:, :, :, 0]) + kernel_product(
        wform, factors_v[:, 1], row_share[:, :, :, 1]
    )
    wave_imag = kernel_product(wform, factors_v[:, 0], row_share[:, :, :, 1]) - kernel_product(
        wform, factors_v[:, 1], row_share[:, :, :, 0]
    )
    wave_field = jnp.stack([wave_real, wave_imag], axis=1).reshape(
        freq_dev, 2, vis_dev, sources_dev
    )
    return focusing - wave_field


def mixing_table(count_freq):
    time_steps = np.arange(NT)
    rows = []
    for mine in range(count_freq):
        bins = [KLO + mine] + [KLO + f for f in range(count_freq) if f != mine]
        phases = 2.0 * np.pi * ((np.array(bins)[:, None] * time_steps[None, :]) % NT) / NT
        analyse = np.stack([np.cos(phases), -np.sin(phases)], axis=1).reshape(2 * count_freq, NT)
        table = (analyse[:, None, :] * analyse[None, :, :] * (2.0 / NT)).reshape(-1, NT)
        rest = table.astype(np.float32)
        parts = []
        for _ in range(3):
            part = rest.astype(ml_dtypes.bfloat16)
            parts.append(part)
            rest = rest - part.astype(np.float32)
        rows.append(np.concatenate(parts, axis=0))
    return np.stack(rows)


def dot(left, right, left_dim, right_dim):
    return lax.dot_general(
        left, right, (((left_dim,), (right_dim,)), ((), ())), preferred_element_type=jnp.float32
    )


def list_tiles(owners, tile_of, held, count_col, capacity):
    for owner in range(count_col):
        held[owner] = 0
    for tile in range(owners.shape[0]):
        owner = owners[tile]
        slot = held[owner]
        tile_of[owner * capacity + slot] = tile
        held[owner] = slot + 1


def forward_kernel(count_col, half, owners, ranks, focus, factors, *refs):
    outs = refs[: half * count_col]
    sums, tile_of, held = refs[half * count_col :]
    block = pl.program_id(0)
    blocks = pl.num_programs(0)
    column = lax.axis_index("col")
    mine = lax.axis_index("freq")
    two, vis, width = focus.shape[1:]
    low = focus[0].astype(jnp.bfloat16).reshape(two * vis, width)
    by_real = dot(factors[0, 0], low, 1, 1)
    by_imag = dot(factors[0, 1], low, 1, 1)
    sums[block] = jnp.concatenate(
        [by_real[:, :vis] - by_imag[:, vis:], by_real[:, vis:] + by_imag[:, :vis]], axis=1
    )

    @pl.when(block == blocks - 1)
    def _():
        capacity = 2 * half
        list_tiles(owners, tile_of, held, count_col, capacity)
        row_id = lax.broadcasted_iota(jnp.int32, (R, 2 * vis), 0)
        for s in range(half):
            for d in range(count_col):
                for e in range(2):
                    tile = tile_of[(column ^ d) * capacity + (mine ^ e) * half + s]
                    pieces = []
                    for j in range(sums.shape[0]):
                        rank = ranks[tile, column * sums.shape[0] + j]
                        piece = sums[j, pl.ds(pl.multiple_of(tile * R, 8), R), :]
                        pieces.append(jnp.where(row_id < rank, piece, 0.0))
                    outs[s * count_col + d][e] = jnp.concatenate(pieces, axis=0).astype(jnp.bfloat16)


def forward_products(count_col, half, focusing, v_factors, tile_ranks, owners):
    vis, sources = focusing.shape[2:]
    rows = v_factors.shape[2]
    blocks = sources // TS
    out = jax.ShapeDtypeStruct((2, blocks * R, 2 * vis), jnp.bfloat16)
    whole = pl.BlockSpec((2, blocks * R, 2 * vis), lambda j: (0, 0, 0))
    smem = pl.BlockSpec(memory_space=pltpu.SMEM)
    return pl.pallas_call(
        functools.partial(forward_kernel, count_col, half),
        grid=(blocks,),
        in_specs=[
            smem,
            smem,
            pl.BlockSpec((1, 2, vis, TS), lambda j: (0, 0, 0, j)),
            pl.BlockSpec((1, 2, rows, TS), lambda j: (0, 0, 0, j)),
        ],
        out_specs=[whole] * (half * count_col),
        out_shape=[out] * (half * count_col),
        scratch_shapes=[
            pltpu.VMEM((blocks, rows, 2 * vis), jnp.float32),
            pltpu.SMEM((count_col * 2 * half,), jnp.int32),
            pltpu.SMEM((count_col,), jnp.int32),
        ],
        compiler_params=pltpu.CompilerParams(
            dimension_semantics=("arbitrary",), vmem_limit_bytes=40 * 2**20
        ),
        cost_estimate=pl.CostEstimate(
            flops=8 * rows * vis * sources, bytes_accessed=8 * vis * sources + 4 * rows * sources, transcendentals=0
        ),
        name="forward_products",
    )(owners, tile_ranks, focusing, v_factors)


def receiver_kernel(count_col, half, chunk, owners, ranks, onsets, table, kept, *refs):
    others = refs[: count_col - 1]
    crossed, u_own, quarter_0, quarter_1, quarter_2, quarter_3 = refs[count_col - 1 : count_col + 5]
    outs = refs[count_col + 5 : 2 * count_col + 5]
    factors, coefs, field, windowed, tile_of, held, sems = refs[2 * count_col + 5 :]
    column = lax.axis_index("col")
    mine = lax.axis_index("freq")
    place = lax.axis_index("grp") * 2 + lax.axis_index("rep")
    vis = field.shape[1]
    rows = factors.shape[2]
    quarter = rows // 4
    copies = [
        pltpu.make_async_copy(u_own.at[0, :, mine * half + chunk], factors.at[0], sems.at[0])
    ]
    for n, ref in enumerate((quarter_0, quarter_1, quarter_2, quarter_3)):
        start = pl.multiple_of((place ^ n) * quarter, quarter)
        copies.append(
            pltpu.make_async_copy(ref, factors.at[1, :, pl.ds(start, quarter), :], sems.at[n + 1])
        )
    for copy in copies:
        copy.start()
    list_tiles(owners, tile_of, held, count_col, 2 * half)
    tile = tile_of[column * 2 * half + mine * half + chunk]
    strip = crossed.shape[1]
    for d in range(count_col):
        start = pl.multiple_of((column ^ d) * strip, strip)
        arrived = (kept if d == 0 else others[d - 1])[0]
        for e, values in enumerate((arrived, crossed[d])):
            coefs[e, 0, pl.ds(start, strip), :] = values
            coefs[e, 1, pl.ds(start, strip), :] = jnp.concatenate([-values[:, vis:], values[:, :vis]], axis=1)
    times = lax.broadcasted_iota(jnp.int32, (NT, TS), 0)
    inside = jnp.where(times < onsets[tile], 1.0, 0.0).astype(jnp.bfloat16)
    tables = dot(table[mine], inside, 1, 0)
    count = tables.shape[0] // 3
    mixing = tables[:count] + tables[count : 2 * count] + tables[2 * count :]
    for e in range(2):
        for copy in copies[:1] if e == 0 else copies[1:]:
            copy.wait()
        product = dot(coefs[e].reshape(2 * rows, 2 * vis), factors[e].reshape(2 * rows, TS), 0, 0)
        low = product.astype(jnp.bfloat16).astype(jnp.float32)
        field[2 * e] = low[:vis]
        field[2 * e + 1] = low[vis:]
    for p in range(4):
        total = mixing[4 * p : 4 * p + 1] * field[0]
        for q in range(1, 4):
            total = total + mixing[4 * p + q : 4 * p + q + 1] * field[q]
        windowed[p // 2, (p % 2) * vis : (p % 2 + 1) * vis, :] = total.astype(jnp.bfloat16)
    row_id = lax.broadcasted_iota(jnp.int32, (R, 2 * vis), 0)
    per_column = strip // R
    for e in range(2):
        back = dot(factors[e].reshape(2 * rows, TS), windowed[e], 1, 1)
        by_real, by_imag = back[:rows], back[rows:]
        adjoint = jnp.concatenate(
            [by_real[:, :vis] + by_imag[:, vis:], by_real[:, vis:] - by_imag[:, :vis]], axis=1
        )
        pieces = []
        for j in range(rows // R):
            pieces.append(jnp.where(row_id < ranks[tile, j], adjoint[j * R : (j + 1) * R], 0.0))
        coefs[e, 0] = jnp.concatenate(pieces, axis=0).astype(jnp.bfloat16)
        for d in range(count_col):
            start = pl.multiple_of((column ^ d) * strip, strip)
            outs[d][e] = coefs[e, 0, pl.ds(start, strip), :]


def receiver_products(count_col, half, chunk, owners, tile_ranks, onsets, table, arrived, crossed, u_factors, quarters):
    strip, columns = crossed.shape[1:]
    rows = u_factors.shape[3]
    vis = columns // 2
    smem = pl.BlockSpec(memory_space=pltpu.SMEM)
    vmem = pl.BlockSpec(memory_space=pltpu.VMEM)
    anywhere = pl.BlockSpec(memory_space=pl.ANY)
    out = jax.ShapeDtypeStruct((2, strip, columns), jnp.bfloat16)
    return pl.pallas_call(
        functools.partial(receiver_kernel, count_col, half, chunk),
        in_specs=[smem, smem, vmem, vmem] + [vmem] * (count_col + 1) + [anywhere] * 5,
        out_specs=[vmem] * count_col,
        out_shape=[out] * count_col,
        scratch_shapes=[
            pltpu.VMEM((2, 2, rows, TS), jnp.bfloat16),
            pltpu.VMEM((2, 2, rows, columns), jnp.bfloat16),
            pltpu.VMEM((4, vis, TS), jnp.float32),
            pltpu.VMEM((2, columns, TS), jnp.bfloat16),
            pltpu.SMEM((count_col * 2 * half,), jnp.int32),
            pltpu.SMEM((count_col,), jnp.int32),
            pltpu.SemaphoreType.DMA((5,)),
        ],
        compiler_params=pltpu.CompilerParams(vmem_limit_bytes=40 * 2**20),
        cost_estimate=pl.CostEstimate(
            flops=32 * rows * vis * TS, bytes_accessed=8 * rows * TS, transcendentals=0
        ),
        name="receiver_products",
    )(owners, tile_ranks, onsets, table, *arrived, crossed, u_factors, *quarters)


def update_kernel(count_col, half, owners, *refs):
    per = count_col + 1
    arrivals = [refs[s * per : (s + 1) * per] for s in range(half)]
    focus, factors, out, gathered, adjoint, tile_of, held = refs[half * per :]
    step = pl.program_id(0)
    column = lax.axis_index("col")
    mine = lax.axis_index("freq")
    two, vis, width = focus.shape[1:]
    rows = factors.shape[2]

    @pl.when(step == 0)
    def _():
        capacity = 2 * half
        list_tiles(owners, tile_of, held, count_col, capacity)
        for s in range(half):
            crossed = arrivals[s][count_col]
            for d in range(count_col):
                for e in range(2):
                    tile = tile_of[(column ^ d) * capacity + (mine ^ e) * half + s]
                    values = (arrivals[s][d][0] if e == 0 else crossed[d]).astype(jnp.float32)
                    for j in range(gathered.shape[0]):
                        gathered[j, pl.ds(pl.multiple_of(tile * R, 8), R), :] = values[j * R : (j + 1) * R]
        for j in range(gathered.shape[0]):
            values = gathered[j]
            adjoint[j, :rows] = values.astype(jnp.bfloat16)
            adjoint[j, rows:] = jnp.concatenate([values[:, vis:], -values[:, :vis]], axis=1).astype(jnp.bfloat16)

    block = step * width // TS
    wave = dot(adjoint[block], factors[0].reshape(2 * rows, width), 0, 0)
    out[0] = focus[0] - wave.reshape(two, vis, width)


def update_products(count_col, half, owners, arrivals, focusing, v_factors):
    vis, sources = focusing.shape[2:]
    rows = v_factors.shape[2]
    blocks = sources // TS
    width = 512
    smem = pl.BlockSpec(memory_space=pltpu.SMEM)
    specs = [smem]
    for group in arrivals:
        for array in group:
            specs.append(pl.BlockSpec(array.shape, lambda j: (0, 0, 0)))
    return pl.pallas_call(
        functools.partial(update_kernel, count_col, half),
        grid=(sources // width,),
        in_specs=specs
        + [
            pl.BlockSpec((1, 2, vis, width), lambda j: (0, 0, 0, j)),
            pl.BlockSpec((1, 2, rows, width), lambda j: (0, 0, 0, j)),
        ],
        out_specs=pl.BlockSpec((1, 2, vis, width), lambda j: (0, 0, 0, j)),
        out_shape=jax.ShapeDtypeStruct(focusing.shape, jnp.float32),
        scratch_shapes=[
            pltpu.VMEM((blocks, rows, 2 * vis), jnp.float32),
            pltpu.VMEM((blocks, 2 * rows, 2 * vis), jnp.bfloat16),
            pltpu.SMEM((count_col * 2 * half,), jnp.int32),
            pltpu.SMEM((count_col,), jnp.int32),
        ],
        compiler_params=pltpu.CompilerParams(
            dimension_semantics=("arbitrary",), vmem_limit_bytes=40 * 2**20
        ),
        cost_estimate=pl.CostEstimate(
            flops=8 * rows * vis * sources, bytes_accessed=16 * vis * sources + 4 * rows * sources, transcendentals=0
        ),
        name="update_products",
    )(owners, *[array for group in arrivals for array in group], focusing, v_factors)


def swap(array, axis):
    return lax.ppermute(array, axis, [(0, 1), (1, 0)])


def exchange_columns(arrays, count_col):
    moved = list(arrays)
    for d in range(count_col - 1, 0, -1):
        moved[d] = lax.ppermute(arrays[d], "col", [(i, i ^ d) for i in range(count_col)])
    return moved


def per_device_paired(focusing, v_factors, u_factors, tile_ranks, owners, onsets):
    count_col = lax.axis_size("col")
    mine = lax.axis_index("freq")
    capacity = u_factors.shape[2]
    half = capacity // 2
    rows = u_factors.shape[3]
    place = lax.axis_index("grp") * 2 + lax.axis_index("rep")
    table = jnp.asarray(mixing_table(2))
    tile_onsets = onsets.reshape(NR // TS, 1, TS)
    quarters = []
    for s in range(half):
        piece = lax.dynamic_slice(
            u_factors, (0, 0, (1 - mine) * half + s, place * (rows // 4), 0), (1, 2, 1, rows // 4, TS)
        ).reshape(2, rows // 4, TS)
        first = swap(piece, "freq")
        second = swap(first, "grp")
        quarters.append([first, swap(first, "rep"), second, swap(second, "rep")])
    outgoing = forward_products(count_col, half, focusing, v_factors, tile_ranks, owners)
    arrivals = []
    for s in range(half):
        arrived = exchange_columns(outgoing[s * count_col : (s + 1) * count_col], count_col)
        crossed = swap(jnp.stack([array[1] for array in arrived]), "freq")
        back = receiver_products(
            count_col, half, s, owners, tile_ranks, tile_onsets, table, arrived, crossed, u_factors, quarters[s]
        )
        returned = exchange_columns(back, count_col)
        arrivals.append(returned + [swap(jnp.stack([array[1] for array in returned]), "freq")])
    return update_products(count_col, half, owners, arrivals, focusing, v_factors)


def per_device(focusing, v_factors, u_factors, tile_ranks, owners, onsets):
    count_col = lax.axis_size("col")
    paired = (
        lax.axis_size("freq") == 2
        and lax.axis_size("grp") == 2
        and lax.axis_size("rep") == 2
        and focusing.shape[0] == 1
        and count_col & (count_col - 1) == 0
        and u_factors.shape[2] % 2 == 0
        and u_factors.shape[2] * count_col == NR // TS
        and focusing.shape[2] % 128 == 0
        and focusing.shape[3] % TS == 0
        and (focusing.shape[3] // TS * R) % 16 == 0
        and u_factors.shape[3] % 64 == 0
    )
    chosen = per_device_paired if paired else per_device_general
    return chosen(focusing, v_factors, u_factors, tile_ranks, owners, onsets)


def solution(mesh):
    return jax.shard_map(
        per_device,
        mesh=mesh,
        in_specs=(
            P("freq", None, ("grp", "rep"), "col"),
            P("freq", None, None, "col"),
            P("freq", None, "col", None, None),
            P(),
            P(),
            P(),
        ),
        out_specs=P("freq", None, ("grp", "rep"), "col"),
        check_vma=False,
    )
```

```python
import functools

import jax
import jax.numpy as jnp
import ml_dtypes
import numpy as np
from jax import lax
from jax.experimental import pallas as pl
from jax.experimental.pallas import tpu as pltpu
from jax.sharding import PartitionSpec as P

TS = 1024
R = 24
NR = 16384
NS = 16384
NT = 512
KLO = 8


def window_tables(count_freq, onset_rows):
    time_steps = jnp.arange(NT, dtype=jnp.int32)
    freq_bins = KLO + jnp.arange(count_freq, dtype=jnp.int32)
    phases = 2.0 * jnp.pi * (freq_bins[None, :] * time_steps[:, None] % NT).astype(jnp.float32) / NT
    cosine = jnp.cos(phases)
    sines = jnp.sin(phases)
    analyse = jnp.stack([cosine, -sines], axis=2).reshape(NT, 2 * count_freq)
    synthesis = analyse * (2.0 / NT)
    product_table = (analyse[:, :, None] * synthesis[:, None, :]).reshape(
        NT, 4 * count_freq * count_freq
    )
    running_table = jnp.cumsum(product_table, axis=0)
    mixing = jnp.take(running_table, onset_rows - 1, axis=0)
    return mixing.reshape(-1, 2 * count_freq, 2 * count_freq)


def kernel_product(einsum_recipe, left_side, right_side):
    return jnp.einsum(einsum_recipe, left_side, right_side, preferred_element_type=jnp.float32)


def per_device_general(focusing, v_factors, u_factors, tile_ranks, owners, onsets):
    count_col = lax.axis_size("col")
    my_column = lax.axis_index("col")
    count_freq = lax.axis_size("freq")
    my_freq = lax.axis_index("freq")
    freq_dev = focusing.shape[0]
    vis_dev = focusing.shape[2]
    sources_dev = focusing.shape[3]
    capacity = u_factors.shape[2]
    block_width = min(sources_dev, TS)
    blocks_dev = sources_dev // block_width
    per_tile = TS // block_width
    all_blocks = count_col * blocks_dev
    row_tiles = NR // TS
    col_tiles = NS // TS
    freq_all = freq_dev * count_freq
    quarter = TS // count_freq
    tile_ids = jnp.arange(row_tiles, dtype=jnp.int32)
    same_owner = owners[:, None] == owners[None, :]
    earlier = tile_ids[None, :] < tile_ids[:, None]
    slot_of = jnp.sum((same_owner & earlier).astype(jnp.int32), axis=1)
    slot_ids = jnp.arange(capacity, dtype=jnp.int32)
    routing = (owners[None, None, :] == jnp.arange(count_col, dtype=jnp.int32)[:, None, None]) & (
        slot_of[None, None, :] == slot_ids[None, :, None]
    )
    lower_routing = routing.astype(jnp.bfloat16)
    my_slots = ((owners[None, :] == my_column) & (slot_of[None, :] == slot_ids[:, None])).astype(
        jnp.int32
    )
    slot_ranks = jnp.sum(my_slots[:, :, None] * tile_ranks[None, :, :], axis=1)
    rank_mask = (jnp.arange(R, dtype=jnp.int32)[None, None, :] < slot_ranks[:, :, None]).astype(
        jnp.float32
    )
    slot_onsets = jnp.sum(my_slots[:, :, None] * onsets.reshape(row_tiles, TS)[None], axis=1)
    slot_onsets = jnp.maximum(slot_onsets, 1)
    focus_low = focusing.astype(jnp.bfloat16).reshape(freq_dev, 2, vis_dev, blocks_dev, block_width)
    factors_v = v_factors.reshape(freq_dev, 2, row_tiles, R, blocks_dev, block_width)
    einsum_recipe = "fikbs,fvbs->ifbkv"
    real_portion = kernel_product(einsum_recipe, factors_v[:, 0], focus_low[:, 0]) - kernel_product(
        einsum_recipe, factors_v[:, 1], focus_low[:, 1]
    )
    part_imag = kernel_product(einsum_recipe, factors_v[:, 0], focus_low[:, 1]) + kernel_product(
        einsum_recipe, factors_v[:, 1], focus_low[:, 0]
    )
    partial_sums = jnp.stack([real_portion, part_imag], axis=3).astype(jnp.bfloat16)
    outgoing_parts = kernel_product("way,ymleno->amwleno", lower_routing, partial_sums).astype(
        jnp.bfloat16
    )
    outgoing_parts = outgoing_parts.reshape(capacity, freq_dev, all_blocks, 2, R, vis_dev)
    arrived = lax.all_to_all(outgoing_parts, "col", split_axis=2, concat_axis=2, tiled=True)
    coefficients = jnp.sum(
        arrived.astype(jnp.float32).reshape(capacity, freq_dev, col_tiles, per_tile, 2, R, vis_dev),
        axis=3,
    )
    coefficients = (coefficients * rank_mask[:, None, :, None, :, None]).astype(jnp.bfloat16)
    factors_u = u_factors.reshape(freq_dev, 2, capacity, col_tiles, R, TS)
    uform = "fcjka,cfjkv->cfav"
    field_real = kernel_product(uform, factors_u[:, 0], coefficients[:, :, :, 0]) - kernel_product(
        uform, factors_u[:, 1], coefficients[:, :, :, 1]
    )
    field_imag = kernel_product(uform, factors_u[:, 0], coefficients[:, :, :, 1]) + kernel_product(
        uform, factors_u[:, 1], coefficients[:, :, :, 0]
    )
    receiver_field = jnp.stack([field_real, field_imag], axis=2).astype(jnp.bfloat16)
    turned = lax.all_to_all(receiver_field, "freq", split_axis=3, concat_axis=1, tiled=True)
    quarter_onsets = lax.dynamic_slice_in_dim(slot_onsets, my_freq * quarter, quarter, 1)
    mixing = window_tables(freq_all, quarter_onsets.reshape(-1)).reshape(
        capacity, quarter, 2 * freq_all, 2 * freq_all
    )
    flat_field = turned.reshape(capacity, 2 * freq_all, quarter, vis_dev).astype(jnp.float32)
    mixed_field = jnp.einsum("crpq,cqrv->cprv", mixing, flat_field, precision=lax.Precision.HIGHEST)
    mixed_field = mixed_field.astype(jnp.bfloat16).reshape(capacity, freq_all, 2, quarter, vis_dev)
    windowed = lax.all_to_all(mixed_field, "freq", split_axis=1, concat_axis=3, tiled=True)
    aform = "fcjka,cfav->cfjkv"
    back_real = kernel_product(aform, factors_u[:, 0], windowed[:, :, 0]) + kernel_product(
        aform, factors_u[:, 1], windowed[:, :, 1]
    )
    back_imag = kernel_product(aform, factors_u[:, 0], windowed[:, :, 1]) - kernel_product(
        aform, factors_u[:, 1], windowed[:, :, 0]
    )
    adjoint = jnp.stack([back_real, back_imag], axis=3) * rank_mask[:, None, :, None, :, None]
    adjoint = adjoint.astype(jnp.bfloat16)
    spread = jnp.broadcast_to(
        adjoint[:, :, :, None], (capacity, freq_dev, col_tiles, per_tile, 2, R, vis_dev)
    )
    spread = spread.reshape(capacity, freq_dev, all_blocks, 2, R, vis_dev)
    result_field = lax.all_to_all(spread, "col", split_axis=2, concat_axis=2, tiled=True)
    result_field = result_field.reshape(capacity, freq_dev, count_col, blocks_dev, 2, R, vis_dev)
    row_share = kernel_product("prq,rjpagwu->qjagwu", lower_routing, result_field).astype(
        jnp.bfloat16
    )
    wform = "fikbs,ifbkv->fvbs"
    wave_real = kernel_product(wform, factors_v[:, 0], row_share[:, :, :, 0]) + kernel_product(
        wform, factors_v[:, 1], row_share[:, :, :, 1]
    )
    wave_imag = kernel_product(wform, factors_v[:, 0], row_share[:, :, :, 1]) - kernel_product(
        wform, factors_v[:, 1], row_share[:, :, :, 0]
    )
    wave_field = jnp.stack([wave_real, wave_imag], axis=1).reshape(
        freq_dev, 2, vis_dev, sources_dev
    )
    return focusing - wave_field


def mixing_table(count_freq):
    time_steps = np.arange(NT)
    rows = []
    for mine in range(count_freq):
        bins = [KLO + mine] + [KLO + f for f in range(count_freq) if f != mine]
        phases = 2.0 * np.pi * ((np.array(bins)[:, None] * time_steps[None, :]) % NT) / NT
        analyse = np.stack([np.cos(phases), -np.sin(phases)], axis=1).reshape(2 * count_freq, NT)
        table = (analyse[:, None, :] * analyse[None, :, :] * (2.0 / NT)).reshape(-1, NT)
        rest = table.astype(np.float32)
        parts = []
        for _ in range(3):
            part = rest.astype(ml_dtypes.bfloat16)
            parts.append(part)
            rest = rest - part.astype(np.float32)
        rows.append(np.concatenate(parts, axis=0))
    return np.stack(rows)


def dot(left, right, left_dim, right_dim):
    return lax.dot_general(
        left, right, (((left_dim,), (right_dim,)), ((), ())), preferred_element_type=jnp.float32
    )


def list_tiles(owners, tile_of, held, count_col, capacity):
    for owner in range(count_col):
        held[owner] = 0
    for tile in range(owners.shape[0]):
        owner = owners[tile]
        slot = held[owner]
        tile_of[owner * capacity + slot] = tile
        held[owner] = slot + 1


def forward_kernel(count_col, half, owners_far, ranks_far, focus, factors, *refs):
    outs = refs[: 2 * count_col]
    focus_here, factors_here, sums, owners, ranks, tile_of, held, sems = refs[2 * count_col :]
    column = lax.axis_index("col")
    mine = lax.axis_index("freq")
    two, vis, sources = focus_here.shape
    blocks = sources // TS
    copies = []
    for j in range(blocks):
        at = pl.ds(j * TS, TS)
        copies.append(
            [
                pltpu.make_async_copy(focus.at[0, :, :, at], focus_here.at[:, :, at], sems.at[0, j]),
                pltpu.make_async_copy(factors.at[0, :, :, at], factors_here.at[:, :, at], sems.at[1, j]),
            ]
        )
        for copy in copies[j]:
            copy.start()
    small = [
        pltpu.make_async_copy(owners_far, owners, sems.at[2, 0]),
        pltpu.make_async_copy(ranks_far, ranks, sems.at[2, 1]),
    ]
    for copy in small:
        copy.start()
    for copy in small:
        copy.wait()
    capacity = 2 * half
    list_tiles(owners, tile_of, held, count_col, capacity)
    for j in range(blocks):
        for copy in copies[j]:
            copy.wait()
        at = pl.ds(j * TS, TS)
        low = focus_here[:, :, at].astype(jnp.bfloat16).reshape(two * vis, TS)
        by_real = dot(factors_here[0, :, at], low, 1, 1)
        by_imag = dot(factors_here[1, :, at], low, 1, 1)
        sums[j, :, :vis] = by_real[:, :vis] - by_imag[:, vis:]
        sums[j, :, vis:] = by_real[:, vis:] + by_imag[:, :vis]
    row_id = lax.broadcasted_iota(jnp.int32, (R, 2 * vis), 0)
    for d in range(count_col):
        for e in range(2):
            for s in range(half):
                tile = tile_of[(column ^ d) * capacity + (mine ^ e) * half + s]
                pieces = []
                for j in range(blocks):
                    rank = ranks[tile, column * blocks + j]
                    piece = sums[j, pl.ds(pl.multiple_of(tile * R, 8), R), :]
                    pieces.append(jnp.where(row_id < rank, piece, 0.0))
                outs[2 * d + e][s] = jnp.concatenate(pieces, axis=0).astype(jnp.bfloat16)


def forward_products(count_col, half, focusing, v_factors, tile_ranks, owners):
    vis, sources = focusing.shape[2:]
    rows = v_factors.shape[2]
    blocks = sources // TS
    out = jax.ShapeDtypeStruct((half, blocks * R, 2 * vis), jnp.bfloat16)
    vmem = pl.BlockSpec(memory_space=pltpu.VMEM)
    anywhere = pl.BlockSpec(memory_space=pl.ANY)
    return pl.pallas_call(
        functools.partial(forward_kernel, count_col, half),
        in_specs=[anywhere] * 4,
        out_specs=[vmem] * (2 * count_col + 2),
        out_shape=[out] * (2 * count_col)
        + [
            jax.ShapeDtypeStruct(focusing.shape[1:], jnp.float32),
            jax.ShapeDtypeStruct(v_factors.shape[1:], jnp.bfloat16),
        ],
        scratch_shapes=[
            pltpu.VMEM((blocks, rows, 2 * vis), jnp.float32),
            pltpu.SMEM(owners.shape, jnp.int32),
            pltpu.SMEM(tile_ranks.shape, jnp.int32),
            pltpu.SMEM((count_col * 2 * half,), jnp.int32),
            pltpu.SMEM((count_col,), jnp.int32),
            pltpu.SemaphoreType.DMA((3, blocks)),
        ],
        compiler_params=pltpu.CompilerParams(vmem_limit_bytes=46 * 2**20),
        cost_estimate=pl.CostEstimate(
            flops=8 * rows * vis * sources, bytes_accessed=8 * vis * sources + 4 * rows * sources, transcendentals=0
        ),
        name="forward_products",
    )(owners, tile_ranks, focusing, v_factors)


def load_kernel(half, u_factors, u_here, sem):
    start = lax.axis_index("freq") * half
    copy = pltpu.make_async_copy(u_factors.at[0, :, pl.ds(start, half)], u_here, sem)
    copy.start()
    copy.wait()


def load_factors(half, u_factors):
    shape = (2, half) + u_factors.shape[3:]
    return pl.pallas_call(
        functools.partial(load_kernel, half),
        in_specs=[pl.BlockSpec(memory_space=pl.ANY)],
        out_specs=pl.BlockSpec(memory_space=pltpu.VMEM),
        out_shape=jax.ShapeDtypeStruct(shape, jnp.bfloat16),
        scratch_shapes=[pltpu.SemaphoreType.DMA],
        compiler_params=pltpu.CompilerParams(vmem_limit_bytes=46 * 2**20),
        cost_estimate=pl.CostEstimate(flops=0, bytes_accessed=2 * int(np.prod(shape)), transcendentals=0),
        name="load_factors",
    )(u_factors)


def receiver_kernel(count_col, half, chunk, owners, ranks, onsets, table, *refs):
    arrived = refs[: 2 * count_col]
    u_own = refs[2 * count_col]
    u_other = refs[2 * count_col + 1 : 2 * count_col + 5]
    outs = refs[-2 * count_col - 7 : -7]
    earlier = refs[2 * count_col + 5 : -2 * count_col - 7]
    factors, coefs, field, windowed, tile_of, held, sems = refs[-7:]
    column = lax.axis_index("col")
    mine = lax.axis_index("freq")
    vis = field.shape[1]
    rows = factors.shape[1]
    place = lax.axis_index("grp") * 2 + lax.axis_index("rep")
    quarter = u_other[0].shape[1]
    copies = []
    for n, ref in enumerate(u_other):
        start = pl.multiple_of((place ^ n) * quarter, quarter)
        copies.append(
            pltpu.make_async_copy(ref, factors.at[:, pl.ds(start, quarter), :], sems.at[n])
        )
    for copy in copies:
        copy.start()
    list_tiles(owners, tile_of, held, count_col, 2 * half)
    tile = tile_of[column * 2 * half + mine * half + chunk]
    strip = arrived[0].shape[1]
    for d in range(count_col):
        start = pl.multiple_of((column ^ d) * strip, strip)
        for e in range(2):
            values = arrived[2 * d + e][chunk]
            coefs[e, 0, pl.ds(start, strip), :] = values
            coefs[e, 1, pl.ds(start, strip), :] = jnp.concatenate([-values[:, vis:], values[:, :vis]], axis=1)
    times = lax.broadcasted_iota(jnp.int32, (NT, TS), 0)
    inside = jnp.where(times < onsets[tile], 1.0, 0.0).astype(jnp.bfloat16)
    tables = dot(table[mine], inside, 1, 0)
    count = tables.shape[0] // 3
    mixing = tables[:count] + tables[count : 2 * count] + tables[2 * count :]
    for e in range(2):
        for copy in copies if e == 1 else []:
            copy.wait()
        matrix = (u_own[:, chunk] if e == 0 else factors[...]).reshape(2 * rows, TS)
        product = dot(coefs[e].reshape(2 * rows, 2 * vis), matrix, 0, 0)
        low = product.astype(jnp.bfloat16).astype(jnp.float32)
        field[2 * e] = low[:vis]
        field[2 * e + 1] = low[vis:]
    for p in range(4):
        total = mixing[4 * p : 4 * p + 1] * field[0]
        for q in range(1, 4):
            total = total + mixing[4 * p + q : 4 * p + q + 1] * field[q]
        windowed[p // 2, (p % 2) * vis : (p % 2 + 1) * vis, :] = total.astype(jnp.bfloat16)
    row_id = lax.broadcasted_iota(jnp.int32, (R, 2 * vis), 0)
    for e in range(2):
        matrix = (u_own[:, chunk] if e == 0 else factors[...]).reshape(2 * rows, TS)
        back = dot(matrix, windowed[e], 1, 1)
        by_real, by_imag = back[:rows], back[rows:]
        adjoint = jnp.concatenate(
            [by_real[:, :vis] + by_imag[:, vis:], by_real[:, vis:] - by_imag[:, :vis]], axis=1
        )
        pieces = []
        for j in range(rows // R):
            pieces.append(jnp.where(row_id < ranks[tile, j], adjoint[j * R : (j + 1) * R], 0.0))
        coefs[e, 0] = jnp.concatenate(pieces, axis=0).astype(jnp.bfloat16)
        for d in range(count_col):
            start = pl.multiple_of((column ^ d) * strip, strip)
            outs[2 * d + e][chunk] = coefs[e, 0, pl.ds(start, strip), :]
            for s in range(chunk):
                outs[2 * d + e][s] = earlier[2 * d + e][s]


def receiver_products(count_col, half, chunk, owners, tile_ranks, onsets, table, arrived, u_factors, u_other, earlier):
    strip, columns = arrived[0].shape[1:]
    rows = u_factors.shape[2]
    vis = columns // 2
    smem = pl.BlockSpec(memory_space=pltpu.SMEM)
    vmem = pl.BlockSpec(memory_space=pltpu.VMEM)
    out = jax.ShapeDtypeStruct((chunk + 1, strip, columns), jnp.bfloat16)
    return pl.pallas_call(
        functools.partial(receiver_kernel, count_col, half, chunk),
        in_specs=[smem, smem, vmem, vmem]
        + [vmem] * (2 * count_col)
        + [vmem] * 5
        + [vmem] * len(earlier),
        out_specs=[vmem] * (2 * count_col),
        out_shape=[out] * (2 * count_col),
        scratch_shapes=[
            pltpu.VMEM((2, rows, TS), jnp.bfloat16),
            pltpu.VMEM((2, 2, rows, columns), jnp.bfloat16),
            pltpu.VMEM((4, vis, TS), jnp.float32),
            pltpu.VMEM((2, columns, TS), jnp.bfloat16),
            pltpu.SMEM((count_col * 2 * half,), jnp.int32),
            pltpu.SMEM((count_col,), jnp.int32),
            pltpu.SemaphoreType.DMA((4,)),
        ],
        compiler_params=pltpu.CompilerParams(vmem_limit_bytes=24 * 2**20),
        cost_estimate=pl.CostEstimate(
            flops=32 * rows * vis * TS, bytes_accessed=8 * rows * TS, transcendentals=0
        ),
        name="receiver_products",
    )(owners, tile_ranks, onsets, table, *arrived, u_factors, *u_other, *earlier)


def update_kernel(count_col, half, owners, *refs):
    arrivals = refs[: 2 * count_col]
    focus, factors, out, out_here, gathered, adjoint, tile_of, held, sems = refs[2 * count_col :]
    column = lax.axis_index("col")
    mine = lax.axis_index("freq")
    two, vis, sources = out_here.shape
    rows = factors.shape[1]
    blocks = sources // TS
    width = 512
    capacity = 2 * half
    list_tiles(owners, tile_of, held, count_col, capacity)
    for s in range(half):
        for d in range(count_col):
            for e in range(2):
                tile = tile_of[(column ^ d) * capacity + (mine ^ e) * half + s]
                values = arrivals[2 * d + e][s].astype(jnp.float32)
                for j in range(blocks):
                    gathered[j, pl.ds(pl.multiple_of(tile * R, 8), R), :] = values[j * R : (j + 1) * R]
    row_id = lax.broadcasted_iota(jnp.int32, (2 * vis, 2 * vis), 0)
    column_id = lax.broadcasted_iota(jnp.int32, (2 * vis, 2 * vis), 1)
    identity = jnp.where(row_id == column_id, 1.0, 0.0).astype(jnp.bfloat16)
    for j in range(blocks):
        values = gathered[j]
        adjoint[j, :rows] = values.astype(jnp.bfloat16)
        adjoint[j, rows:] = jnp.concatenate([values[:, vis:], -values[:, :vis]], axis=1).astype(jnp.bfloat16)

    writes = []
    for n in range(sources // width):
        j = n * width // TS
        at = pl.ds(n * width, width)
        right = factors[:, :, at].reshape(2 * rows, width)
        wave = dot(adjoint[j], right, 0, 0)
        out_here[:, :, at] = focus[:, :, at] - wave.reshape(two, vis, width)
        writes.append(pltpu.make_async_copy(out_here.at[:, :, at], out.at[0, :, :, at], sems.at[n]))
        writes[n].start()
    for write in writes:
        write.wait()


def update_products(count_col, half, owners, arrivals, focusing, v_factors):
    vis, sources = focusing.shape[1:]
    rows = v_factors.shape[1]
    blocks = sources // TS
    smem = pl.BlockSpec(memory_space=pltpu.SMEM)
    vmem = pl.BlockSpec(memory_space=pltpu.VMEM)
    anywhere = pl.BlockSpec(memory_space=pl.ANY)
    return pl.pallas_call(
        functools.partial(update_kernel, count_col, half),
        in_specs=[smem] + [vmem] * (len(arrivals) + 2),
        out_specs=anywhere,
        out_shape=jax.ShapeDtypeStruct((1,) + focusing.shape, jnp.float32),
        scratch_shapes=[
            pltpu.VMEM(focusing.shape, jnp.float32),
            pltpu.VMEM((blocks, rows, 2 * vis), jnp.float32),
            pltpu.VMEM((blocks, 2 * rows, 2 * vis), jnp.bfloat16),
            pltpu.SMEM((count_col * 2 * half,), jnp.int32),
            pltpu.SMEM((count_col,), jnp.int32),
            pltpu.SemaphoreType.DMA((sources // 512,)),
        ],
        compiler_params=pltpu.CompilerParams(vmem_limit_bytes=24 * 2**20),
        cost_estimate=pl.CostEstimate(
            flops=8 * rows * vis * sources, bytes_accessed=16 * vis * sources + 4 * rows * sources, transcendentals=0
        ),
        name="update_products",
    )(owners, *arrivals, focusing, v_factors)


def swap(array, axis):
    return lax.ppermute(array, axis, [(0, 1), (1, 0)])


def exchange(arrays, count_col):
    moved = list(arrays)
    for d in range(count_col - 1, -1, -1):
        for e in (1, 0):
            offset = 2 * d + e
            if offset:
                moved[offset] = lax.ppermute(
                    arrays[offset], ("col", "freq"), [(i, i ^ offset) for i in range(2 * count_col)]
                )
    return moved


def per_device_paired(focusing, v_factors, u_factors, tile_ranks, owners, onsets):
    count_col = lax.axis_size("col")
    mine = lax.axis_index("freq")
    capacity = u_factors.shape[2]
    half = capacity // 2
    rows = u_factors.shape[3]
    place = lax.axis_index("grp") * 2 + lax.axis_index("rep")
    table = jnp.asarray(mixing_table(2))
    tile_onsets = onsets.reshape(NR // TS, 1, TS)
    first = []
    for s in range(half):
        piece = lax.dynamic_slice(
            u_factors, (0, 0, (1 - mine) * half + s, place * (rows // 4), 0), (1, 2, 1, rows // 4, TS)
        ).reshape(2, rows // 4, TS)
        first.append(swap(piece, "freq"))
    *outgoing, focus_here, v_here = forward_products(count_col, half, focusing, v_factors, tile_ranks, owners)
    def move(offset, payload):
        return lax.ppermute(payload, ("col", "freq"), [(i, i ^ offset) for i in range(2 * count_col)])
    arrived = list(outgoing)
    far, _ = lax.optimization_barrier((u_factors, outgoing[0]))
    u_here = load_factors(half, far)
    second = []
    if 2 == 2:
        first[0], _ = lax.optimization_barrier((first[0], outgoing[0]))
        second.append(swap(first[0], "grp"))
    for offset in (6, 4, 2):
        arrived[offset] = move(offset, arrived[offset])
    held = lax.optimization_barrier(tuple(arrived + first + [u_here] + second))
    if 2 == 2:
        second = [held[-1]]
        held = held[:-1]
    arrived, first, u_here = list(held[: 2 * count_col]), list(held[2 * count_col : -1]), held[-1]
    if 2 == 3:
        second.append(swap(first[0], "grp"))
    second.append(swap(first[1], "grp"))
    for offset in (7, 5, 3, 1):
        arrived[offset] = move(offset, arrived[offset])
    held = lax.optimization_barrier(tuple(arrived + first + second[:1]))
    arrived = list(held[:-3])
    first, second = list(held[-3:-1]), [held[-1], second[1]]
    back = []
    for s in range(half):
        gathered = [first[s], swap(first[s], "rep"), second[s], swap(second[s], "rep")]
        back = receiver_products(
            count_col, half, s, owners, tile_ranks, tile_onsets, table, arrived, u_here, gathered, back
        )
    returned = exchange(back, count_col)
    return update_products(count_col, half, owners, returned, focus_here, v_here)


def per_device(focusing, v_factors, u_factors, tile_ranks, owners, onsets):
    count_col = lax.axis_size("col")
    paired = (
        lax.axis_size("freq") == 2
        and lax.axis_size("grp") == 2
        and lax.axis_size("rep") == 2
        and focusing.shape[0] == 1
        and count_col & (count_col - 1) == 0
        and u_factors.shape[2] % 2 == 0
        and u_factors.shape[2] * count_col == NR // TS
        and focusing.shape[2] % 128 == 0
        and focusing.shape[3] % TS == 0
        and (focusing.shape[3] // TS * R) % 16 == 0
        and u_factors.shape[3] % 64 == 0
    )
    chosen = per_device_paired if paired else per_device_general
    return chosen(focusing, v_factors, u_factors, tile_ranks, owners, onsets)


def solution(mesh):
    return jax.shard_map(
        per_device,
        mesh=mesh,
        in_specs=(
            P("freq", None, ("grp", "rep"), "col"),
            P("freq", None, None, "col"),
            P("freq", None, "col", None, None),
            P(),
            P(),
            P(),
        ),
        out_specs=P("freq", None, ("grp", "rep"), "col"),
        check_vma=False,
    )
```

```python
import functools

import jax
import jax.numpy as jnp
import ml_dtypes
import numpy as np
from jax import lax
from jax.experimental import pallas as pl
from jax.experimental.pallas import tpu as pltpu
from jax.sharding import PartitionSpec as P

TS = 1024
R = 24
NR = 16384
NS = 16384
NT = 512
KLO = 8


def window_tables(count_freq, onset_rows):
    time_steps = jnp.arange(NT, dtype=jnp.int32)
    freq_bins = KLO + jnp.arange(count_freq, dtype=jnp.int32)
    phases = 2.0 * jnp.pi * (freq_bins[None, :] * time_steps[:, None] % NT).astype(jnp.float32) / NT
    cosine = jnp.cos(phases)
    sines = jnp.sin(phases)
    analyse = jnp.stack([cosine, -sines], axis=2).reshape(NT, 2 * count_freq)
    synthesis = analyse * (2.0 / NT)
    product_table = (analyse[:, :, None] * synthesis[:, None, :]).reshape(
        NT, 4 * count_freq * count_freq
    )
    running_table = jnp.cumsum(product_table, axis=0)
    mixing = jnp.take(running_table, onset_rows - 1, axis=0)
    return mixing.reshape(-1, 2 * count_freq, 2 * count_freq)


def kernel_product(einsum_recipe, left_side, right_side):
    return jnp.einsum(einsum_recipe, left_side, right_side, preferred_element_type=jnp.float32)


def per_device_general(focusing, v_factors, u_factors, tile_ranks, owners, onsets):
    count_col = lax.axis_size("col")
    my_column = lax.axis_index("col")
    count_freq = lax.axis_size("freq")
    my_freq = lax.axis_index("freq")
    freq_dev = focusing.shape[0]
    vis_dev = focusing.shape[2]
    sources_dev = focusing.shape[3]
    capacity = u_factors.shape[2]
    block_width = min(sources_dev, TS)
    blocks_dev = sources_dev // block_width
    per_tile = TS // block_width
    all_blocks = count_col * blocks_dev
    row_tiles = NR // TS
    col_tiles = NS // TS
    freq_all = freq_dev * count_freq
    quarter = TS // count_freq
    tile_ids = jnp.arange(row_tiles, dtype=jnp.int32)
    same_owner = owners[:, None] == owners[None, :]
    earlier = tile_ids[None, :] < tile_ids[:, None]
    slot_of = jnp.sum((same_owner & earlier).astype(jnp.int32), axis=1)
    slot_ids = jnp.arange(capacity, dtype=jnp.int32)
    routing = (owners[None, None, :] == jnp.arange(count_col, dtype=jnp.int32)[:, None, None]) & (
        slot_of[None, None, :] == slot_ids[None, :, None]
    )
    lower_routing = routing.astype(jnp.bfloat16)
    my_slots = ((owners[None, :] == my_column) & (slot_of[None, :] == slot_ids[:, None])).astype(
        jnp.int32
    )
    slot_ranks = jnp.sum(my_slots[:, :, None] * tile_ranks[None, :, :], axis=1)
    rank_mask = (jnp.arange(R, dtype=jnp.int32)[None, None, :] < slot_ranks[:, :, None]).astype(
        jnp.float32
    )
    slot_onsets = jnp.sum(my_slots[:, :, None] * onsets.reshape(row_tiles, TS)[None], axis=1)
    slot_onsets = jnp.maximum(slot_onsets, 1)
    focus_low = focusing.astype(jnp.bfloat16).reshape(freq_dev, 2, vis_dev, blocks_dev, block_width)
    factors_v = v_factors.reshape(freq_dev, 2, row_tiles, R, blocks_dev, block_width)
    einsum_recipe = "fikbs,fvbs->ifbkv"
    real_portion = kernel_product(einsum_recipe, factors_v[:, 0], focus_low[:, 0]) - kernel_product(
        einsum_recipe, factors_v[:, 1], focus_low[:, 1]
    )
    part_imag = kernel_product(einsum_recipe, factors_v[:, 0], focus_low[:, 1]) + kernel_product(
        einsum_recipe, factors_v[:, 1], focus_low[:, 0]
    )
    partial_sums = jnp.stack([real_portion, part_imag], axis=3).astype(jnp.bfloat16)
    outgoing_parts = kernel_product("way,ymleno->amwleno", lower_routing, partial_sums).astype(
        jnp.bfloat16
    )
    outgoing_parts = outgoing_parts.reshape(capacity, freq_dev, all_blocks, 2, R, vis_dev)
    arrived = lax.all_to_all(outgoing_parts, "col", split_axis=2, concat_axis=2, tiled=True)
    coefficients = jnp.sum(
        arrived.astype(jnp.float32).reshape(capacity, freq_dev, col_tiles, per_tile, 2, R, vis_dev),
        axis=3,
    )
    coefficients = (coefficients * rank_mask[:, None, :, None, :, None]).astype(jnp.bfloat16)
    factors_u = u_factors.reshape(freq_dev, 2, capacity, col_tiles, R, TS)
    uform = "fcjka,cfjkv->cfav"
    field_real = kernel_product(uform, factors_u[:, 0], coefficients[:, :, :, 0]) - kernel_product(
        uform, factors_u[:, 1], coefficients[:, :, :, 1]
    )
    field_imag = kernel_product(uform, factors_u[:, 0], coefficients[:, :, :, 1]) + kernel_product(
        uform, factors_u[:, 1], coefficients[:, :, :, 0]
    )
    receiver_field = jnp.stack([field_real, field_imag], axis=2).astype(jnp.bfloat16)
    turned = lax.all_to_all(receiver_field, "freq", split_axis=3, concat_axis=1, tiled=True)
    quarter_onsets = lax.dynamic_slice_in_dim(slot_onsets, my_freq * quarter, quarter, 1)
    mixing = window_tables(freq_all, quarter_onsets.reshape(-1)).reshape(
        capacity, quarter, 2 * freq_all, 2 * freq_all
    )
    flat_field = turned.reshape(capacity, 2 * freq_all, quarter, vis_dev).astype(jnp.float32)
    mixed_field = jnp.einsum("crpq,cqrv->cprv", mixing, flat_field, precision=lax.Precision.HIGHEST)
    mixed_field = mixed_field.astype(jnp.bfloat16).reshape(capacity, freq_all, 2, quarter, vis_dev)
    windowed = lax.all_to_all(mixed_field, "freq", split_axis=1, concat_axis=3, tiled=True)
    aform = "fcjka,cfav->cfjkv"
    back_real = kernel_product(aform, factors_u[:, 0], windowed[:, :, 0]) + kernel_product(
        aform, factors_u[:, 1], windowed[:, :, 1]
    )
    back_imag = kernel_product(aform, factors_u[:, 0], windowed[:, :, 1]) - kernel_product(
        aform, factors_u[:, 1], windowed[:, :, 0]
    )
    adjoint = jnp.stack([back_real, back_imag], axis=3) * rank_mask[:, None, :, None, :, None]
    adjoint = adjoint.astype(jnp.bfloat16)
    spread = jnp.broadcast_to(
        adjoint[:, :, :, None], (capacity, freq_dev, col_tiles, per_tile, 2, R, vis_dev)
    )
    spread = spread.reshape(capacity, freq_dev, all_blocks, 2, R, vis_dev)
    result_field = lax.all_to_all(spread, "col", split_axis=2, concat_axis=2, tiled=True)
    result_field = result_field.reshape(capacity, freq_dev, count_col, blocks_dev, 2, R, vis_dev)
    row_share = kernel_product("prq,rjpagwu->qjagwu", lower_routing, result_field).astype(
        jnp.bfloat16
    )
    wform = "fikbs,ifbkv->fvbs"
    wave_real = kernel_product(wform, factors_v[:, 0], row_share[:, :, :, 0]) + kernel_product(
        wform, factors_v[:, 1], row_share[:, :, :, 1]
    )
    wave_imag = kernel_product(wform, factors_v[:, 0], row_share[:, :, :, 1]) - kernel_product(
        wform, factors_v[:, 1], row_share[:, :, :, 0]
    )
    wave_field = jnp.stack([wave_real, wave_imag], axis=1).reshape(
        freq_dev, 2, vis_dev, sources_dev
    )
    return focusing - wave_field


def mixing_table(count_freq):
    time_steps = np.arange(NT)
    rows = []
    for mine in range(count_freq):
        bins = [KLO + mine] + [KLO + f for f in range(count_freq) if f != mine]
        phases = 2.0 * np.pi * ((np.array(bins)[:, None] * time_steps[None, :]) % NT) / NT
        analyse = np.stack([np.cos(phases), -np.sin(phases)], axis=1).reshape(2 * count_freq, NT)
        table = (analyse[:, None, :] * analyse[None, :, :] * (2.0 / NT)).reshape(-1, NT)
        rest = table.astype(np.float32)
        parts = []
        for _ in range(3):
            part = rest.astype(ml_dtypes.bfloat16)
            parts.append(part)
            rest = rest - part.astype(np.float32)
        rows.append(np.concatenate(parts, axis=0))
    return np.stack(rows)


def dot(left, right, left_dim, right_dim):
    return lax.dot_general(
        left, right, (((left_dim,), (right_dim,)), ((), ())), preferred_element_type=jnp.float32
    )


def list_tiles(owners, tile_of, held, count_col, capacity):
    for owner in range(count_col):
        held[owner] = 0
    for tile in range(owners.shape[0]):
        owner = owners[tile]
        slot = held[owner]
        tile_of[owner * capacity + slot] = tile
        held[owner] = slot + 1


def forward_kernel(count_col, half, owners_far, focus, factors, *refs):
    outs = refs[: 2 * count_col]
    focus_here, factors_here, sums, owners, tile_of, held, sems = refs[2 * count_col :]
    column = lax.axis_index("col")
    mine = lax.axis_index("freq")
    two, vis, sources = focus_here.shape
    blocks = sources // TS
    copies = []
    for j in range(blocks):
        at = pl.ds(j * TS, TS)
        copies.append(
            [
                pltpu.make_async_copy(focus.at[0, :, :, at], focus_here.at[:, :, at], sems.at[0, j]),
                pltpu.make_async_copy(factors.at[0, :, :, at], factors_here.at[:, :, at], sems.at[1, j]),
            ]
        )
        for copy in copies[j]:
            copy.start()
    owners_copy = pltpu.make_async_copy(owners_far, owners, sems.at[2, 0])
    owners_copy.start()
    owners_copy.wait()
    capacity = 2 * half
    list_tiles(owners, tile_of, held, count_col, capacity)
    for j in range(blocks):
        for copy in copies[j]:
            copy.wait()
        at = pl.ds(j * TS, TS)
        low = focus_here[:, :, at].astype(jnp.bfloat16).reshape(two * vis, TS)
        by_real = dot(factors_here[0, :, at], low, 1, 1)
        by_imag = dot(factors_here[1, :, at], low, 1, 1)
        sums[j, :, :vis] = by_real[:, :vis] - by_imag[:, vis:]
        sums[j, :, vis:] = by_real[:, vis:] + by_imag[:, :vis]
    for d in range(count_col):
        for e in range(2):
            for s in range(half):
                tile = tile_of[(column ^ d) * capacity + (mine ^ e) * half + s]
                at = pl.ds(pl.multiple_of(tile * R, 8), R)
                pieces = [sums[j, at, :] for j in range(blocks)]
                outs[2 * d + e][s] = jnp.concatenate(pieces, axis=0).astype(jnp.bfloat16)


def forward_products(count_col, half, focusing, v_factors, owners):
    vis, sources = focusing.shape[2:]
    rows = v_factors.shape[2]
    blocks = sources // TS
    out = jax.ShapeDtypeStruct((half, blocks * R, 2 * vis), jnp.bfloat16)
    vmem = pl.BlockSpec(memory_space=pltpu.VMEM)
    anywhere = pl.BlockSpec(memory_space=pl.ANY)
    return pl.pallas_call(
        functools.partial(forward_kernel, count_col, half),
        in_specs=[anywhere] * 3,
        out_specs=[vmem] * (2 * count_col + 2),
        out_shape=[out] * (2 * count_col)
        + [
            jax.ShapeDtypeStruct(focusing.shape[1:], jnp.float32),
            jax.ShapeDtypeStruct(v_factors.shape[1:], jnp.bfloat16),
        ],
        scratch_shapes=[
            pltpu.VMEM((blocks, rows, 2 * vis), jnp.float32),
            pltpu.SMEM(owners.shape, jnp.int32),
            pltpu.SMEM((count_col * 2 * half,), jnp.int32),
            pltpu.SMEM((count_col,), jnp.int32),
            pltpu.SemaphoreType.DMA((3, blocks)),
        ],
        compiler_params=pltpu.CompilerParams(vmem_limit_bytes=46 * 2**20),
        cost_estimate=pl.CostEstimate(
            flops=8 * rows * vis * sources, bytes_accessed=8 * vis * sources + 4 * rows * sources, transcendentals=0
        ),
        name="forward_products",
    )(owners, focusing, v_factors)


def prepare_kernel(count_col, half, owners, ranks, onsets, table, u_factors, u_here, mixing, mask, tile_of, held, sem):
    column = lax.axis_index("col")
    mine = lax.axis_index("freq")
    copy = pltpu.make_async_copy(u_factors.at[0, :, pl.ds(mine * half, half)], u_here, sem)
    copy.start()
    list_tiles(owners, tile_of, held, count_col, 2 * half)
    times = lax.broadcasted_iota(jnp.int32, (NT, TS), 0)
    row_id = lax.broadcasted_iota(jnp.int32, (R, mask.shape[2]), 0)
    for s in range(half):
        tile = tile_of[column * 2 * half + mine * half + s]
        inside = jnp.where(times < onsets[tile], 1.0, 0.0).astype(jnp.bfloat16)
        tables = dot(table[mine], inside, 1, 0)
        count = tables.shape[0] // 3
        mixing[s] = tables[:count] + tables[count : 2 * count] + tables[2 * count :]
        pieces = [jnp.where(row_id < ranks[tile, j], 1.0, 0.0) for j in range(mask.shape[1] // R)]
        mask[s] = jnp.concatenate(pieces, axis=0).astype(jnp.bfloat16)
    copy.wait()


def prepare(count_col, half, columns, owners, tile_ranks, onsets, table, u_factors):
    shape = (2, half) + u_factors.shape[3:]
    vmem = pl.BlockSpec(memory_space=pltpu.VMEM)
    return pl.pallas_call(
        functools.partial(prepare_kernel, count_col, half),
        in_specs=[pl.BlockSpec(memory_space=pltpu.SMEM)] * 2 + [vmem, vmem, pl.BlockSpec(memory_space=pl.ANY)],
        out_specs=[vmem, vmem, vmem],
        out_shape=[
            jax.ShapeDtypeStruct(shape, jnp.bfloat16),
            jax.ShapeDtypeStruct((half, table.shape[1] // 3, TS), jnp.float32),
            jax.ShapeDtypeStruct((half, shape[2], columns), jnp.bfloat16),
        ],
        scratch_shapes=[
            pltpu.SMEM((count_col * 2 * half,), jnp.int32),
            pltpu.SMEM((count_col,), jnp.int32),
            pltpu.SemaphoreType.DMA,
        ],
        compiler_params=pltpu.CompilerParams(vmem_limit_bytes=40 * 2**20),
        cost_estimate=pl.CostEstimate(flops=0, bytes_accessed=4 * int(np.prod(shape)), transcendentals=0),
        name="prepare",
    )(owners, tile_ranks, onsets, table, u_factors)


def stack_coefficients(column, arrived, vis, slot, mask, matrix):
    strip = arrived[0].shape[1]
    for d, ref in enumerate(arrived):
        start = pl.multiple_of((column ^ d) * strip, strip)
        values = ref[slot] * mask[slot, pl.ds(start, strip), :]
        matrix[0, pl.ds(start, strip), :] = values
        matrix[1, pl.ds(start, strip), :] = jnp.concatenate([-values[:, vis:], values[:, :vis]], axis=1)


def own_field_kernel(count_col, half, mask, u_own, *refs):
    arrived = refs[:count_col]
    field, coefs = refs[count_col:]
    column = lax.axis_index("col")
    rows, columns = coefs.shape[2:]
    for s in range(half):
        stack_coefficients(column, arrived, columns // 2, s, mask, coefs.at[s])
        factors = u_own[:, s].reshape(2 * rows, TS)
        field[s] = dot(coefs[s].reshape(2 * rows, columns), factors, 0, 0).astype(jnp.bfloat16)


def own_field(count_col, half, mask, u_own, arrived):
    columns = arrived[0].shape[2]
    rows = u_own.shape[2]
    vmem = pl.BlockSpec(memory_space=pltpu.VMEM)
    return pl.pallas_call(
        functools.partial(own_field_kernel, count_col, half),
        in_specs=[vmem] * (2 + count_col),
        out_specs=vmem,
        out_shape=jax.ShapeDtypeStruct((half, columns, TS), jnp.bfloat16),
        scratch_shapes=[pltpu.VMEM((half, 2, rows, columns), jnp.bfloat16)],
        compiler_params=pltpu.CompilerParams(vmem_limit_bytes=20 * 2**20),
        cost_estimate=pl.CostEstimate(
            flops=4 * half * rows * columns * TS, bytes_accessed=2 * half * rows * TS, transcendentals=0
        ),
        name="own_field",
    )(mask, u_own, *arrived)


def receiver_kernel(count_col, half, mask, mixing, own, u_own, *refs):
    arrived = refs[:count_col]
    u_other = refs[count_col : -2 * count_col - 5]
    outs = refs[-2 * count_col - 5 : -5]
    factors, coefs, field, windowed, sems = refs[-5:]
    column = lax.axis_index("col")
    place = lax.axis_index("grp") * 2 + lax.axis_index("rep")
    rows, columns = coefs.shape[2:]
    vis = columns // 2
    copies = []
    for n, ref in enumerate(u_other):
        cuts = len(u_other) // 4
        start = (place ^ (n // cuts)) * (rows // 4) + sum(ref.shape[2] for ref in u_other[: n % cuts])
        at = pl.ds(pl.multiple_of(start, 16), ref.shape[2])
        copies.append(pltpu.make_async_copy(ref, factors.at[:, :, at, :], sems.at[n]))
        copies[n].start()
    for s in range(half):
        stack_coefficients(column, arrived, vis, s, mask, coefs.at[s])
    for copy in copies:
        copy.wait()
    strip = arrived[0].shape[1]
    for s in range(half):
        matrix = factors[:, s].reshape(2 * rows, TS)
        field[s] = dot(coefs[s].reshape(2 * rows, columns), matrix, 0, 0).astype(jnp.bfloat16)
    for s in range(half):
        high = 64
        for lane in range(0, TS, 128):
            at = pl.ds(lane, 128)
            mix = mixing[s, :, at]
            for row in range(0, vis, high):
                inputs = []
                for source in (own, field):
                    for part in range(2):
                        inputs.append(source[s, pl.ds(part * vis + row, high), at].astype(jnp.float32))
                for p in range(4):
                    total = mix[4 * p : 4 * p + 1] * inputs[0]
                    for q in range(1, 4):
                        total = total + mix[4 * p + q : 4 * p + q + 1] * inputs[q]
                    windowed[s, p // 2, pl.ds((p % 2) * vis + row, high), at] = total.astype(jnp.bfloat16)
        for e in range(2):
            if e == 0:
                matrix = u_own[:, s].reshape(2 * rows, TS)
            back = dot(matrix, windowed[s, e], 1, 1)
            by_real, by_imag = back[:rows], back[rows:]
            adjoint = jnp.concatenate(
                [by_real[:, :vis] + by_imag[:, vis:], by_real[:, vis:] - by_imag[:, :vis]], axis=1
            )
            coefs[s, 0] = adjoint.astype(jnp.bfloat16) * mask[s]
            for d in range(count_col):
                start = pl.multiple_of((column ^ d) * strip, strip)
                outs[2 * d + e][s] = coefs[s, 0, pl.ds(start, strip), :]
            if e == 0:
                matrix = factors[:, s].reshape(2 * rows, TS)


def receiver_products(count_col, half, mask, mixing, own, arrived, u_own, u_other):
    strip, columns = arrived[0].shape[1:]
    rows = u_own.shape[2]
    vmem = pl.BlockSpec(memory_space=pltpu.VMEM)
    out = jax.ShapeDtypeStruct((half, strip, columns), jnp.bfloat16)
    return pl.pallas_call(
        functools.partial(receiver_kernel, count_col, half),
        in_specs=[vmem] * (4 + count_col + len(u_other)),
        out_specs=[vmem] * (2 * count_col),
        out_shape=[out] * (2 * count_col),
        scratch_shapes=[
            pltpu.VMEM((2, half, rows, TS), jnp.bfloat16),
            pltpu.VMEM((half, 2, rows, columns), jnp.bfloat16),
            pltpu.VMEM((half, columns, TS), jnp.bfloat16),
            pltpu.VMEM((half, 2, columns, TS), jnp.bfloat16),
            pltpu.SemaphoreType.DMA((len(u_other),)),
        ],
        compiler_params=pltpu.CompilerParams(vmem_limit_bytes=24 * 2**20),
        cost_estimate=pl.CostEstimate(
            flops=12 * half * rows * columns * TS, bytes_accessed=8 * half * rows * TS, transcendentals=0
        ),
        name="receiver_products",
    )(mask, mixing, own, u_own, *arrived, *u_other)


def update_kernel(count_col, half, owners, *refs):
    arrivals = refs[: 2 * count_col]
    focus, factors, out, out_here, gathered, adjoint, tile_of, held, sems = refs[2 * count_col :]
    column = lax.axis_index("col")
    mine = lax.axis_index("freq")
    two, vis, sources = out_here.shape
    rows = factors.shape[1]
    blocks = sources // TS
    width = 512
    capacity = 2 * half
    list_tiles(owners, tile_of, held, count_col, capacity)
    for s in range(half):
        for d in range(count_col):
            for e in range(2):
                tile = tile_of[(column ^ d) * capacity + (mine ^ e) * half + s]
                values = arrivals[2 * d + e][s].astype(jnp.float32)
                for j in range(blocks):
                    gathered[j, pl.ds(pl.multiple_of(tile * R, 8), R), :] = values[j * R : (j + 1) * R]
    row_id = lax.broadcasted_iota(jnp.int32, (2 * vis, 2 * vis), 0)
    column_id = lax.broadcasted_iota(jnp.int32, (2 * vis, 2 * vis), 1)
    identity = jnp.where(row_id == column_id, 1.0, 0.0).astype(jnp.bfloat16)
    for j in range(blocks):
        values = gathered[j]
        adjoint[j, :rows] = values.astype(jnp.bfloat16)
        adjoint[j, rows:] = jnp.concatenate([values[:, vis:], -values[:, :vis]], axis=1).astype(jnp.bfloat16)

    writes = []
    for n in range(sources // width):
        j = n * width // TS
        at = pl.ds(n * width, width)
        right = factors[:, :, at].reshape(2 * rows, width)
        wave = dot(adjoint[j], right, 0, 0)
        out_here[:, :, at] = focus[:, :, at] - wave.reshape(two, vis, width)
        writes.append(pltpu.make_async_copy(out_here.at[:, :, at], out.at[0, :, :, at], sems.at[n]))
        writes[n].start()
    for write in writes:
        write.wait()


def update_products(count_col, half, owners, arrivals, focusing, v_factors):
    vis, sources = focusing.shape[1:]
    rows = v_factors.shape[1]
    blocks = sources // TS
    smem = pl.BlockSpec(memory_space=pltpu.SMEM)
    vmem = pl.BlockSpec(memory_space=pltpu.VMEM)
    anywhere = pl.BlockSpec(memory_space=pl.ANY)
    return pl.pallas_call(
        functools.partial(update_kernel, count_col, half),
        in_specs=[smem] + [vmem] * (len(arrivals) + 2),
        out_specs=anywhere,
        out_shape=jax.ShapeDtypeStruct((1,) + focusing.shape, jnp.float32),
        scratch_shapes=[
            pltpu.VMEM(focusing.shape, jnp.float32),
            pltpu.VMEM((blocks, rows, 2 * vis), jnp.float32),
            pltpu.VMEM((blocks, 2 * rows, 2 * vis), jnp.bfloat16),
            pltpu.SMEM((count_col * 2 * half,), jnp.int32),
            pltpu.SMEM((count_col,), jnp.int32),
            pltpu.SemaphoreType.DMA((sources // 512,)),
        ],
        compiler_params=pltpu.CompilerParams(vmem_limit_bytes=24 * 2**20),
        cost_estimate=pl.CostEstimate(
            flops=8 * rows * vis * sources, bytes_accessed=16 * vis * sources + 4 * rows * sources, transcendentals=0
        ),
        name="update_products",
    )(owners, *arrivals, focusing, v_factors)


def swap(array, axis):
    return lax.ppermute(array, axis, [(0, 1), (1, 0)])


def exchange(arrays, count_col):
    moved = list(arrays)
    for d in range(count_col - 1, -1, -1):
        for e in (1, 0):
            offset = 2 * d + e
            if offset:
                moved[offset] = lax.ppermute(
                    arrays[offset], ("col", "freq"), [(i, i ^ offset) for i in range(2 * count_col)]
                )
    return moved


def per_device_paired(focusing, v_factors, u_factors, tile_ranks, owners, onsets):
    count_col = lax.axis_size("col")
    mine = lax.axis_index("freq")
    capacity = u_factors.shape[2]
    half = capacity // 2
    rows = u_factors.shape[3]
    place = lax.axis_index("grp") * 2 + lax.axis_index("rep")
    table = jnp.asarray(mixing_table(2))
    tile_onsets = onsets.reshape(NR // TS, 1, TS)
    quarter = rows // 4
    cuts = (quarter // 2, quarter - quarter // 2)
    first = []
    share = lax.dynamic_slice(
        u_factors, (0, 0, (1 - mine) * half, place * quarter, 0), (1, 2, half, quarter, TS)
    ).reshape(2, half, quarter, TS)
    first = [swap(share[:, :, : cuts[0]], "freq"), swap(share[:, :, cuts[0] :], "freq")]
    *outgoing, focus_here, v_here = forward_products(count_col, half, focusing, v_factors, owners)
    def move(offset, payload):
        return lax.ppermute(payload, ("col", "freq"), [(i, i ^ offset) for i in range(2 * count_col)])
    arrived = list(outgoing)
    far, _ = lax.optimization_barrier((u_factors, outgoing[0]))
    u_here, mixing, mask = prepare(
        count_col, half, outgoing[0].shape[2], owners, tile_ranks, tile_onsets, table, far
    )
    first[0], _ = lax.optimization_barrier((first[0], outgoing[0]))
    second = [swap(first[0], "grp")]
    for offset in (6, 4, 2):
        arrived[offset] = move(offset, arrived[offset])
    held = lax.optimization_barrier(tuple(arrived + first + [u_here, mixing] + second))
    arrived, (*first, u_here, mixing, head) = list(held[: 2 * count_col]), held[2 * count_col :]
    second = [head, swap(first[1], "grp")]
    for offset in (7, 5, 3, 1):
        arrived[offset] = move(offset, arrived[offset])
    held = lax.optimization_barrier(tuple(arrived + first + second + [u_here]))
    arrived, (*pieces, u_here) = list(held[: 2 * count_col]), held[2 * count_col :]
    first, second = pieces[: len(cuts)], pieces[len(cuts) :]
    own = own_field(count_col, half, mask, u_here, arrived[::2])
    gathered = []
    for group in (first, second):
        gathered.extend(group)
        gathered.extend([swap(piece, "rep") for piece in group])
    back = receiver_products(count_col, half, mask, mixing, own, arrived[1::2], u_here, gathered)
    returned = exchange(back, count_col)
    return update_products(count_col, half, owners, returned, focus_here, v_here)


def per_device(focusing, v_factors, u_factors, tile_ranks, owners, onsets):
    count_col = lax.axis_size("col")
    paired = (
        lax.axis_size("freq") == 2
        and lax.axis_size("grp") == 2
        and lax.axis_size("rep") == 2
        and focusing.shape[0] == 1
        and count_col & (count_col - 1) == 0
        and u_factors.shape[2] % 2 == 0
        and u_factors.shape[2] * count_col == NR // TS
        and focusing.shape[2] % 128 == 0
        and focusing.shape[3] % TS == 0
        and (focusing.shape[3] // TS * R) % 16 == 0
        and u_factors.shape[3] % 64 == 0
    )
    chosen = per_device_paired if paired else per_device_general
    return chosen(focusing, v_factors, u_factors, tile_ranks, owners, onsets)


def solution(mesh):
    return jax.shard_map(
        per_device,
        mesh=mesh,
        in_specs=(
            P("freq", None, ("grp", "rep"), "col"),
            P("freq", None, None, "col"),
            P("freq", None, "col", None, None),
            P(),
            P(),
            P(),
        ),
        out_specs=P("freq", None, ("grp", "rep"), "col"),
        check_vma=False,
    )
```

```python
import functools

import jax
import jax.numpy as jnp
import ml_dtypes
import numpy as np
from jax import lax
from jax.experimental import pallas as pl
from jax.experimental.pallas import tpu as pltpu
from jax.sharding import PartitionSpec as P

TS = 1024
R = 24
NR = 16384
NS = 16384
NT = 512
KLO = 8


def window_tables(count_freq, onset_rows):
    time_steps = jnp.arange(NT, dtype=jnp.int32)
    freq_bins = KLO + jnp.arange(count_freq, dtype=jnp.int32)
    phases = 2.0 * jnp.pi * (freq_bins[None, :] * time_steps[:, None] % NT).astype(jnp.float32) / NT
    cosine = jnp.cos(phases)
    sines = jnp.sin(phases)
    analyse = jnp.stack([cosine, -sines], axis=2).reshape(NT, 2 * count_freq)
    synthesis = analyse * (2.0 / NT)
    product_table = (analyse[:, :, None] * synthesis[:, None, :]).reshape(
        NT, 4 * count_freq * count_freq
    )
    running_table = jnp.cumsum(product_table, axis=0)
    mixing = jnp.take(running_table, onset_rows - 1, axis=0)
    return mixing.reshape(-1, 2 * count_freq, 2 * count_freq)


def kernel_product(einsum_recipe, left_side, right_side):
    return jnp.einsum(einsum_recipe, left_side, right_side, preferred_element_type=jnp.float32)


def per_device_general(focusing, v_factors, u_factors, tile_ranks, owners, onsets):
    count_col = lax.axis_size("col")
    my_column = lax.axis_index("col")
    count_freq = lax.axis_size("freq")
    my_freq = lax.axis_index("freq")
    freq_dev = focusing.shape[0]
    vis_dev = focusing.shape[2]
    sources_dev = focusing.shape[3]
    capacity = u_factors.shape[2]
    block_width = min(sources_dev, TS)
    blocks_dev = sources_dev // block_width
    per_tile = TS // block_width
    all_blocks = count_col * blocks_dev
    row_tiles = NR // TS
    col_tiles = NS // TS
    freq_all = freq_dev * count_freq
    quarter = TS // count_freq
    tile_ids = jnp.arange(row_tiles, dtype=jnp.int32)
    same_owner = owners[:, None] == owners[None, :]
    earlier = tile_ids[None, :] < tile_ids[:, None]
    slot_of = jnp.sum((same_owner & earlier).astype(jnp.int32), axis=1)
    slot_ids = jnp.arange(capacity, dtype=jnp.int32)
    routing = (owners[None, None, :] == jnp.arange(count_col, dtype=jnp.int32)[:, None, None]) & (
        slot_of[None, None, :] == slot_ids[None, :, None]
    )
    lower_routing = routing.astype(jnp.bfloat16)
    my_slots = ((owners[None, :] == my_column) & (slot_of[None, :] == slot_ids[:, None])).astype(
        jnp.int32
    )
    slot_ranks = jnp.sum(my_slots[:, :, None] * tile_ranks[None, :, :], axis=1)
    rank_mask = (jnp.arange(R, dtype=jnp.int32)[None, None, :] < slot_ranks[:, :, None]).astype(
        jnp.float32
    )
    slot_onsets = jnp.sum(my_slots[:, :, None] * onsets.reshape(row_tiles, TS)[None], axis=1)
    slot_onsets = jnp.maximum(slot_onsets, 1)
    focus_low = focusing.astype(jnp.bfloat16).reshape(freq_dev, 2, vis_dev, blocks_dev, block_width)
    factors_v = v_factors.reshape(freq_dev, 2, row_tiles, R, blocks_dev, block_width)
    einsum_recipe = "fikbs,fvbs->ifbkv"
    real_portion = kernel_product(einsum_recipe, factors_v[:, 0], focus_low[:, 0]) - kernel_product(
        einsum_recipe, factors_v[:, 1], focus_low[:, 1]
    )
    part_imag = kernel_product(einsum_recipe, factors_v[:, 0], focus_low[:, 1]) + kernel_product(
        einsum_recipe, factors_v[:, 1], focus_low[:, 0]
    )
    partial_sums = jnp.stack([real_portion, part_imag], axis=3).astype(jnp.bfloat16)
    outgoing_parts = kernel_product("way,ymleno->amwleno", lower_routing, partial_sums).astype(
        jnp.bfloat16
    )
    outgoing_parts = outgoing_parts.reshape(capacity, freq_dev, all_blocks, 2, R, vis_dev)
    arrived = lax.all_to_all(outgoing_parts, "col", split_axis=2, concat_axis=2, tiled=True)
    coefficients = jnp.sum(
        arrived.astype(jnp.float32).reshape(capacity, freq_dev, col_tiles, per_tile, 2, R, vis_dev),
        axis=3,
    )
    coefficients = (coefficients * rank_mask[:, None, :, None, :, None]).astype(jnp.bfloat16)
    factors_u = u_factors.reshape(freq_dev, 2, capacity, col_tiles, R, TS)
    uform = "fcjka,cfjkv->cfav"
    field_real = kernel_product(uform, factors_u[:, 0], coefficients[:, :, :, 0]) - kernel_product(
        uform, factors_u[:, 1], coefficients[:, :, :, 1]
    )
    field_imag = kernel_product(uform, factors_u[:, 0], coefficients[:, :, :, 1]) + kernel_product(
        uform, factors_u[:, 1], coefficients[:, :, :, 0]
    )
    receiver_field = jnp.stack([field_real, field_imag], axis=2).astype(jnp.bfloat16)
    turned = lax.all_to_all(receiver_field, "freq", split_axis=3, concat_axis=1, tiled=True)
    quarter_onsets = lax.dynamic_slice_in_dim(slot_onsets, my_freq * quarter, quarter, 1)
    mixing = window_tables(freq_all, quarter_onsets.reshape(-1)).reshape(
        capacity, quarter, 2 * freq_all, 2 * freq_all
    )
    flat_field = turned.reshape(capacity, 2 * freq_all, quarter, vis_dev).astype(jnp.float32)
    mixed_field = jnp.einsum("crpq,cqrv->cprv", mixing, flat_field, precision=lax.Precision.HIGHEST)
    mixed_field = mixed_field.astype(jnp.bfloat16).reshape(capacity, freq_all, 2, quarter, vis_dev)
    windowed = lax.all_to_all(mixed_field, "freq", split_axis=1, concat_axis=3, tiled=True)
    aform = "fcjka,cfav->cfjkv"
    back_real = kernel_product(aform, factors_u[:, 0], windowed[:, :, 0]) + kernel_product(
        aform, factors_u[:, 1], windowed[:, :, 1]
    )
    back_imag = kernel_product(aform, factors_u[:, 0], windowed[:, :, 1]) - kernel_product(
        aform, factors_u[:, 1], windowed[:, :, 0]
    )
    adjoint = jnp.stack([back_real, back_imag], axis=3) * rank_mask[:, None, :, None, :, None]
    adjoint = adjoint.astype(jnp.bfloat16)
    spread = jnp.broadcast_to(
        adjoint[:, :, :, None], (capacity, freq_dev, col_tiles, per_tile, 2, R, vis_dev)
    )
    spread = spread.reshape(capacity, freq_dev, all_blocks, 2, R, vis_dev)
    result_field = lax.all_to_all(spread, "col", split_axis=2, concat_axis=2, tiled=True)
    result_field = result_field.reshape(capacity, freq_dev, count_col, blocks_dev, 2, R, vis_dev)
    row_share = kernel_product("prq,rjpagwu->qjagwu", lower_routing, result_field).astype(
        jnp.bfloat16
    )
    wform = "fikbs,ifbkv->fvbs"
    wave_real = kernel_product(wform, factors_v[:, 0], row_share[:, :, :, 0]) + kernel_product(
        wform, factors_v[:, 1], row_share[:, :, :, 1]
    )
    wave_imag = kernel_product(wform, factors_v[:, 0], row_share[:, :, :, 1]) - kernel_product(
        wform, factors_v[:, 1], row_share[:, :, :, 0]
    )
    wave_field = jnp.stack([wave_real, wave_imag], axis=1).reshape(
        freq_dev, 2, vis_dev, sources_dev
    )
    return focusing - wave_field


def mixing_table(count_freq):
    time_steps = np.arange(NT)
    rows = []
    for mine in range(count_freq):
        bins = [KLO + mine] + [KLO + f for f in range(count_freq) if f != mine]
        phases = 2.0 * np.pi * ((np.array(bins)[:, None] * time_steps[None, :]) % NT) / NT
        analyse = np.stack([np.cos(phases), -np.sin(phases)], axis=1).reshape(2 * count_freq, NT)
        table = (analyse[:, None, :] * analyse[None, :, :] * (2.0 / NT)).reshape(-1, NT)
        rest = table.astype(np.float32)
        parts = []
        for _ in range(3):
            part = rest.astype(ml_dtypes.bfloat16)
            parts.append(part)
            rest = rest - part.astype(np.float32)
        rows.append(np.concatenate(parts, axis=0))
    return np.stack(rows)


def dot(left, right, left_dim, right_dim):
    return lax.dot_general(
        left, right, (((left_dim,), (right_dim,)), ((), ())), preferred_element_type=jnp.float32
    )


def list_tiles(owners, tile_of, held, count_col, capacity):
    for owner in range(count_col):
        held[owner] = 0
    for tile in range(owners.shape[0]):
        owner = owners[tile]
        slot = held[owner]
        tile_of[owner * capacity + slot] = tile
        held[owner] = slot + 1


def forward_kernel(count_col, half, owners_far, focus, factors, *refs):
    outs = refs[: 2 * count_col]
    focus_here, factors_here, sums, owners, tile_of, held, sems = refs[2 * count_col :]
    column = lax.axis_index("col")
    mine = lax.axis_index("freq")
    two, vis, sources = focus_here.shape
    blocks = sources // TS
    copies = []
    for j in range(blocks):
        at = pl.ds(j * TS, TS)
        copies.append(
            [
                pltpu.make_async_copy(focus.at[0, :, :, at], focus_here.at[:, :, at], sems.at[0, j]),
                pltpu.make_async_copy(factors.at[0, :, :, at], factors_here.at[:, :, at], sems.at[1, j]),
            ]
        )
        for copy in copies[j]:
            copy.start()
    owners_copy = pltpu.make_async_copy(owners_far, owners, sems.at[2, 0])
    owners_copy.start()
    owners_copy.wait()
    capacity = 2 * half
    list_tiles(owners, tile_of, held, count_col, capacity)
    for j in range(blocks):
        for copy in copies[j]:
            copy.wait()
        at = pl.ds(j * TS, TS)
        low = focus_here[:, :, at].astype(jnp.bfloat16).reshape(two * vis, TS)
        by_real = dot(factors_here[0, :, at], low, 1, 1)
        by_imag = dot(factors_here[1, :, at], low, 1, 1)
        sums[j, :, :vis] = by_real[:, :vis] - by_imag[:, vis:]
        sums[j, :, vis:] = by_real[:, vis:] + by_imag[:, :vis]
    for d in range(count_col):
        for e in range(2):
            for s in range(half):
                tile = tile_of[(column ^ d) * capacity + (mine ^ e) * half + s]
                at = pl.ds(pl.multiple_of(tile * R, 8), R)
                pieces = [sums[j, at, :] for j in range(blocks)]
                outs[2 * d + e][s] = jnp.concatenate(pieces, axis=0).astype(jnp.bfloat16)


def forward_products(count_col, half, focusing, v_factors, owners):
    vis, sources = focusing.shape[2:]
    rows = v_factors.shape[2]
    blocks = sources // TS
    out = jax.ShapeDtypeStruct((half, blocks * R, 2 * vis), jnp.bfloat16)
    vmem = pl.BlockSpec(memory_space=pltpu.VMEM)
    anywhere = pl.BlockSpec(memory_space=pl.ANY)
    return pl.pallas_call(
        functools.partial(forward_kernel, count_col, half),
        in_specs=[anywhere] * 3,
        out_specs=[vmem] * (2 * count_col + 2),
        out_shape=[out] * (2 * count_col)
        + [
            jax.ShapeDtypeStruct(focusing.shape[1:], jnp.float32),
            jax.ShapeDtypeStruct(v_factors.shape[1:], jnp.bfloat16),
        ],
        scratch_shapes=[
            pltpu.VMEM((blocks, rows, 2 * vis), jnp.float32),
            pltpu.SMEM(owners.shape, jnp.int32),
            pltpu.SMEM((count_col * 2 * half,), jnp.int32),
            pltpu.SMEM((count_col,), jnp.int32),
            pltpu.SemaphoreType.DMA((3, blocks)),
        ],
        compiler_params=pltpu.CompilerParams(vmem_limit_bytes=46 * 2**20),
        cost_estimate=pl.CostEstimate(
            flops=8 * rows * vis * sources, bytes_accessed=8 * vis * sources + 4 * rows * sources, transcendentals=0
        ),
        name="forward_products",
    )(owners, focusing, v_factors)


def prepare_kernel(count_col, half, owners, ranks, onsets, table, u_factors, u_here, mixing, mask, tile_of, held, sem):
    column = lax.axis_index("col")
    mine = lax.axis_index("freq")
    copy = pltpu.make_async_copy(u_factors.at[0, :, pl.ds(mine * half, half)], u_here, sem)
    copy.start()
    list_tiles(owners, tile_of, held, count_col, 2 * half)
    times = lax.broadcasted_iota(jnp.int32, (NT, TS), 0)
    row_id = lax.broadcasted_iota(jnp.int32, (R, mask.shape[2]), 0)
    for s in range(half):
        tile = tile_of[column * 2 * half + mine * half + s]
        inside = jnp.where(times < onsets[tile], 1.0, 0.0).astype(jnp.bfloat16)
        tables = dot(table[mine], inside, 1, 0)
        count = tables.shape[0] // 3
        mixing[s] = tables[:count] + tables[count : 2 * count] + tables[2 * count :]
        pieces = [jnp.where(row_id < ranks[tile, j], 1.0, 0.0) for j in range(mask.shape[1] // R)]
        mask[s] = jnp.concatenate(pieces, axis=0).astype(jnp.bfloat16)
    copy.wait()


def prepare(count_col, half, columns, owners, tile_ranks, onsets, table, u_factors):
    shape = (2, half) + u_factors.shape[3:]
    vmem = pl.BlockSpec(memory_space=pltpu.VMEM)
    return pl.pallas_call(
        functools.partial(prepare_kernel, count_col, half),
        in_specs=[pl.BlockSpec(memory_space=pltpu.SMEM)] * 2 + [vmem, vmem, pl.BlockSpec(memory_space=pl.ANY)],
        out_specs=[vmem, vmem, vmem],
        out_shape=[
            jax.ShapeDtypeStruct(shape, jnp.bfloat16),
            jax.ShapeDtypeStruct((half, table.shape[1] // 3, TS), jnp.float32),
            jax.ShapeDtypeStruct((half, shape[2], columns), jnp.bfloat16),
        ],
        scratch_shapes=[
            pltpu.SMEM((count_col * 2 * half,), jnp.int32),
            pltpu.SMEM((count_col,), jnp.int32),
            pltpu.SemaphoreType.DMA,
        ],
        compiler_params=pltpu.CompilerParams(vmem_limit_bytes=40 * 2**20),
        cost_estimate=pl.CostEstimate(flops=0, bytes_accessed=4 * int(np.prod(shape)), transcendentals=0),
        name="prepare",
    )(owners, tile_ranks, onsets, table, u_factors)


def stack_coefficients(column, arrived, vis, slot, mask, matrix):
    strip = arrived[0].shape[1]
    for d, ref in enumerate(arrived):
        start = pl.multiple_of((column ^ d) * strip, strip)
        values = ref[slot] * mask[slot, pl.ds(start, strip), :]
        matrix[0, pl.ds(start, strip), :] = values
        matrix[1, pl.ds(start, strip), :] = jnp.concatenate([-values[:, vis:], values[:, :vis]], axis=1)


def own_field_kernel(count_col, half, mask, u_own, *refs):
    arrived = refs[:count_col]
    field, coefs = refs[count_col:]
    column = lax.axis_index("col")
    rows, columns = coefs.shape[2:]
    for s in range(half):
        stack_coefficients(column, arrived, columns // 2, s, mask, coefs.at[s])
        factors = u_own[:, s].reshape(2 * rows, TS)
        field[s] = dot(coefs[s].reshape(2 * rows, columns), factors, 0, 0).astype(jnp.bfloat16)


def own_field(count_col, half, mask, u_own, arrived):
    columns = arrived[0].shape[2]
    rows = u_own.shape[2]
    vmem = pl.BlockSpec(memory_space=pltpu.VMEM)
    return pl.pallas_call(
        functools.partial(own_field_kernel, count_col, half),
        in_specs=[vmem] * (2 + count_col),
        out_specs=vmem,
        out_shape=jax.ShapeDtypeStruct((half, columns, TS), jnp.bfloat16),
        scratch_shapes=[pltpu.VMEM((half, 2, rows, columns), jnp.bfloat16)],
        compiler_params=pltpu.CompilerParams(vmem_limit_bytes=20 * 2**20),
        cost_estimate=pl.CostEstimate(
            flops=4 * half * rows * columns * TS, bytes_accessed=2 * half * rows * TS, transcendentals=0
        ),
        name="own_field",
    )(mask, u_own, *arrived)


def receiver_kernel(count_col, half, mask, mixing, own, u_own, *refs):
    arrived = refs[:count_col]
    u_other = refs[count_col : -2 * count_col - 5]
    outs = refs[-2 * count_col - 5 : -5]
    factors, coefs, field, windowed, sems = refs[-5:]
    column = lax.axis_index("col")
    place = lax.axis_index("grp") * 2 + lax.axis_index("rep")
    rows, columns = coefs.shape[2:]
    vis = columns // 2
    copies = []
    for n, ref in enumerate(u_other):
        cuts = len(u_other) // 4
        start = (place ^ (n // cuts)) * (rows // 4) + sum(ref.shape[2] for ref in u_other[: n % cuts])
        at = pl.ds(pl.multiple_of(start, 16), ref.shape[2])
        copies.append(pltpu.make_async_copy(ref, factors.at[:, :, at, :], sems.at[n]))
        copies[n].start()
    for s in range(half):
        stack_coefficients(column, arrived, vis, s, mask, coefs.at[s])
    for copy in copies:
        copy.wait()
    strip = arrived[0].shape[1]
    for s in range(half):
        matrix = factors[:, s].reshape(2 * rows, TS)
        field[s] = dot(coefs[s].reshape(2 * rows, columns), matrix, 0, 0).astype(jnp.bfloat16)
    for s in range(half):
        high = 64
        for lane in range(0, TS, 128):
            at = pl.ds(lane, 128)
            mix = mixing[s, :, at]
            for row in range(0, vis, high):
                inputs = []
                for source in (own, field):
                    for part in range(2):
                        inputs.append(source[s, pl.ds(part * vis + row, high), at].astype(jnp.float32))
                for p in range(4):
                    total = mix[4 * p : 4 * p + 1] * inputs[0]
                    for q in range(1, 4):
                        total = total + mix[4 * p + q : 4 * p + q + 1] * inputs[q]
                    windowed[s, p // 2, pl.ds((p % 2) * vis + row, high), at] = total.astype(jnp.bfloat16)
        for e in range(2):
            if e == 0:
                matrix = u_own[:, s].reshape(2 * rows, TS)
            back = dot(matrix, windowed[s, e], 1, 1)
            by_real, by_imag = back[:rows], back[rows:]
            adjoint = jnp.concatenate(
                [by_real[:, :vis] + by_imag[:, vis:], by_real[:, vis:] - by_imag[:, :vis]], axis=1
            )
            coefs[s, 0] = adjoint.astype(jnp.bfloat16) * mask[s]
            for d in range(count_col):
                start = pl.multiple_of((column ^ d) * strip, strip)
                outs[2 * d + e][s] = coefs[s, 0, pl.ds(start, strip), :]
            if e == 0:
                matrix = factors[:, s].reshape(2 * rows, TS)


def receiver_products(count_col, half, mask, mixing, own, arrived, u_own, u_other):
    strip, columns = arrived[0].shape[1:]
    rows = u_own.shape[2]
    vmem = pl.BlockSpec(memory_space=pltpu.VMEM)
    out = jax.ShapeDtypeStruct((half, strip, columns), jnp.bfloat16)
    return pl.pallas_call(
        functools.partial(receiver_kernel, count_col, half),
        in_specs=[vmem] * (4 + count_col + len(u_other)),
        out_specs=[vmem] * (2 * count_col),
        out_shape=[out] * (2 * count_col),
        scratch_shapes=[
            pltpu.VMEM((2, half, rows, TS), jnp.bfloat16),
            pltpu.VMEM((half, 2, rows, columns), jnp.bfloat16),
            pltpu.VMEM((half, columns, TS), jnp.bfloat16),
            pltpu.VMEM((half, 2, columns, TS), jnp.bfloat16),
            pltpu.SemaphoreType.DMA((len(u_other),)),
        ],
        compiler_params=pltpu.CompilerParams(vmem_limit_bytes=24 * 2**20),
        cost_estimate=pl.CostEstimate(
            flops=12 * half * rows * columns * TS, bytes_accessed=8 * half * rows * TS, transcendentals=0
        ),
        name="receiver_products",
    )(mask, mixing, own, u_own, *arrived, *u_other)


def update_kernel(count_col, half, owners, *refs):
    arrivals = refs[: 2 * count_col]
    focus, factors, out, out_here, gathered, adjoint, tile_of, held, sems = refs[2 * count_col :]
    column = lax.axis_index("col")
    mine = lax.axis_index("freq")
    two, vis, sources = out_here.shape
    rows = factors.shape[1]
    blocks = sources // TS
    width = 512
    capacity = 2 * half
    list_tiles(owners, tile_of, held, count_col, capacity)
    def gather(j):
        for s in range(half):
            for d in range(count_col):
                for e in range(2):
                    tile = tile_of[(column ^ d) * capacity + (mine ^ e) * half + s]
                    values = arrivals[2 * d + e][s].astype(jnp.float32)
                    gathered[j, pl.ds(pl.multiple_of(tile * R, 8), R), :] = values[j * R : (j + 1) * R]
        values = gathered[j]
        adjoint[j, :rows] = values.astype(jnp.bfloat16)
        adjoint[j, rows:] = jnp.concatenate([values[:, vis:], -values[:, :vis]], axis=1).astype(jnp.bfloat16)

    writes = []
    for n in range(sources // width):
        j = n * width // TS
        at = pl.ds(n * width, width)
        if n * width % TS == 0:
            gather(j)
        right = factors[:, :, at].reshape(2 * rows, width)
        wave = dot(adjoint[j], right, 0, 0)
        out_here[:, :, at] = focus[:, :, at] - wave.reshape(two, vis, width)
        writes.append(pltpu.make_async_copy(out_here.at[:, :, at], out.at[0, :, :, at], sems.at[n]))
        writes[n].start()
    for write in writes:
        write.wait()


def update_products(count_col, half, owners, arrivals, focusing, v_factors):
    vis, sources = focusing.shape[1:]
    rows = v_factors.shape[1]
    blocks = sources // TS
    smem = pl.BlockSpec(memory_space=pltpu.SMEM)
    vmem = pl.BlockSpec(memory_space=pltpu.VMEM)
    anywhere = pl.BlockSpec(memory_space=pl.ANY)
    return pl.pallas_call(
        functools.partial(update_kernel, count_col, half),
        in_specs=[smem] + [vmem] * (len(arrivals) + 2),
        out_specs=anywhere,
        out_shape=jax.ShapeDtypeStruct((1,) + focusing.shape, jnp.float32),
        scratch_shapes=[
            pltpu.VMEM(focusing.shape, jnp.float32),
            pltpu.VMEM((blocks, rows, 2 * vis), jnp.float32),
            pltpu.VMEM((blocks, 2 * rows, 2 * vis), jnp.bfloat16),
            pltpu.SMEM((count_col * 2 * half,), jnp.int32),
            pltpu.SMEM((count_col,), jnp.int32),
            pltpu.SemaphoreType.DMA((sources // 512,)),
        ],
        compiler_params=pltpu.CompilerParams(vmem_limit_bytes=24 * 2**20),
        cost_estimate=pl.CostEstimate(
            flops=8 * rows * vis * sources, bytes_accessed=16 * vis * sources + 4 * rows * sources, transcendentals=0
        ),
        name="update_products",
    )(owners, *arrivals, focusing, v_factors)


def swap(array, axis):
    return lax.ppermute(array, axis, [(0, 1), (1, 0)])


def exchange(arrays, count_col):
    moved = list(arrays)
    for d in range(count_col - 1, -1, -1):
        for e in (1, 0):
            offset = 2 * d + e
            if offset:
                moved[offset] = lax.ppermute(
                    arrays[offset], ("col", "freq"), [(i, i ^ offset) for i in range(2 * count_col)]
                )
    return moved


def per_device_paired(focusing, v_factors, u_factors, tile_ranks, owners, onsets):
    count_col = lax.axis_size("col")
    mine = lax.axis_index("freq")
    capacity = u_factors.shape[2]
    half = capacity // 2
    rows = u_factors.shape[3]
    place = lax.axis_index("grp") * 2 + lax.axis_index("rep")
    table = jnp.asarray(mixing_table(2))
    tile_onsets = onsets.reshape(NR // TS, 1, TS)
    quarter = rows // 4
    cuts = (quarter // 2, quarter - quarter // 2)
    first = []
    share = lax.dynamic_slice(
        u_factors, (0, 0, (1 - mine) * half, place * quarter, 0), (1, 2, half, quarter, TS)
    ).reshape(2, half, quarter, TS)
    first = [swap(share[:, :, : cuts[0]], "freq"), swap(share[:, :, cuts[0] :], "freq")]
    *outgoing, focus_here, v_here = forward_products(count_col, half, focusing, v_factors, owners)
    def move(offset, payload):
        return lax.ppermute(payload, ("col", "freq"), [(i, i ^ offset) for i in range(2 * count_col)])
    arrived = list(outgoing)
    far, _ = lax.optimization_barrier((u_factors, outgoing[0]))
    u_here, mixing, mask = prepare(
        count_col, half, outgoing[0].shape[2], owners, tile_ranks, tile_onsets, table, far
    )
    first[0], _ = lax.optimization_barrier((first[0], outgoing[0]))
    second = [swap(first[0], "grp")]
    for offset in (6, 4, 2):
        arrived[offset] = move(offset, arrived[offset])
    held = lax.optimization_barrier(tuple(arrived + first + [u_here, mixing] + second))
    arrived, (*first, u_here, mixing, head) = list(held[: 2 * count_col]), held[2 * count_col :]
    second = [head, swap(first[1], "grp")]
    for offset in (7, 5, 3, 1):
        arrived[offset] = move(offset, arrived[offset])
    tied = lax.optimization_barrier(tuple(first + [arrived[n] for n in (7, 5)]))
    first = list(tied[:2])
    mates = [swap(piece, "rep") for piece in first]
    own = own_field(count_col, half, mask, u_here, arrived[::2])
    held = lax.optimization_barrier(tuple(arrived + first + second + [u_here, own]))
    arrived, (*pieces, u_here, own) = list(held[: 2 * count_col]), held[2 * count_col :]
    first, second = pieces[:2], pieces[2:4]
    gathered = first + mates + second + [swap(piece, "rep") for piece in second]
    back = receiver_products(count_col, half, mask, mixing, own, arrived[1::2], u_here, gathered)
    returned = exchange(back, count_col)
    return update_products(count_col, half, owners, returned, focus_here, v_here)


def per_device(focusing, v_factors, u_factors, tile_ranks, owners, onsets):
    count_col = lax.axis_size("col")
    paired = (
        lax.axis_size("freq") == 2
        and lax.axis_size("grp") == 2
        and lax.axis_size("rep") == 2
        and focusing.shape[0] == 1
        and count_col & (count_col - 1) == 0
        and u_factors.shape[2] % 2 == 0
        and u_factors.shape[2] * count_col == NR // TS
        and focusing.shape[2] % 128 == 0
        and focusing.shape[3] % TS == 0
        and (focusing.shape[3] // TS * R) % 16 == 0
        and u_factors.shape[3] % 64 == 0
    )
    chosen = per_device_paired if paired else per_device_general
    return chosen(focusing, v_factors, u_factors, tile_ranks, owners, onsets)


def solution(mesh):
    return jax.shard_map(
        per_device,
        mesh=mesh,
        in_specs=(
            P("freq", None, ("grp", "rep"), "col"),
            P("freq", None, None, "col"),
            P("freq", None, "col", None, None),
            P(),
            P(),
            P(),
        ),
        out_specs=P("freq", None, ("grp", "rep"), "col"),
        check_vma=False,
    )
```

```python
import functools

import jax
import jax.numpy as jnp
import ml_dtypes
import numpy as np
from jax import lax
from jax.experimental import pallas as pl
from jax.experimental.pallas import tpu as pltpu
from jax.sharding import PartitionSpec as P

TS = 1024
R = 24
NR = 16384
NS = 16384
NT = 512
KLO = 8


def window_tables(count_freq, onset_rows):
    time_steps = jnp.arange(NT, dtype=jnp.int32)
    freq_bins = KLO + jnp.arange(count_freq, dtype=jnp.int32)
    phases = 2.0 * jnp.pi * (freq_bins[None, :] * time_steps[:, None] % NT).astype(jnp.float32) / NT
    cosine = jnp.cos(phases)
    sines = jnp.sin(phases)
    analyse = jnp.stack([cosine, -sines], axis=2).reshape(NT, 2 * count_freq)
    synthesis = analyse * (2.0 / NT)
    product_table = (analyse[:, :, None] * synthesis[:, None, :]).reshape(
        NT, 4 * count_freq * count_freq
    )
    running_table = jnp.cumsum(product_table, axis=0)
    mixing = jnp.take(running_table, onset_rows - 1, axis=0)
    return mixing.reshape(-1, 2 * count_freq, 2 * count_freq)


def kernel_product(einsum_recipe, left_side, right_side):
    return jnp.einsum(einsum_recipe, left_side, right_side, preferred_element_type=jnp.float32)


def per_device_general(focusing, v_factors, u_factors, tile_ranks, owners, onsets):
    count_col = lax.axis_size("col")
    my_column = lax.axis_index("col")
    count_freq = lax.axis_size("freq")
    my_freq = lax.axis_index("freq")
    freq_dev = focusing.shape[0]
    vis_dev = focusing.shape[2]
    sources_dev = focusing.shape[3]
    capacity = u_factors.shape[2]
    block_width = min(sources_dev, TS)
    blocks_dev = sources_dev // block_width
    per_tile = TS // block_width
    all_blocks = count_col * blocks_dev
    row_tiles = NR // TS
    col_tiles = NS // TS
    freq_all = freq_dev * count_freq
    quarter = TS // count_freq
    tile_ids = jnp.arange(row_tiles, dtype=jnp.int32)
    same_owner = owners[:, None] == owners[None, :]
    earlier = tile_ids[None, :] < tile_ids[:, None]
    slot_of = jnp.sum((same_owner & earlier).astype(jnp.int32), axis=1)
    slot_ids = jnp.arange(capacity, dtype=jnp.int32)
    routing = (owners[None, None, :] == jnp.arange(count_col, dtype=jnp.int32)[:, None, None]) & (
        slot_of[None, None, :] == slot_ids[None, :, None]
    )
    lower_routing = routing.astype(jnp.bfloat16)
    my_slots = ((owners[None, :] == my_column) & (slot_of[None, :] == slot_ids[:, None])).astype(
        jnp.int32
    )
    slot_ranks = jnp.sum(my_slots[:, :, None] * tile_ranks[None, :, :], axis=1)
    rank_mask = (jnp.arange(R, dtype=jnp.int32)[None, None, :] < slot_ranks[:, :, None]).astype(
        jnp.float32
    )
    slot_onsets = jnp.sum(my_slots[:, :, None] * onsets.reshape(row_tiles, TS)[None], axis=1)
    slot_onsets = jnp.maximum(slot_onsets, 1)
    focus_low = focusing.astype(jnp.bfloat16).reshape(freq_dev, 2, vis_dev, blocks_dev, block_width)
    factors_v = v_factors.reshape(freq_dev, 2, row_tiles, R, blocks_dev, block_width)
    einsum_recipe = "fikbs,fvbs->ifbkv"
    real_portion = kernel_product(einsum_recipe, factors_v[:, 0], focus_low[:, 0]) - kernel_product(
        einsum_recipe, factors_v[:, 1], focus_low[:, 1]
    )
    part_imag = kernel_product(einsum_recipe, factors_v[:, 0], focus_low[:, 1]) + kernel_product(
        einsum_recipe, factors_v[:, 1], focus_low[:, 0]
    )
    partial_sums = jnp.stack([real_portion, part_imag], axis=3).astype(jnp.bfloat16)
    outgoing_parts = kernel_product("way,ymleno->amwleno", lower_routing, partial_sums).astype(
        jnp.bfloat16
    )
    outgoing_parts = outgoing_parts.reshape(capacity, freq_dev, all_blocks, 2, R, vis_dev)
    arrived = lax.all_to_all(outgoing_parts, "col", split_axis=2, concat_axis=2, tiled=True)
    coefficients = jnp.sum(
        arrived.astype(jnp.float32).reshape(capacity, freq_dev, col_tiles, per_tile, 2, R, vis_dev),
        axis=3,
    )
    coefficients = (coefficients * rank_mask[:, None, :, None, :, None]).astype(jnp.bfloat16)
    factors_u = u_factors.reshape(freq_dev, 2, capacity, col_tiles, R, TS)
    uform = "fcjka,cfjkv->cfav"
    field_real = kernel_product(uform, factors_u[:, 0], coefficients[:, :, :, 0]) - kernel_product(
        uform, factors_u[:, 1], coefficients[:, :, :, 1]
    )
    field_imag = kernel_product(uform, factors_u[:, 0], coefficients[:, :, :, 1]) + kernel_product(
        uform, factors_u[:, 1], coefficients[:, :, :, 0]
    )
    receiver_field = jnp.stack([field_real, field_imag], axis=2).astype(jnp.bfloat16)
    turned = lax.all_to_all(receiver_field, "freq", split_axis=3, concat_axis=1, tiled=True)
    quarter_onsets = lax.dynamic_slice_in_dim(slot_onsets, my_freq * quarter, quarter, 1)
    mixing = window_tables(freq_all, quarter_onsets.reshape(-1)).reshape(
        capacity, quarter, 2 * freq_all, 2 * freq_all
    )
    flat_field = turned.reshape(capacity, 2 * freq_all, quarter, vis_dev).astype(jnp.float32)
    mixed_field = jnp.einsum("crpq,cqrv->cprv", mixing, flat_field, precision=lax.Precision.HIGHEST)
    mixed_field = mixed_field.astype(jnp.bfloat16).reshape(capacity, freq_all, 2, quarter, vis_dev)
    windowed = lax.all_to_all(mixed_field, "freq", split_axis=1, concat_axis=3, tiled=True)
    aform = "fcjka,cfav->cfjkv"
    back_real = kernel_product(aform, factors_u[:, 0], windowed[:, :, 0]) + kernel_product(
        aform, factors_u[:, 1], windowed[:, :, 1]
    )
    back_imag = kernel_product(aform, factors_u[:, 0], windowed[:, :, 1]) - kernel_product(
        aform, factors_u[:, 1], windowed[:, :, 0]
    )
    adjoint = jnp.stack([back_real, back_imag], axis=3) * rank_mask[:, None, :, None, :, None]
    adjoint = adjoint.astype(jnp.bfloat16)
    spread = jnp.broadcast_to(
        adjoint[:, :, :, None], (capacity, freq_dev, col_tiles, per_tile, 2, R, vis_dev)
    )
    spread = spread.reshape(capacity, freq_dev, all_blocks, 2, R, vis_dev)
    result_field = lax.all_to_all(spread, "col", split_axis=2, concat_axis=2, tiled=True)
    result_field = result_field.reshape(capacity, freq_dev, count_col, blocks_dev, 2, R, vis_dev)
    row_share = kernel_product("prq,rjpagwu->qjagwu", lower_routing, result_field).astype(
        jnp.bfloat16
    )
    wform = "fikbs,ifbkv->fvbs"
    wave_real = kernel_product(wform, factors_v[:, 0], row_share[:, :, :, 0]) + kernel_product(
        wform, factors_v[:, 1], row_share[:, :, :, 1]
    )
    wave_imag = kernel_product(wform, factors_v[:, 0], row_share[:, :, :, 1]) - kernel_product(
        wform, factors_v[:, 1], row_share[:, :, :, 0]
    )
    wave_field = jnp.stack([wave_real, wave_imag], axis=1).reshape(
        freq_dev, 2, vis_dev, sources_dev
    )
    return focusing - wave_field


def mixing_table(count_freq):
    time_steps = np.arange(NT)
    rows = []
    for mine in range(count_freq):
        bins = [KLO + mine] + [KLO + f for f in range(count_freq) if f != mine]
        phases = 2.0 * np.pi * ((np.array(bins)[:, None] * time_steps[None, :]) % NT) / NT
        analyse = np.stack([np.cos(phases), -np.sin(phases)], axis=1).reshape(2 * count_freq, NT)
        table = (analyse[:, None, :] * analyse[None, :, :] * (2.0 / NT)).reshape(-1, NT)
        rest = table.astype(np.float32)
        parts = []
        for _ in range(3):
            part = rest.astype(ml_dtypes.bfloat16)
            parts.append(part)
            rest = rest - part.astype(np.float32)
        rows.append(np.concatenate(parts, axis=0))
    return np.stack(rows)


def dot(left, right, left_dim, right_dim):
    return lax.dot_general(
        left, right, (((left_dim,), (right_dim,)), ((), ())), preferred_element_type=jnp.float32
    )


def list_tiles(owners, tile_of, held, count_col, capacity):
    for owner in range(count_col):
        held[owner] = 0
    for tile in range(owners.shape[0]):
        owner = owners[tile]
        slot = held[owner]
        tile_of[owner * capacity + slot] = tile
        held[owner] = slot + 1


def forward_kernel(count_col, half, owners_far, focus, factors, *refs):
    outs = refs[: 2 * count_col]
    focus_here, factors_here, sums, owners, tile_of, held, sems = refs[2 * count_col :]
    column = lax.axis_index("col")
    mine = lax.axis_index("freq")
    two, vis, sources = focus_here.shape
    blocks = sources // TS
    copies = []
    for j in range(blocks):
        at = pl.ds(j * TS, TS)
        copies.append(
            [
                pltpu.make_async_copy(focus.at[0, :, :, at], focus_here.at[:, :, at], sems.at[0, j]),
                pltpu.make_async_copy(factors.at[0, :, :, at], factors_here.at[:, :, at], sems.at[1, j]),
            ]
        )
        for copy in copies[j]:
            copy.start()
    owners_copy = pltpu.make_async_copy(owners_far, owners, sems.at[2, 0])
    owners_copy.start()
    owners_copy.wait()
    capacity = 2 * half
    list_tiles(owners, tile_of, held, count_col, capacity)
    for j in range(blocks):
        for copy in copies[j]:
            copy.wait()
        at = pl.ds(j * TS, TS)
        low = focus_here[:, :, at].astype(jnp.bfloat16).reshape(two * vis, TS)
        by_real = dot(factors_here[0, :, at], low, 1, 1)
        by_imag = dot(factors_here[1, :, at], low, 1, 1)
        sums[j, :, :vis] = by_real[:, :vis] - by_imag[:, vis:]
        sums[j, :, vis:] = by_real[:, vis:] + by_imag[:, :vis]
    for d in range(count_col):
        for e in range(2):
            for s in range(half):
                tile = tile_of[(column ^ d) * capacity + (mine ^ e) * half + s]
                at = pl.ds(pl.multiple_of(tile * R, 8), R)
                pieces = [sums[j, at, :] for j in range(blocks)]
                outs[2 * d + e][s] = jnp.concatenate(pieces, axis=0).astype(jnp.bfloat16)


def forward_products(count_col, half, focusing, v_factors, owners):
    vis, sources = focusing.shape[2:]
    rows = v_factors.shape[2]
    blocks = sources // TS
    out = jax.ShapeDtypeStruct((half, blocks * R, 2 * vis), jnp.bfloat16)
    vmem = pl.BlockSpec(memory_space=pltpu.VMEM)
    anywhere = pl.BlockSpec(memory_space=pl.ANY)
    return pl.pallas_call(
        functools.partial(forward_kernel, count_col, half),
        in_specs=[anywhere] * 3,
        out_specs=[vmem] * (2 * count_col + 2),
        out_shape=[out] * (2 * count_col)
        + [
            jax.ShapeDtypeStruct(focusing.shape[1:], jnp.float32),
            jax.ShapeDtypeStruct(v_factors.shape[1:], jnp.bfloat16),
        ],
        scratch_shapes=[
            pltpu.VMEM((blocks, rows, 2 * vis), jnp.float32),
            pltpu.SMEM(owners.shape, jnp.int32),
            pltpu.SMEM((count_col * 2 * half,), jnp.int32),
            pltpu.SMEM((count_col,), jnp.int32),
            pltpu.SemaphoreType.DMA((3, blocks)),
        ],
        compiler_params=pltpu.CompilerParams(vmem_limit_bytes=46 * 2**20),
        cost_estimate=pl.CostEstimate(
            flops=8 * rows * vis * sources, bytes_accessed=8 * vis * sources + 4 * rows * sources, transcendentals=0
        ),
        name="forward_products",
    )(owners, focusing, v_factors)


def prepare_kernel(count_col, half, owners, ranks, onsets, table, u_factors, u_here, mixing, mask, tile_of, held, sem):
    column = lax.axis_index("col")
    mine = lax.axis_index("freq")
    copy = pltpu.make_async_copy(u_factors.at[0, :, pl.ds(mine * half, half)], u_here, sem)
    copy.start()
    list_tiles(owners, tile_of, held, count_col, 2 * half)
    times = lax.broadcasted_iota(jnp.int32, (NT, TS), 0)
    row_id = lax.broadcasted_iota(jnp.int32, (R, mask.shape[2]), 0)
    for s in range(half):
        tile = tile_of[column * 2 * half + mine * half + s]
        inside = jnp.where(times < onsets[tile], 1.0, 0.0).astype(jnp.bfloat16)
        tables = dot(table[mine], inside, 1, 0)
        count = tables.shape[0] // 3
        mixing[s] = tables[:count] + tables[count : 2 * count] + tables[2 * count :]
        pieces = [jnp.where(row_id < ranks[tile, j], 1.0, 0.0) for j in range(mask.shape[1] // R)]
        mask[s] = jnp.concatenate(pieces, axis=0).astype(jnp.bfloat16)
    copy.wait()


def prepare(count_col, half, columns, owners, tile_ranks, onsets, table, u_factors):
    shape = (2, half) + u_factors.shape[3:]
    vmem = pl.BlockSpec(memory_space=pltpu.VMEM)
    return pl.pallas_call(
        functools.partial(prepare_kernel, count_col, half),
        in_specs=[pl.BlockSpec(memory_space=pltpu.SMEM)] * 2 + [vmem, vmem, pl.BlockSpec(memory_space=pl.ANY)],
        out_specs=[vmem, vmem, vmem],
        out_shape=[
            jax.ShapeDtypeStruct(shape, jnp.bfloat16),
            jax.ShapeDtypeStruct((half, table.shape[1] // 3, TS), jnp.float32),
            jax.ShapeDtypeStruct((half, shape[2], columns), jnp.bfloat16),
        ],
        scratch_shapes=[
            pltpu.SMEM((count_col * 2 * half,), jnp.int32),
            pltpu.SMEM((count_col,), jnp.int32),
            pltpu.SemaphoreType.DMA,
        ],
        compiler_params=pltpu.CompilerParams(vmem_limit_bytes=40 * 2**20),
        cost_estimate=pl.CostEstimate(flops=0, bytes_accessed=4 * int(np.prod(shape)), transcendentals=0),
        name="prepare",
    )(owners, tile_ranks, onsets, table, u_factors)


def stack_coefficients(column, arrived, vis, slot, mask, matrix):
    strip = arrived[0].shape[1]
    for d, ref in enumerate(arrived):
        start = pl.multiple_of((column ^ d) * strip, strip)
        values = ref[slot] * mask[slot, pl.ds(start, strip), :]
        matrix[0, pl.ds(start, strip), :] = values
        matrix[1, pl.ds(start, strip), :] = jnp.concatenate([-values[:, vis:], values[:, :vis]], axis=1)


def own_field_kernel(count_col, half, mask, u_own, *refs):
    arrived = refs[:count_col]
    field, coefs = refs[count_col:]
    column = lax.axis_index("col")
    rows, columns = coefs.shape[2:]
    for s in range(half):
        stack_coefficients(column, arrived, columns // 2, s, mask, coefs.at[s])
        factors = u_own[:, s].reshape(2 * rows, TS)
        field[s] = dot(coefs[s].reshape(2 * rows, columns), factors, 0, 0).astype(jnp.bfloat16)


def own_field(count_col, half, mask, u_own, arrived):
    columns = arrived[0].shape[2]
    rows = u_own.shape[2]
    vmem = pl.BlockSpec(memory_space=pltpu.VMEM)
    return pl.pallas_call(
        functools.partial(own_field_kernel, count_col, half),
        in_specs=[vmem] * (2 + count_col),
        out_specs=vmem,
        out_shape=jax.ShapeDtypeStruct((half, columns, TS), jnp.bfloat16),
        scratch_shapes=[pltpu.VMEM((half, 2, rows, columns), jnp.bfloat16)],
        compiler_params=pltpu.CompilerParams(vmem_limit_bytes=20 * 2**20),
        cost_estimate=pl.CostEstimate(
            flops=4 * half * rows * columns * TS, bytes_accessed=2 * half * rows * TS, transcendentals=0
        ),
        name="own_field",
    )(mask, u_own, *arrived)


def copy_quarters(pieces, half_place, turn, matrix, sems):
    copies = []
    quarter = matrix.shape[2] // 2
    for n in range(2):
        start = (turn ^ n) * quarter
        for cut in range(len(pieces) // 2):
            ref = pieces[cut * 2 + n]
            at = pl.ds(pl.multiple_of(start, 16), ref.shape[2])
            copies.append(pltpu.make_async_copy(ref, matrix.at[:, :, at, :], sems.at[cut * 2 + n]))
            copies[-1].start()
            start = start + ref.shape[2]
    return copies


def stack_other(column, arrived, mask, slot, coefs):
    strip, columns = arrived[0].shape[1:]
    vis = columns // 2
    for d, ref in enumerate(arrived):
        values = ref[slot] * mask[slot, pl.ds(pl.multiple_of((column ^ d) * strip, strip), strip), :]
        coefs[0, column ^ d] = values
        coefs[1, column ^ d] = jnp.concatenate([-values[:, vis:], values[:, :vis]], axis=1)


def other_field(coefs, half_place, matrix):
    rows, width = matrix.shape[1:]
    left = coefs[:, pl.ds(2 * half_place, 2)].reshape(2 * rows, coefs.shape[3])
    return dot(left, matrix.reshape(2 * rows, width), 0, 0)


def near_kernel(count_col, half, mask, *refs):
    arrived = refs[:count_col]
    pieces = refs[count_col:-4]
    near, partial, coefs, sems = refs[-4:]
    column = lax.axis_index("col")
    group = lax.axis_index("grp")
    copies = copy_quarters(pieces, group, lax.axis_index("rep"), near, sems)
    for s in range(half):
        stack_other(column, arrived, mask, s, coefs.at[s])
    for copy in copies:
        copy.wait()
    for s in range(half):
        partial[s] = other_field(coefs.at[s], group, near[:, s])


def near_products(count_col, half, mask, arrived, pieces):
    strip, columns = arrived[0].shape[1:]
    vmem = pl.BlockSpec(memory_space=pltpu.VMEM)
    return pl.pallas_call(
        functools.partial(near_kernel, count_col, half),
        in_specs=[vmem] * (1 + count_col + len(pieces)),
        out_specs=[vmem] * 2,
        out_shape=[
            jax.ShapeDtypeStruct((2, half, 2 * strip, TS), jnp.bfloat16),
            jax.ShapeDtypeStruct((half, columns, TS), jnp.float32),
        ],
        scratch_shapes=[
            pltpu.VMEM((half, 2, count_col, strip, columns), jnp.bfloat16),
            pltpu.SemaphoreType.DMA((len(pieces),)),
        ],
        compiler_params=pltpu.CompilerParams(vmem_limit_bytes=16 * 2**20),
        cost_estimate=pl.CostEstimate(
            flops=8 * half * strip * columns * TS, bytes_accessed=8 * half * strip * TS, transcendentals=0
        ),
        name="near_products",
    )(mask, *arrived, *pieces)


def receiver_kernel(count_col, half, mask, mixing, own, u_own, near, partial, *refs):
    arrived = refs[:count_col]
    pieces = refs[count_col : -2 * count_col - 6]
    outs = refs[-2 * count_col - 6 : -6]
    far, coefs, field, windowed, adjoint, sems = refs[-6:]
    column = lax.axis_index("col")
    group = lax.axis_index("grp")
    strip, columns = arrived[0].shape[1:]
    rows = adjoint.shape[2]
    vis = columns // 2
    copies = copy_quarters(pieces, 1 - group, lax.axis_index("rep"), far, sems)
    for s in range(half):
        stack_other(column, arrived, mask, s, coefs.at[s])
    for copy in copies:
        copy.wait()
    for s in range(half):
        field[s] = (partial[s] + other_field(coefs.at[s], 1 - group, far[:, s])).astype(jnp.bfloat16)
    for s in range(half):
        high = 64
        for lane in range(0, TS, 128):
            at = pl.ds(lane, 128)
            mix = mixing[s, :, at]
            for row in range(0, vis, high):
                inputs = []
                for source in (own, field):
                    for part in range(2):
                        inputs.append(source[s, pl.ds(part * vis + row, high), at].astype(jnp.float32))
                for p in range(4):
                    total = mix[4 * p : 4 * p + 1] * inputs[0]
                    for q in range(1, 4):
                        total = total + mix[4 * p + q : 4 * p + q + 1] * inputs[q]
                    windowed[s, p // 2, pl.ds((p % 2) * vis + row, high), at] = total.astype(jnp.bfloat16)
        for e in range(2):
            parts = [(u_own, 0)] if e == 0 else [(near, group * 2 * strip), (far, (1 - group) * 2 * strip)]
            for factors, start in parts:
                here = factors.shape[2]
                back = dot(factors[:, s].reshape(2 * here, TS), windowed[s, e], 1, 1)
                by_real, by_imag = back[:here], back[here:]
                values = jnp.concatenate(
                    [by_real[:, :vis] + by_imag[:, vis:], by_real[:, vis:] - by_imag[:, :vis]], axis=1
                )
                at = pl.ds(start if e == 0 else pl.multiple_of(start, strip), here)
                adjoint[s, e, at, :] = values.astype(jnp.bfloat16) * mask[s, at, :]
            for d in range(count_col):
                start = pl.multiple_of((column ^ d) * strip, strip)
                outs[2 * d + e][s] = adjoint[s, e, pl.ds(start, strip), :]


def receiver_products(count_col, half, mask, mixing, own, arrived, u_own, near, partial, pieces):
    strip, columns = arrived[0].shape[1:]
    rows = u_own.shape[2]
    vmem = pl.BlockSpec(memory_space=pltpu.VMEM)
    out = jax.ShapeDtypeStruct((half, strip, columns), jnp.bfloat16)
    return pl.pallas_call(
        functools.partial(receiver_kernel, count_col, half),
        in_specs=[vmem] * (6 + count_col + len(pieces)),
        out_specs=[vmem] * (2 * count_col),
        out_shape=[out] * (2 * count_col),
        scratch_shapes=[
            pltpu.VMEM((2, half, 2 * strip, TS), jnp.bfloat16),
            pltpu.VMEM((half, 2, count_col, strip, columns), jnp.bfloat16),
            pltpu.VMEM((half, columns, TS), jnp.bfloat16),
            pltpu.VMEM((half, 2, columns, TS), jnp.bfloat16),
            pltpu.VMEM((half, 2, rows, columns), jnp.bfloat16),
            pltpu.SemaphoreType.DMA((len(pieces),)),
        ],
        compiler_params=pltpu.CompilerParams(vmem_limit_bytes=24 * 2**20),
        cost_estimate=pl.CostEstimate(
            flops=12 * half * rows * columns * TS, bytes_accessed=8 * half * rows * TS, transcendentals=0
        ),
        name="receiver_products",
    )(mask, mixing, own, u_own, near, partial, *arrived, *pieces)


def update_kernel(count_col, half, owners, *refs):
    arrivals = refs[: 2 * count_col]
    focus, factors, out, out_here, gathered, adjoint, tile_of, held, sems = refs[2 * count_col :]
    column = lax.axis_index("col")
    mine = lax.axis_index("freq")
    two, vis, sources = out_here.shape
    rows = factors.shape[1]
    blocks = sources // TS
    width = 512
    capacity = 2 * half
    list_tiles(owners, tile_of, held, count_col, capacity)
    def gather(j):
        for s in range(half):
            for d in range(count_col):
                for e in range(2):
                    tile = tile_of[(column ^ d) * capacity + (mine ^ e) * half + s]
                    values = arrivals[2 * d + e][s].astype(jnp.float32)
                    gathered[j, pl.ds(pl.multiple_of(tile * R, 8), R), :] = values[j * R : (j + 1) * R]
        values = gathered[j]
        adjoint[j, :rows] = values.astype(jnp.bfloat16)
        adjoint[j, rows:] = jnp.concatenate([values[:, vis:], -values[:, :vis]], axis=1).astype(jnp.bfloat16)

    writes = []
    for n in range(sources // width):
        j = n * width // TS
        at = pl.ds(n * width, width)
        if n * width % TS == 0:
            gather(j)
        right = factors[:, :, at].reshape(2 * rows, width)
        wave = dot(adjoint[j], right, 0, 0)
        out_here[:, :, at] = focus[:, :, at] - wave.reshape(two, vis, width)
        writes.append(pltpu.make_async_copy(out_here.at[:, :, at], out.at[0, :, :, at], sems.at[n]))
        writes[n].start()
    for write in writes:
        write.wait()


def update_products(count_col, half, owners, arrivals, focusing, v_factors):
    vis, sources = focusing.shape[1:]
    rows = v_factors.shape[1]
    blocks = sources // TS
    smem = pl.BlockSpec(memory_space=pltpu.SMEM)
    vmem = pl.BlockSpec(memory_space=pltpu.VMEM)
    anywhere = pl.BlockSpec(memory_space=pl.ANY)
    return pl.pallas_call(
        functools.partial(update_kernel, count_col, half),
        in_specs=[smem] + [vmem] * (len(arrivals) + 2),
        out_specs=anywhere,
        out_shape=jax.ShapeDtypeStruct((1,) + focusing.shape, jnp.float32),
        scratch_shapes=[
            pltpu.VMEM(focusing.shape, jnp.float32),
            pltpu.VMEM((blocks, rows, 2 * vis), jnp.float32),
            pltpu.VMEM((blocks, 2 * rows, 2 * vis), jnp.bfloat16),
            pltpu.SMEM((count_col * 2 * half,), jnp.int32),
            pltpu.SMEM((count_col,), jnp.int32),
            pltpu.SemaphoreType.DMA((sources // 512,)),
        ],
        compiler_params=pltpu.CompilerParams(vmem_limit_bytes=24 * 2**20),
        cost_estimate=pl.CostEstimate(
            flops=8 * rows * vis * sources, bytes_accessed=16 * vis * sources + 4 * rows * sources, transcendentals=0
        ),
        name="update_products",
    )(owners, *arrivals, focusing, v_factors)


def swap(array, axis):
    return lax.ppermute(array, axis, [(0, 1), (1, 0)])


def exchange(arrays, count_col):
    moved = list(arrays)
    for d in range(count_col - 1, -1, -1):
        for e in (1, 0):
            offset = 2 * d + e
            if offset:
                moved[offset] = lax.ppermute(
                    arrays[offset], ("col", "freq"), [(i, i ^ offset) for i in range(2 * count_col)]
                )
    return moved


def per_device_paired(focusing, v_factors, u_factors, tile_ranks, owners, onsets):
    count_col = lax.axis_size("col")
    mine = lax.axis_index("freq")
    capacity = u_factors.shape[2]
    half = capacity // 2
    rows = u_factors.shape[3]
    place = lax.axis_index("grp") * 2 + lax.axis_index("rep")
    table = jnp.asarray(mixing_table(2))
    tile_onsets = onsets.reshape(NR // TS, 1, TS)
    quarter = rows // 4
    cuts = (quarter // 2, quarter - quarter // 2)
    first = []
    share = lax.dynamic_slice(
        u_factors, (0, 0, (1 - mine) * half, place * quarter, 0), (1, 2, half, quarter, TS)
    ).reshape(2, half, quarter, TS)
    first = [swap(share[:, :, : cuts[0]], "freq"), swap(share[:, :, cuts[0] :], "freq")]
    *outgoing, focus_here, v_here = forward_products(count_col, half, focusing, v_factors, owners)
    def move(offset, payload):
        return lax.ppermute(payload, ("col", "freq"), [(i, i ^ offset) for i in range(2 * count_col)])
    arrived = list(outgoing)
    far, _ = lax.optimization_barrier((u_factors, outgoing[0]))
    u_here, mixing, mask = prepare(
        count_col, half, outgoing[0].shape[2], owners, tile_ranks, tile_onsets, table, far
    )
    first[0], _ = lax.optimization_barrier((first[0], outgoing[0]))
    second = [swap(first[0], "grp")]
    for offset in (4, 7, 2):
        arrived[offset] = move(offset, arrived[offset])
    held = lax.optimization_barrier(tuple(arrived + first + [u_here, mixing] + second))
    arrived, (*first, u_here, mixing, head) = list(held[: 2 * count_col]), held[2 * count_col :]
    second = [head, swap(first[1], "grp")]
    for offset in (5, 6, 3, 1):
        arrived[offset] = move(offset, arrived[offset])
    tied = lax.optimization_barrier(tuple(first + [arrived[n] for n in (5,)]))
    first = list(tied[:2])
    mates = [swap(piece, "rep") for piece in first]
    own = own_field(count_col, half, mask, u_here, arrived[::2])
    held = lax.optimization_barrier(tuple(arrived + first + second + [u_here, own]))
    arrived, (*pieces, u_here, own) = list(held[: 2 * count_col]), held[2 * count_col :]
    first, second = pieces[:2], pieces[2:4]
    near, partial = near_products(
        count_col, half, mask, arrived[1::2], [first[0], mates[0], first[1], mates[1]]
    )
    pieces = []
    for piece in second:
        pieces.extend([piece, swap(piece, "rep")])
    back = receiver_products(count_col, half, mask, mixing, own, arrived[1::2], u_here, near, partial, pieces)
    returned = exchange(back, count_col)
    return update_products(count_col, half, owners, returned, focus_here, v_here)


def per_device(focusing, v_factors, u_factors, tile_ranks, owners, onsets):
    count_col = lax.axis_size("col")
    paired = (
        lax.axis_size("freq") == 2
        and lax.axis_size("grp") == 2
        and lax.axis_size("rep") == 2
        and focusing.shape[0] == 1
        and count_col == 4
        and u_factors.shape[2] % 2 == 0
        and u_factors.shape[2] * count_col == NR // TS
        and focusing.shape[2] % 128 == 0
        and focusing.shape[3] % TS == 0
        and (focusing.shape[3] // TS * R) % 16 == 0
        and u_factors.shape[3] % 64 == 0
    )
    chosen = per_device_paired if paired else per_device_general
    return chosen(focusing, v_factors, u_factors, tile_ranks, owners, onsets)


def solution(mesh):
    return jax.shard_map(
        per_device,
        mesh=mesh,
        in_specs=(
            P("freq", None, ("grp", "rep"), "col"),
            P("freq", None, None, "col"),
            P("freq", None, "col", None, None),
            P(),
            P(),
            P(),
        ),
        out_specs=P("freq", None, ("grp", "rep"), "col"),
        check_vma=False,
    )
```

```python
import functools

import jax
import jax.numpy as jnp
import ml_dtypes
import numpy as np
from jax import lax
from jax.experimental import pallas as pl
from jax.experimental.pallas import tpu as pltpu
from jax.sharding import PartitionSpec as P

TS = 1024
R = 24
NR = 16384
NS = 16384
NT = 512
KLO = 8


def window_tables(count_freq, onset_rows):
    time_steps = jnp.arange(NT, dtype=jnp.int32)
    freq_bins = KLO + jnp.arange(count_freq, dtype=jnp.int32)
    phases = 2.0 * jnp.pi * (freq_bins[None, :] * time_steps[:, None] % NT).astype(jnp.float32) / NT
    cosine = jnp.cos(phases)
    sines = jnp.sin(phases)
    analyse = jnp.stack([cosine, -sines], axis=2).reshape(NT, 2 * count_freq)
    synthesis = analyse * (2.0 / NT)
    product_table = (analyse[:, :, None] * synthesis[:, None, :]).reshape(
        NT, 4 * count_freq * count_freq
    )
    running_table = jnp.cumsum(product_table, axis=0)
    mixing = jnp.take(running_table, onset_rows - 1, axis=0)
    return mixing.reshape(-1, 2 * count_freq, 2 * count_freq)


def kernel_product(einsum_recipe, left_side, right_side):
    return jnp.einsum(einsum_recipe, left_side, right_side, preferred_element_type=jnp.float32)


def per_device_general(focusing, v_factors, u_factors, tile_ranks, owners, onsets):
    count_col = lax.axis_size("col")
    my_column = lax.axis_index("col")
    count_freq = lax.axis_size("freq")
    my_freq = lax.axis_index("freq")
    freq_dev = focusing.shape[0]
    vis_dev = focusing.shape[2]
    sources_dev = focusing.shape[3]
    capacity = u_factors.shape[2]
    block_width = min(sources_dev, TS)
    blocks_dev = sources_dev // block_width
    per_tile = TS // block_width
    all_blocks = count_col * blocks_dev
    row_tiles = NR // TS
    col_tiles = NS // TS
    freq_all = freq_dev * count_freq
    quarter = TS // count_freq
    tile_ids = jnp.arange(row_tiles, dtype=jnp.int32)
    same_owner = owners[:, None] == owners[None, :]
    earlier = tile_ids[None, :] < tile_ids[:, None]
    slot_of = jnp.sum((same_owner & earlier).astype(jnp.int32), axis=1)
    slot_ids = jnp.arange(capacity, dtype=jnp.int32)
    routing = (owners[None, None, :] == jnp.arange(count_col, dtype=jnp.int32)[:, None, None]) & (
        slot_of[None, None, :] == slot_ids[None, :, None]
    )
    lower_routing = routing.astype(jnp.bfloat16)
    my_slots = ((owners[None, :] == my_column) & (slot_of[None, :] == slot_ids[:, None])).astype(
        jnp.int32
    )
    slot_ranks = jnp.sum(my_slots[:, :, None] * tile_ranks[None, :, :], axis=1)
    rank_mask = (jnp.arange(R, dtype=jnp.int32)[None, None, :] < slot_ranks[:, :, None]).astype(
        jnp.float32
    )
    slot_onsets = jnp.sum(my_slots[:, :, None] * onsets.reshape(row_tiles, TS)[None], axis=1)
    slot_onsets = jnp.maximum(slot_onsets, 1)
    focus_low = focusing.astype(jnp.bfloat16).reshape(freq_dev, 2, vis_dev, blocks_dev, block_width)
    factors_v = v_factors.reshape(freq_dev, 2, row_tiles, R, blocks_dev, block_width)
    einsum_recipe = "fikbs,fvbs->ifbkv"
    real_portion = kernel_product(einsum_recipe, factors_v[:, 0], focus_low[:, 0]) - kernel_product(
        einsum_recipe, factors_v[:, 1], focus_low[:, 1]
    )
    part_imag = kernel_product(einsum_recipe, factors_v[:, 0], focus_low[:, 1]) + kernel_product(
        einsum_recipe, factors_v[:, 1], focus_low[:, 0]
    )
    partial_sums = jnp.stack([real_portion, part_imag], axis=3).astype(jnp.bfloat16)
    outgoing_parts = kernel_product("way,ymleno->amwleno", lower_routing, partial_sums).astype(
        jnp.bfloat16
    )
    outgoing_parts = outgoing_parts.reshape(capacity, freq_dev, all_blocks, 2, R, vis_dev)
    arrived = lax.all_to_all(outgoing_parts, "col", split_axis=2, concat_axis=2, tiled=True)
    coefficients = jnp.sum(
        arrived.astype(jnp.float32).reshape(capacity, freq_dev, col_tiles, per_tile, 2, R, vis_dev),
        axis=3,
    )
    coefficients = (coefficients * rank_mask[:, None, :, None, :, None]).astype(jnp.bfloat16)
    factors_u = u_factors.reshape(freq_dev, 2, capacity, col_tiles, R, TS)
    uform = "fcjka,cfjkv->cfav"
    field_real = kernel_product(uform, factors_u[:, 0], coefficients[:, :, :, 0]) - kernel_product(
        uform, factors_u[:, 1], coefficients[:, :, :, 1]
    )
    field_imag = kernel_product(uform, factors_u[:, 0], coefficients[:, :, :, 1]) + kernel_product(
        uform, factors_u[:, 1], coefficients[:, :, :, 0]
    )
    receiver_field = jnp.stack([field_real, field_imag], axis=2).astype(jnp.bfloat16)
    turned = lax.all_to_all(receiver_field, "freq", split_axis=3, concat_axis=1, tiled=True)
    quarter_onsets = lax.dynamic_slice_in_dim(slot_onsets, my_freq * quarter, quarter, 1)
    mixing = window_tables(freq_all, quarter_onsets.reshape(-1)).reshape(
        capacity, quarter, 2 * freq_all, 2 * freq_all
    )
    flat_field = turned.reshape(capacity, 2 * freq_all, quarter, vis_dev).astype(jnp.float32)
    mixed_field = jnp.einsum("crpq,cqrv->cprv", mixing, flat_field, precision=lax.Precision.HIGHEST)
    mixed_field = mixed_field.astype(jnp.bfloat16).reshape(capacity, freq_all, 2, quarter, vis_dev)
    windowed = lax.all_to_all(mixed_field, "freq", split_axis=1, concat_axis=3, tiled=True)
    aform = "fcjka,cfav->cfjkv"
    back_real = kernel_product(aform, factors_u[:, 0], windowed[:, :, 0]) + kernel_product(
        aform, factors_u[:, 1], windowed[:, :, 1]
    )
    back_imag = kernel_product(aform, factors_u[:, 0], windowed[:, :, 1]) - kernel_product(
        aform, factors_u[:, 1], windowed[:, :, 0]
    )
    adjoint = jnp.stack([back_real, back_imag], axis=3) * rank_mask[:, None, :, None, :, None]
    adjoint = adjoint.astype(jnp.bfloat16)
    spread = jnp.broadcast_to(
        adjoint[:, :, :, None], (capacity, freq_dev, col_tiles, per_tile, 2, R, vis_dev)
    )
    spread = spread.reshape(capacity, freq_dev, all_blocks, 2, R, vis_dev)
    result_field = lax.all_to_all(spread, "col", split_axis=2, concat_axis=2, tiled=True)
    result_field = result_field.reshape(capacity, freq_dev, count_col, blocks_dev, 2, R, vis_dev)
    row_share = kernel_product("prq,rjpagwu->qjagwu", lower_routing, result_field).astype(
        jnp.bfloat16
    )
    wform = "fikbs,ifbkv->fvbs"
    wave_real = kernel_product(wform, factors_v[:, 0], row_share[:, :, :, 0]) + kernel_product(
        wform, factors_v[:, 1], row_share[:, :, :, 1]
    )
    wave_imag = kernel_product(wform, factors_v[:, 0], row_share[:, :, :, 1]) - kernel_product(
        wform, factors_v[:, 1], row_share[:, :, :, 0]
    )
    wave_field = jnp.stack([wave_real, wave_imag], axis=1).reshape(
        freq_dev, 2, vis_dev, sources_dev
    )
    return focusing - wave_field


def mixing_table(count_freq):
    time_steps = np.arange(NT)
    rows = []
    for mine in range(count_freq):
        bins = [KLO + mine] + [KLO + f for f in range(count_freq) if f != mine]
        phases = 2.0 * np.pi * ((np.array(bins)[:, None] * time_steps[None, :]) % NT) / NT
        analyse = np.stack([np.cos(phases), -np.sin(phases)], axis=1).reshape(2 * count_freq, NT)
        table = (analyse[:, None, :] * analyse[None, :, :] * (2.0 / NT)).reshape(-1, NT)
        rest = table.astype(np.float32)
        parts = []
        for _ in range(3):
            part = rest.astype(ml_dtypes.bfloat16)
            parts.append(part)
            rest = rest - part.astype(np.float32)
        rows.append(np.concatenate(parts, axis=0))
    return np.stack(rows)


def dot(left, right, left_dim, right_dim):
    return lax.dot_general(
        left, right, (((left_dim,), (right_dim,)), ((), ())), preferred_element_type=jnp.float32
    )


def list_tiles(owners, tile_of, held, count_col, capacity):
    for owner in range(count_col):
        held[owner] = 0
    for tile in range(owners.shape[0]):
        owner = owners[tile]
        slot = held[owner]
        tile_of[owner * capacity + slot] = tile
        held[owner] = slot + 1


def forward_kernel(count_col, half, owners_far, focus, factors, *refs):
    outs = refs[: 2 * count_col]
    focus_here, factors_here, sums, owners, tile_of, held, sems = refs[2 * count_col :]
    column = lax.axis_index("col")
    mine = lax.axis_index("freq")
    two, vis, sources = focus_here.shape
    blocks = sources // TS
    copies = []
    for j in range(blocks):
        at = pl.ds(j * TS, TS)
        copies.append(
            [
                pltpu.make_async_copy(focus.at[0, :, :, at], focus_here.at[:, :, at], sems.at[0, j]),
                pltpu.make_async_copy(factors.at[0, :, :, at], factors_here.at[:, :, at], sems.at[1, j]),
            ]
        )
        for copy in copies[j]:
            copy.start()
    owners_copy = pltpu.make_async_copy(owners_far, owners, sems.at[2, 0])
    owners_copy.start()
    owners_copy.wait()
    capacity = 2 * half
    list_tiles(owners, tile_of, held, count_col, capacity)
    for j in range(blocks):
        for copy in copies[j]:
            copy.wait()
        at = pl.ds(j * TS, TS)
        low = focus_here[:, :, at].astype(jnp.bfloat16).reshape(two * vis, TS)
        by_real = dot(factors_here[0, :, at], low, 1, 1)
        by_imag = dot(factors_here[1, :, at], low, 1, 1)
        sums[j, :, :vis] = by_real[:, :vis] - by_imag[:, vis:]
        sums[j, :, vis:] = by_real[:, vis:] + by_imag[:, :vis]
    for d in range(count_col):
        for e in range(2):
            for s in range(half):
                tile = tile_of[(column ^ d) * capacity + (mine ^ e) * half + s]
                at = pl.ds(pl.multiple_of(tile * R, 8), R)
                pieces = [sums[j, at, :] for j in range(blocks)]
                outs[2 * d + e][s] = jnp.concatenate(pieces, axis=0).astype(jnp.bfloat16)


def forward_products(count_col, half, focusing, v_factors, owners):
    vis, sources = focusing.shape[2:]
    rows = v_factors.shape[2]
    blocks = sources // TS
    out = jax.ShapeDtypeStruct((half, blocks * R, 2 * vis), jnp.bfloat16)
    vmem = pl.BlockSpec(memory_space=pltpu.VMEM)
    anywhere = pl.BlockSpec(memory_space=pl.ANY)
    return pl.pallas_call(
        functools.partial(forward_kernel, count_col, half),
        in_specs=[anywhere] * 3,
        out_specs=[vmem] * (2 * count_col + 2),
        out_shape=[out] * (2 * count_col)
        + [
            jax.ShapeDtypeStruct(focusing.shape[1:], jnp.float32),
            jax.ShapeDtypeStruct(v_factors.shape[1:], jnp.bfloat16),
        ],
        scratch_shapes=[
            pltpu.VMEM((blocks, rows, 2 * vis), jnp.float32),
            pltpu.SMEM(owners.shape, jnp.int32),
            pltpu.SMEM((count_col * 2 * half,), jnp.int32),
            pltpu.SMEM((count_col,), jnp.int32),
            pltpu.SemaphoreType.DMA((3, blocks)),
        ],
        compiler_params=pltpu.CompilerParams(vmem_limit_bytes=46 * 2**20),
        cost_estimate=pl.CostEstimate(
            flops=8 * rows * vis * sources, bytes_accessed=8 * vis * sources + 4 * rows * sources, transcendentals=0
        ),
        name="forward_products",
    )(owners, focusing, v_factors)


def prepare_kernel(count_col, half, owners, ranks, onsets, table, u_factors, u_here, mixing, mask, tile_of, held, sem):
    column = lax.axis_index("col")
    mine = lax.axis_index("freq")
    copy = pltpu.make_async_copy(u_factors.at[0, :, pl.ds(mine * half, half)], u_here, sem)
    copy.start()
    list_tiles(owners, tile_of, held, count_col, 2 * half)
    times = lax.broadcasted_iota(jnp.int32, (NT, TS), 0)
    row_id = lax.broadcasted_iota(jnp.int32, (R, mask.shape[2]), 0)
    for s in range(half):
        tile = tile_of[column * 2 * half + mine * half + s]
        inside = jnp.where(times < onsets[tile], 1.0, 0.0).astype(jnp.bfloat16)
        tables = dot(table[mine], inside, 1, 0)
        count = tables.shape[0] // 3
        mixing[s] = tables[:count] + tables[count : 2 * count] + tables[2 * count :]
        pieces = [jnp.where(row_id < ranks[tile, j], 1.0, 0.0) for j in range(mask.shape[1] // R)]
        mask[s] = jnp.concatenate(pieces, axis=0).astype(jnp.bfloat16)
    copy.wait()


def prepare(count_col, half, columns, owners, tile_ranks, onsets, table, u_factors):
    shape = (2, half) + u_factors.shape[3:]
    vmem = pl.BlockSpec(memory_space=pltpu.VMEM)
    return pl.pallas_call(
        functools.partial(prepare_kernel, count_col, half),
        in_specs=[pl.BlockSpec(memory_space=pltpu.SMEM)] * 2 + [vmem, vmem, pl.BlockSpec(memory_space=pl.ANY)],
        out_specs=[vmem, vmem, vmem],
        out_shape=[
            jax.ShapeDtypeStruct(shape, jnp.bfloat16),
            jax.ShapeDtypeStruct((half, table.shape[1] // 3, TS), jnp.float32),
            jax.ShapeDtypeStruct((half, shape[2], columns), jnp.bfloat16),
        ],
        scratch_shapes=[
            pltpu.SMEM((count_col * 2 * half,), jnp.int32),
            pltpu.SMEM((count_col,), jnp.int32),
            pltpu.SemaphoreType.DMA,
        ],
        compiler_params=pltpu.CompilerParams(vmem_limit_bytes=40 * 2**20),
        cost_estimate=pl.CostEstimate(flops=0, bytes_accessed=4 * int(np.prod(shape)), transcendentals=0),
        name="prepare",
    )(owners, tile_ranks, onsets, table, u_factors)


def stack_coefficients(column, arrived, vis, slot, mask, matrix):
    strip = arrived[0].shape[1]
    for d, ref in enumerate(arrived):
        start = pl.multiple_of((column ^ d) * strip, strip)
        values = ref[slot] * mask[slot, pl.ds(start, strip), :]
        matrix[0, pl.ds(start, strip), :] = values
        matrix[1, pl.ds(start, strip), :] = jnp.concatenate([-values[:, vis:], values[:, :vis]], axis=1)


def own_field_kernel(count_col, half, mask, u_own, *refs):
    arrived = refs[:count_col]
    field, coefs = refs[count_col:]
    column = lax.axis_index("col")
    rows, columns = coefs.shape[2:]
    for s in range(half):
        stack_coefficients(column, arrived, columns // 2, s, mask, coefs.at[s])
        factors = u_own[:, s].reshape(2 * rows, TS)
        field[s] = dot(coefs[s].reshape(2 * rows, columns), factors, 0, 0).astype(jnp.bfloat16)


def own_field(count_col, half, mask, u_own, arrived):
    columns = arrived[0].shape[2]
    rows = u_own.shape[2]
    vmem = pl.BlockSpec(memory_space=pltpu.VMEM)
    return pl.pallas_call(
        functools.partial(own_field_kernel, count_col, half),
        in_specs=[vmem] * (2 + count_col),
        out_specs=vmem,
        out_shape=jax.ShapeDtypeStruct((half, columns, TS), jnp.bfloat16),
        scratch_shapes=[pltpu.VMEM((half, 2, rows, columns), jnp.bfloat16)],
        compiler_params=pltpu.CompilerParams(vmem_limit_bytes=20 * 2**20),
        cost_estimate=pl.CostEstimate(
            flops=4 * half * rows * columns * TS, bytes_accessed=2 * half * rows * TS, transcendentals=0
        ),
        name="own_field",
    )(mask, u_own, *arrived)


def copy_quarters(pieces, half_place, turn, matrix, sems):
    copies = []
    quarter = matrix.shape[2] // 2
    for n in range(2):
        start = (turn ^ n) * quarter
        for cut in range(len(pieces) // 2):
            ref = pieces[cut * 2 + n]
            at = pl.ds(pl.multiple_of(start, 16), ref.shape[2])
            copies.append(pltpu.make_async_copy(ref, matrix.at[:, :, at, :], sems.at[cut * 2 + n]))
            copies[-1].start()
            start = start + ref.shape[2]
    return copies


def stack_other(column, arrived, mask, slot, coefs):
    strip, columns = arrived[0].shape[1:]
    vis = columns // 2
    for d, ref in enumerate(arrived):
        values = ref[slot] * mask[slot, pl.ds(pl.multiple_of((column ^ d) * strip, strip), strip), :]
        coefs[0, column ^ d] = values
        coefs[1, column ^ d] = jnp.concatenate([-values[:, vis:], values[:, :vis]], axis=1)


def other_field(coefs, half_place, matrix):
    rows, width = matrix.shape[1:]
    left = coefs[:, pl.ds(2 * half_place, 2)].reshape(2 * rows, coefs.shape[3])
    return dot(left, matrix.reshape(2 * rows, width), 0, 0)


def near_kernel(count_col, half, mask, *refs):
    arrived = refs[:count_col]
    pieces = refs[count_col:-4]
    near, partial, coefs, sems = refs[-4:]
    column = lax.axis_index("col")
    group = lax.axis_index("grp")
    copies = copy_quarters(pieces, group, lax.axis_index("rep"), near, sems)
    for s in range(half):
        stack_other(column, arrived, mask, s, coefs.at[s])
    for copy in copies:
        copy.wait()
    for s in range(half):
        partial[s] = other_field(coefs.at[s], group, near[:, s])


def near_products(count_col, half, mask, arrived, pieces):
    strip, columns = arrived[0].shape[1:]
    vmem = pl.BlockSpec(memory_space=pltpu.VMEM)
    return pl.pallas_call(
        functools.partial(near_kernel, count_col, half),
        in_specs=[vmem] * (1 + count_col + len(pieces)),
        out_specs=[vmem] * 2,
        out_shape=[
            jax.ShapeDtypeStruct((2, half, 2 * strip, TS), jnp.bfloat16),
            jax.ShapeDtypeStruct((half, columns, TS), jnp.float32),
        ],
        scratch_shapes=[
            pltpu.VMEM((half, 2, count_col, strip, columns), jnp.bfloat16),
            pltpu.SemaphoreType.DMA((len(pieces),)),
        ],
        compiler_params=pltpu.CompilerParams(vmem_limit_bytes=16 * 2**20),
        cost_estimate=pl.CostEstimate(
            flops=8 * half * strip * columns * TS, bytes_accessed=8 * half * strip * TS, transcendentals=0
        ),
        name="near_products",
    )(mask, *arrived, *pieces)


def receiver_kernel(count_col, half, mask, mixing, own, u_own, near, partial, *refs):
    arrived = refs[:count_col]
    pieces = refs[count_col : -2 * count_col - 6]
    outs = refs[-2 * count_col - 6 : -6]
    far, coefs, field, windowed, adjoint, sems = refs[-6:]
    column = lax.axis_index("col")
    group = lax.axis_index("grp")
    strip, columns = arrived[0].shape[1:]
    rows = adjoint.shape[2]
    vis = columns // 2
    copies = copy_quarters(pieces, 1 - group, lax.axis_index("rep"), far, sems)
    for s in range(half):
        stack_other(column, arrived, mask, s, coefs.at[s])
    for copy in copies:
        copy.wait()
    for s in range(half):
        field[s] = (partial[s] + other_field(coefs.at[s], 1 - group, far[:, s])).astype(jnp.bfloat16)
    for s in range(half):
        high = 64
        for lane in range(0, TS, 128):
            at = pl.ds(lane, 128)
            mix = mixing[s, :, at]
            for row in range(0, vis, high):
                inputs = []
                for source in (own, field):
                    for part in range(2):
                        inputs.append(source[s, pl.ds(part * vis + row, high), at].astype(jnp.float32))
                for p in range(4):
                    total = mix[4 * p : 4 * p + 1] * inputs[0]
                    for q in range(1, 4):
                        total = total + mix[4 * p + q : 4 * p + q + 1] * inputs[q]
                    windowed[s, p // 2, pl.ds((p % 2) * vis + row, high), at] = total.astype(jnp.bfloat16)
        for e in range(2):
            parts = [(u_own, 0)] if e == 0 else [(near, group * 2 * strip), (far, (1 - group) * 2 * strip)]
            for factors, start in parts:
                here = factors.shape[2]
                back = dot(factors[:, s].reshape(2 * here, TS), windowed[s, e], 1, 1)
                by_real, by_imag = back[:here], back[here:]
                values = jnp.concatenate(
                    [by_real[:, :vis] + by_imag[:, vis:], by_real[:, vis:] - by_imag[:, :vis]], axis=1
                )
                at = pl.ds(start if e == 0 else pl.multiple_of(start, strip), here)
                adjoint[s, e, at, :] = values.astype(jnp.bfloat16) * mask[s, at, :]
            for d in range(count_col):
                start = pl.multiple_of((column ^ d) * strip, strip)
                outs[2 * d + e][s] = adjoint[s, e, pl.ds(start, strip), :]


def receiver_products(count_col, half, mask, mixing, own, arrived, u_own, near, partial, pieces):
    strip, columns = arrived[0].shape[1:]
    rows = u_own.shape[2]
    vmem = pl.BlockSpec(memory_space=pltpu.VMEM)
    out = jax.ShapeDtypeStruct((half, strip, columns), jnp.bfloat16)
    return pl.pallas_call(
        functools.partial(receiver_kernel, count_col, half),
        in_specs=[vmem] * (6 + count_col + len(pieces)),
        out_specs=[vmem] * (2 * count_col),
        out_shape=[out] * (2 * count_col),
        scratch_shapes=[
            pltpu.VMEM((2, half, 2 * strip, TS), jnp.bfloat16),
            pltpu.VMEM((half, 2, count_col, strip, columns), jnp.bfloat16),
            pltpu.VMEM((half, columns, TS), jnp.bfloat16),
            pltpu.VMEM((half, 2, columns, TS), jnp.bfloat16),
            pltpu.VMEM((half, 2, rows, columns), jnp.bfloat16),
            pltpu.SemaphoreType.DMA((len(pieces),)),
        ],
        compiler_params=pltpu.CompilerParams(vmem_limit_bytes=24 * 2**20),
        cost_estimate=pl.CostEstimate(
            flops=12 * half * rows * columns * TS, bytes_accessed=8 * half * rows * TS, transcendentals=0
        ),
        name="receiver_products",
    )(mask, mixing, own, u_own, near, partial, *arrived, *pieces)


def update_kernel(count_col, half, owners, *refs):
    arrivals = refs[: 2 * count_col]
    focus, factors, out, out_here, gathered, adjoint, tile_of, held, sems = refs[2 * count_col :]
    column = lax.axis_index("col")
    mine = lax.axis_index("freq")
    two, vis, sources = out_here.shape
    rows = factors.shape[1]
    blocks = sources // TS
    width = 512
    capacity = 2 * half
    list_tiles(owners, tile_of, held, count_col, capacity)
    def gather(j):
        for s in range(half):
            for d in range(count_col):
                for e in range(2):
                    tile = tile_of[(column ^ d) * capacity + (mine ^ e) * half + s]
                    values = arrivals[2 * d + e][s].astype(jnp.float32)
                    gathered[j, pl.ds(pl.multiple_of(tile * R, 8), R), :] = values[j * R : (j + 1) * R]
        values = gathered[j]
        adjoint[j, :rows] = values.astype(jnp.bfloat16)
        adjoint[j, rows:] = jnp.concatenate([values[:, vis:], -values[:, :vis]], axis=1).astype(jnp.bfloat16)

    writes = []
    for n in range(sources // width):
        j = n * width // TS
        at = pl.ds(n * width, width)
        if n * width % TS == 0:
            gather(j)
        right = factors[:, :, at].reshape(2 * rows, width)
        wave = dot(adjoint[j], right, 0, 0)
        out_here[:, :, at] = focus[:, :, at] - wave.reshape(two, vis, width)
        writes.append(pltpu.make_async_copy(out_here.at[:, :, at], out.at[0, :, :, at], sems.at[n]))
        writes[n].start()
    for write in writes:
        write.wait()


def update_products(count_col, half, owners, arrivals, focusing, v_factors):
    vis, sources = focusing.shape[1:]
    rows = v_factors.shape[1]
    blocks = sources // TS
    smem = pl.BlockSpec(memory_space=pltpu.SMEM)
    vmem = pl.BlockSpec(memory_space=pltpu.VMEM)
    anywhere = pl.BlockSpec(memory_space=pl.ANY)
    return pl.pallas_call(
        functools.partial(update_kernel, count_col, half),
        in_specs=[smem] + [vmem] * (len(arrivals) + 2),
        out_specs=anywhere,
        out_shape=jax.ShapeDtypeStruct((1,) + focusing.shape, jnp.float32),
        scratch_shapes=[
            pltpu.VMEM(focusing.shape, jnp.float32),
            pltpu.VMEM((blocks, rows, 2 * vis), jnp.float32),
            pltpu.VMEM((blocks, 2 * rows, 2 * vis), jnp.bfloat16),
            pltpu.SMEM((count_col * 2 * half,), jnp.int32),
            pltpu.SMEM((count_col,), jnp.int32),
            pltpu.SemaphoreType.DMA((sources // 512,)),
        ],
        compiler_params=pltpu.CompilerParams(vmem_limit_bytes=24 * 2**20),
        cost_estimate=pl.CostEstimate(
            flops=8 * rows * vis * sources, bytes_accessed=16 * vis * sources + 4 * rows * sources, transcendentals=0
        ),
        name="update_products",
    )(owners, *arrivals, focusing, v_factors)


def swap(array, axis):
    return lax.ppermute(array, axis, [(0, 1), (1, 0)])


def per_device_paired(focusing, v_factors, u_factors, tile_ranks, owners, onsets):
    count_col = lax.axis_size("col")
    mine = lax.axis_index("freq")
    capacity = u_factors.shape[2]
    half = capacity // 2
    rows = u_factors.shape[3]
    place = lax.axis_index("grp") * 2 + lax.axis_index("rep")
    table = jnp.asarray(mixing_table(2))
    tile_onsets = onsets.reshape(NR // TS, 1, TS)
    quarter = rows // 4
    cuts = (quarter // 2, quarter - quarter // 2)
    first = []
    share = lax.dynamic_slice(
        u_factors, (0, 0, (1 - mine) * half, place * quarter, 0), (1, 2, half, quarter, TS)
    ).reshape(2, half, quarter, TS)
    first = [swap(share[:, :, : cuts[0]], "freq"), swap(share[:, :, cuts[0] :], "freq")]
    *outgoing, focus_here, v_here = forward_products(count_col, half, focusing, v_factors, owners)
    def move(offset, payload):
        return lax.ppermute(payload, ("col", "freq"), [(i, i ^ offset) for i in range(2 * count_col)])
    arrived = list(outgoing)
    far, _ = lax.optimization_barrier((u_factors, outgoing[0]))
    u_here, mixing, mask = prepare(
        count_col, half, outgoing[0].shape[2], owners, tile_ranks, tile_onsets, table, far
    )
    first[0], _ = lax.optimization_barrier((first[0], outgoing[0]))
    second = [swap(first[0], "grp")]
    for offset in (4, 7, 2):
        arrived[offset] = move(offset, arrived[offset])
    held = lax.optimization_barrier(tuple(arrived + first + [u_here, mixing] + second))
    arrived, (*first, u_here, mixing, head) = list(held[: 2 * count_col]), held[2 * count_col :]
    second = [head, swap(first[1], "grp")]
    for offset in (5, 6, 3, 1):
        arrived[offset] = move(offset, arrived[offset])
    tied = lax.optimization_barrier(tuple(first + [arrived[n] for n in (5,)]))
    first = list(tied[:2])
    mates = [swap(piece, "rep") for piece in first]
    own = own_field(count_col, half, mask, u_here, arrived[::2])
    held = lax.optimization_barrier(tuple(arrived + first + second + [u_here, own]))
    arrived, (*pieces, u_here, own) = list(held[: 2 * count_col]), held[2 * count_col :]
    first, second = pieces[:2], pieces[2:4]
    near, partial = near_products(
        count_col, half, mask, arrived[1::2], [first[0], mates[0], first[1], mates[1]]
    )
    pieces = []
    for piece in second:
        pieces.extend([piece, swap(piece, "rep")])
    back = receiver_products(count_col, half, mask, mixing, own, arrived[1::2], u_here, near, partial, pieces)
    returned = list(back)
    for offset in (4, 5, 6, 7, 1):
        returned[offset] = move(offset, back[offset])
    *rest, returned[(4, 5, 6, 7, 1)[0]] = lax.optimization_barrier(tuple([back[n] for n in (2, 3)] + [returned[(4, 5, 6, 7, 1)[0]]]))
    for offset, payload in zip((2, 3), rest):
        returned[offset] = move(offset, payload)
    return update_products(count_col, half, owners, returned, focus_here, v_here)


def per_device(focusing, v_factors, u_factors, tile_ranks, owners, onsets):
    count_col = lax.axis_size("col")
    paired = (
        lax.axis_size("freq") == 2
        and lax.axis_size("grp") == 2
        and lax.axis_size("rep") == 2
        and focusing.shape[0] == 1
        and count_col == 4
        and u_factors.shape[2] % 2 == 0
        and u_factors.shape[2] * count_col == NR // TS
        and focusing.shape[2] % 128 == 0
        and focusing.shape[3] % TS == 0
        and (focusing.shape[3] // TS * R) % 16 == 0
        and u_factors.shape[3] % 64 == 0
    )
    chosen = per_device_paired if paired else per_device_general
    return chosen(focusing, v_factors, u_factors, tile_ranks, owners, onsets)


def solution(mesh):
    return jax.shard_map(
        per_device,
        mesh=mesh,
        in_specs=(
            P("freq", None, ("grp", "rep"), "col"),
            P("freq", None, None, "col"),
            P("freq", None, "col", None, None),
            P(),
            P(),
            P(),
        ),
        out_specs=P("freq", None, ("grp", "rep"), "col"),
        check_vma=False,
    )
```

```python
import functools

import jax
import jax.numpy as jnp
import ml_dtypes
import numpy as np
from jax import lax
from jax.experimental import pallas as pl
from jax.experimental.pallas import tpu as pltpu
from jax.sharding import PartitionSpec as P

TS = 1024
R = 24
NR = 16384
NS = 16384
NT = 512
KLO = 8


def window_tables(count_freq, onset_rows):
    time_steps = jnp.arange(NT, dtype=jnp.int32)
    freq_bins = KLO + jnp.arange(count_freq, dtype=jnp.int32)
    phases = 2.0 * jnp.pi * (freq_bins[None, :] * time_steps[:, None] % NT).astype(jnp.float32) / NT
    cosine = jnp.cos(phases)
    sines = jnp.sin(phases)
    analyse = jnp.stack([cosine, -sines], axis=2).reshape(NT, 2 * count_freq)
    synthesis = analyse * (2.0 / NT)
    product_table = (analyse[:, :, None] * synthesis[:, None, :]).reshape(
        NT, 4 * count_freq * count_freq
    )
    running_table = jnp.cumsum(product_table, axis=0)
    mixing = jnp.take(running_table, onset_rows - 1, axis=0)
    return mixing.reshape(-1, 2 * count_freq, 2 * count_freq)


def kernel_product(einsum_recipe, left_side, right_side):
    return jnp.einsum(einsum_recipe, left_side, right_side, preferred_element_type=jnp.float32)


def per_device_general(focusing, v_factors, u_factors, tile_ranks, owners, onsets):
    count_col = lax.axis_size("col")
    my_column = lax.axis_index("col")
    count_freq = lax.axis_size("freq")
    my_freq = lax.axis_index("freq")
    freq_dev = focusing.shape[0]
    vis_dev = focusing.shape[2]
    sources_dev = focusing.shape[3]
    capacity = u_factors.shape[2]
    block_width = min(sources_dev, TS)
    blocks_dev = sources_dev // block_width
    per_tile = TS // block_width
    all_blocks = count_col * blocks_dev
    row_tiles = NR // TS
    col_tiles = NS // TS
    freq_all = freq_dev * count_freq
    quarter = TS // count_freq
    tile_ids = jnp.arange(row_tiles, dtype=jnp.int32)
    same_owner = owners[:, None] == owners[None, :]
    earlier = tile_ids[None, :] < tile_ids[:, None]
    slot_of = jnp.sum((same_owner & earlier).astype(jnp.int32), axis=1)
    slot_ids = jnp.arange(capacity, dtype=jnp.int32)
    routing = (owners[None, None, :] == jnp.arange(count_col, dtype=jnp.int32)[:, None, None]) & (
        slot_of[None, None, :] == slot_ids[None, :, None]
    )
    lower_routing = routing.astype(jnp.bfloat16)
    my_slots = ((owners[None, :] == my_column) & (slot_of[None, :] == slot_ids[:, None])).astype(
        jnp.int32
    )
    slot_ranks = jnp.sum(my_slots[:, :, None] * tile_ranks[None, :, :], axis=1)
    rank_mask = (jnp.arange(R, dtype=jnp.int32)[None, None, :] < slot_ranks[:, :, None]).astype(
        jnp.float32
    )
    slot_onsets = jnp.sum(my_slots[:, :, None] * onsets.reshape(row_tiles, TS)[None], axis=1)
    slot_onsets = jnp.maximum(slot_onsets, 1)
    focus_low = focusing.astype(jnp.bfloat16).reshape(freq_dev, 2, vis_dev, blocks_dev, block_width)
    factors_v = v_factors.reshape(freq_dev, 2, row_tiles, R, blocks_dev, block_width)
    einsum_recipe = "fikbs,fvbs->ifbkv"
    real_portion = kernel_product(einsum_recipe, factors_v[:, 0], focus_low[:, 0]) - kernel_product(
        einsum_recipe, factors_v[:, 1], focus_low[:, 1]
    )
    part_imag = kernel_product(einsum_recipe, factors_v[:, 0], focus_low[:, 1]) + kernel_product(
        einsum_recipe, factors_v[:, 1], focus_low[:, 0]
    )
    partial_sums = jnp.stack([real_portion, part_imag], axis=3).astype(jnp.bfloat16)
    outgoing_parts = kernel_product("way,ymleno->amwleno", lower_routing, partial_sums).astype(
        jnp.bfloat16
    )
    outgoing_parts = outgoing_parts.reshape(capacity, freq_dev, all_blocks, 2, R, vis_dev)
    arrived = lax.all_to_all(outgoing_parts, "col", split_axis=2, concat_axis=2, tiled=True)
    coefficients = jnp.sum(
        arrived.astype(jnp.float32).reshape(capacity, freq_dev, col_tiles, per_tile, 2, R, vis_dev),
        axis=3,
    )
    coefficients = (coefficients * rank_mask[:, None, :, None, :, None]).astype(jnp.bfloat16)
    factors_u = u_factors.reshape(freq_dev, 2, capacity, col_tiles, R, TS)
    uform = "fcjka,cfjkv->cfav"
    field_real = kernel_product(uform, factors_u[:, 0], coefficients[:, :, :, 0]) - kernel_product(
        uform, factors_u[:, 1], coefficients[:, :, :, 1]
    )
    field_imag = kernel_product(uform, factors_u[:, 0], coefficients[:, :, :, 1]) + kernel_product(
        uform, factors_u[:, 1], coefficients[:, :, :, 0]
    )
    receiver_field = jnp.stack([field_real, field_imag], axis=2).astype(jnp.bfloat16)
    turned = lax.all_to_all(receiver_field, "freq", split_axis=3, concat_axis=1, tiled=True)
    quarter_onsets = lax.dynamic_slice_in_dim(slot_onsets, my_freq * quarter, quarter, 1)
    mixing = window_tables(freq_all, quarter_onsets.reshape(-1)).reshape(
        capacity, quarter, 2 * freq_all, 2 * freq_all
    )
    flat_field = turned.reshape(capacity, 2 * freq_all, quarter, vis_dev).astype(jnp.float32)
    mixed_field = jnp.einsum("crpq,cqrv->cprv", mixing, flat_field, precision=lax.Precision.HIGHEST)
    mixed_field = mixed_field.astype(jnp.bfloat16).reshape(capacity, freq_all, 2, quarter, vis_dev)
    windowed = lax.all_to_all(mixed_field, "freq", split_axis=1, concat_axis=3, tiled=True)
    aform = "fcjka,cfav->cfjkv"
    back_real = kernel_product(aform, factors_u[:, 0], windowed[:, :, 0]) + kernel_product(
        aform, factors_u[:, 1], windowed[:, :, 1]
    )
    back_imag = kernel_product(aform, factors_u[:, 0], windowed[:, :, 1]) - kernel_product(
        aform, factors_u[:, 1], windowed[:, :, 0]
    )
    adjoint = jnp.stack([back_real, back_imag], axis=3) * rank_mask[:, None, :, None, :, None]
    adjoint = adjoint.astype(jnp.bfloat16)
    spread = jnp.broadcast_to(
        adjoint[:, :, :, None], (capacity, freq_dev, col_tiles, per_tile, 2, R, vis_dev)
    )
    spread = spread.reshape(capacity, freq_dev, all_blocks, 2, R, vis_dev)
    result_field = lax.all_to_all(spread, "col", split_axis=2, concat_axis=2, tiled=True)
    result_field = result_field.reshape(capacity, freq_dev, count_col, blocks_dev, 2, R, vis_dev)
    row_share = kernel_product("prq,rjpagwu->qjagwu", lower_routing, result_field).astype(
        jnp.bfloat16
    )
    wform = "fikbs,ifbkv->fvbs"
    wave_real = kernel_product(wform, factors_v[:, 0], row_share[:, :, :, 0]) + kernel_product(
        wform, factors_v[:, 1], row_share[:, :, :, 1]
    )
    wave_imag = kernel_product(wform, factors_v[:, 0], row_share[:, :, :, 1]) - kernel_product(
        wform, factors_v[:, 1], row_share[:, :, :, 0]
    )
    wave_field = jnp.stack([wave_real, wave_imag], axis=1).reshape(
        freq_dev, 2, vis_dev, sources_dev
    )
    return focusing - wave_field


def mixing_table(count_freq):
    time_steps = np.arange(NT)
    rows = []
    for mine in range(count_freq):
        bins = [KLO + mine] + [KLO + f for f in range(count_freq) if f != mine]
        phases = 2.0 * np.pi * ((np.array(bins)[:, None] * time_steps[None, :]) % NT) / NT
        analyse = np.stack([np.cos(phases), -np.sin(phases)], axis=1).reshape(2 * count_freq, NT)
        table = (analyse[:, None, :] * analyse[None, :, :] * (2.0 / NT)).reshape(-1, NT)
        rest = table.astype(np.float32)
        parts = []
        for _ in range(3):
            part = rest.astype(ml_dtypes.bfloat16)
            parts.append(part)
            rest = rest - part.astype(np.float32)
        rows.append(np.concatenate(parts, axis=0))
    return np.stack(rows)


def dot(left, right, left_dim, right_dim):
    return lax.dot_general(
        left, right, (((left_dim,), (right_dim,)), ((), ())), preferred_element_type=jnp.float32
    )


def list_tiles(owners, tile_of, held, count_col, capacity):
    for owner in range(count_col):
        held[owner] = 0
    for tile in range(owners.shape[0]):
        owner = owners[tile]
        slot = held[owner]
        tile_of[owner * capacity + slot] = tile
        held[owner] = slot + 1


def forward_kernel(count_col, half, owners_far, focus, factors, *refs):
    outs = refs[: 2 * count_col]
    focus_here, factors_here, sums, owners, tile_of, held, sems = refs[2 * count_col :]
    column = lax.axis_index("col")
    mine = lax.axis_index("freq")
    two, vis, sources = focus_here.shape
    blocks = sources // TS
    copies = []
    for j in range(blocks):
        at = pl.ds(j * TS, TS)
        copies.append(
            [
                pltpu.make_async_copy(focus.at[0, :, :, at], focus_here.at[:, :, at], sems.at[0, j]),
                pltpu.make_async_copy(factors.at[0, :, :, at], factors_here.at[:, :, at], sems.at[1, j]),
            ]
        )
        for copy in copies[j]:
            copy.start()
    owners_copy = pltpu.make_async_copy(owners_far, owners, sems.at[2, 0])
    owners_copy.start()
    owners_copy.wait()
    capacity = 2 * half
    list_tiles(owners, tile_of, held, count_col, capacity)
    for j in range(blocks):
        for copy in copies[j]:
            copy.wait()
        at = pl.ds(j * TS, TS)
        low = focus_here[:, :, at].astype(jnp.bfloat16).reshape(two * vis, TS)
        by_real = dot(factors_here[0, :, at], low, 1, 1)
        by_imag = dot(factors_here[1, :, at], low, 1, 1)
        sums[j, :, :vis] = by_real[:, :vis] - by_imag[:, vis:]
        sums[j, :, vis:] = by_real[:, vis:] + by_imag[:, :vis]
    for d in range(count_col):
        for e in range(2):
            for s in range(half):
                tile = tile_of[(column ^ d) * capacity + (mine ^ e) * half + s]
                at = pl.ds(pl.multiple_of(tile * R, 8), R)
                pieces = [sums[j, at, :] for j in range(blocks)]
                outs[2 * d + e][s] = jnp.concatenate(pieces, axis=0).astype(jnp.bfloat16)


def forward_products(count_col, half, focusing, v_factors, owners):
    vis, sources = focusing.shape[2:]
    rows = v_factors.shape[2]
    blocks = sources // TS
    out = jax.ShapeDtypeStruct((half, blocks * R, 2 * vis), jnp.bfloat16)
    vmem = pl.BlockSpec(memory_space=pltpu.VMEM)
    anywhere = pl.BlockSpec(memory_space=pl.ANY)
    return pl.pallas_call(
        functools.partial(forward_kernel, count_col, half),
        in_specs=[anywhere] * 3,
        out_specs=[vmem] * (2 * count_col + 2),
        out_shape=[out] * (2 * count_col)
        + [
            jax.ShapeDtypeStruct(focusing.shape[1:], jnp.float32),
            jax.ShapeDtypeStruct(v_factors.shape[1:], jnp.bfloat16),
        ],
        scratch_shapes=[
            pltpu.VMEM((blocks, rows, 2 * vis), jnp.float32),
            pltpu.SMEM(owners.shape, jnp.int32),
            pltpu.SMEM((count_col * 2 * half,), jnp.int32),
            pltpu.SMEM((count_col,), jnp.int32),
            pltpu.SemaphoreType.DMA((3, blocks)),
        ],
        compiler_params=pltpu.CompilerParams(vmem_limit_bytes=46 * 2**20),
        cost_estimate=pl.CostEstimate(
            flops=8 * rows * vis * sources, bytes_accessed=8 * vis * sources + 4 * rows * sources, transcendentals=0
        ),
        name="forward_products",
    )(owners, focusing, v_factors)


def prepare_kernel(count_col, half, owners, ranks, onsets, table, u_factors, u_here, mixing, mask, tile_of, held, sem):
    column = lax.axis_index("col")
    mine = lax.axis_index("freq")
    copy = pltpu.make_async_copy(u_factors.at[0, :, pl.ds(mine * half, half)], u_here, sem)
    copy.start()
    list_tiles(owners, tile_of, held, count_col, 2 * half)
    times = lax.broadcasted_iota(jnp.int32, (NT, TS), 0)
    row_id = lax.broadcasted_iota(jnp.int32, (R, mask.shape[2]), 0)
    for s in range(half):
        tile = tile_of[column * 2 * half + mine * half + s]
        inside = jnp.where(times < onsets[tile], 1.0, 0.0).astype(jnp.bfloat16)
        tables = dot(table[mine], inside, 1, 0)
        count = tables.shape[0] // 3
        mixing[s] = tables[:count] + tables[count : 2 * count] + tables[2 * count :]
        pieces = [jnp.where(row_id < ranks[tile, j], 1.0, 0.0) for j in range(mask.shape[1] // R)]
        mask[s] = jnp.concatenate(pieces, axis=0).astype(jnp.bfloat16)
    copy.wait()


def prepare(count_col, half, columns, owners, tile_ranks, onsets, table, u_factors):
    shape = (2, half) + u_factors.shape[3:]
    vmem = pl.BlockSpec(memory_space=pltpu.VMEM)
    return pl.pallas_call(
        functools.partial(prepare_kernel, count_col, half),
        in_specs=[pl.BlockSpec(memory_space=pltpu.SMEM)] * 2 + [vmem, vmem, pl.BlockSpec(memory_space=pl.ANY)],
        out_specs=[vmem, vmem, vmem],
        out_shape=[
            jax.ShapeDtypeStruct(shape, jnp.bfloat16),
            jax.ShapeDtypeStruct((half, table.shape[1] // 3, TS), jnp.float32),
            jax.ShapeDtypeStruct((half, shape[2], columns), jnp.bfloat16),
        ],
        scratch_shapes=[
            pltpu.SMEM((count_col * 2 * half,), jnp.int32),
            pltpu.SMEM((count_col,), jnp.int32),
            pltpu.SemaphoreType.DMA,
        ],
        compiler_params=pltpu.CompilerParams(vmem_limit_bytes=40 * 2**20),
        cost_estimate=pl.CostEstimate(flops=0, bytes_accessed=4 * int(np.prod(shape)), transcendentals=0),
        name="prepare",
    )(owners, tile_ranks, onsets, table, u_factors)


def stack_coefficients(column, arrived, vis, slot, mask, matrix):
    strip = arrived[0].shape[1]
    for d, ref in enumerate(arrived):
        start = pl.multiple_of((column ^ d) * strip, strip)
        values = ref[slot] * mask[slot, pl.ds(start, strip), :]
        matrix[0, pl.ds(start, strip), :] = values
        matrix[1, pl.ds(start, strip), :] = jnp.concatenate([-values[:, vis:], values[:, :vis]], axis=1)


def own_field_kernel(count_col, half, mask, u_own, *refs):
    arrived = refs[:count_col]
    field, coefs = refs[count_col:]
    column = lax.axis_index("col")
    rows, columns = coefs.shape[2:]
    for s in range(half):
        stack_coefficients(column, arrived, columns // 2, s, mask, coefs.at[s])
        factors = u_own[:, s].reshape(2 * rows, TS)
        field[s] = dot(coefs[s].reshape(2 * rows, columns), factors, 0, 0).astype(jnp.bfloat16)


def own_field(count_col, half, mask, u_own, arrived):
    columns = arrived[0].shape[2]
    rows = u_own.shape[2]
    vmem = pl.BlockSpec(memory_space=pltpu.VMEM)
    return pl.pallas_call(
        functools.partial(own_field_kernel, count_col, half),
        in_specs=[vmem] * (2 + count_col),
        out_specs=vmem,
        out_shape=jax.ShapeDtypeStruct((half, columns, TS), jnp.bfloat16),
        scratch_shapes=[pltpu.VMEM((half, 2, rows, columns), jnp.bfloat16)],
        compiler_params=pltpu.CompilerParams(vmem_limit_bytes=20 * 2**20),
        cost_estimate=pl.CostEstimate(
            flops=4 * half * rows * columns * TS, bytes_accessed=2 * half * rows * TS, transcendentals=0
        ),
        name="own_field",
    )(mask, u_own, *arrived)


def copy_quarters(pieces, half_place, turn, matrix, sems):
    copies = []
    quarter = matrix.shape[2] // 2
    for n in range(2):
        start = (turn ^ n) * quarter
        for cut in range(len(pieces) // 2):
            ref = pieces[cut * 2 + n]
            at = pl.ds(pl.multiple_of(start, 16), ref.shape[2])
            copies.append(pltpu.make_async_copy(ref, matrix.at[:, :, at, :], sems.at[cut * 2 + n]))
            copies[-1].start()
            start = start + ref.shape[2]
    return copies


def stack_other(column, arrived, mask, slot, coefs):
    strip, columns = arrived[0].shape[1:]
    vis = columns // 2
    for d, ref in enumerate(arrived):
        values = ref[slot] * mask[slot, pl.ds(pl.multiple_of((column ^ d) * strip, strip), strip), :]
        coefs[0, column ^ d] = values
        coefs[1, column ^ d] = jnp.concatenate([-values[:, vis:], values[:, :vis]], axis=1)


def other_field(coefs, half_place, matrix):
    rows, width = matrix.shape[1:]
    left = coefs[:, pl.ds(2 * half_place, 2)].reshape(2 * rows, coefs.shape[3])
    return dot(left, matrix.reshape(2 * rows, width), 0, 0)


def near_kernel(count_col, half, mask, *refs):
    arrived = refs[:count_col]
    pieces = refs[count_col:-4]
    near, partial, coefs, sems = refs[-4:]
    column = lax.axis_index("col")
    group = lax.axis_index("grp")
    copies = copy_quarters(pieces, group, lax.axis_index("rep"), near, sems)
    for s in range(half):
        stack_other(column, arrived, mask, s, coefs.at[s])
    for copy in copies:
        copy.wait()
    for s in range(half):
        partial[s] = other_field(coefs.at[s], group, near[:, s])


def near_products(count_col, half, mask, arrived, pieces):
    strip, columns = arrived[0].shape[1:]
    vmem = pl.BlockSpec(memory_space=pltpu.VMEM)
    return pl.pallas_call(
        functools.partial(near_kernel, count_col, half),
        in_specs=[vmem] * (1 + count_col + len(pieces)),
        out_specs=[vmem] * 2,
        out_shape=[
            jax.ShapeDtypeStruct((2, half, 2 * strip, TS), jnp.bfloat16),
            jax.ShapeDtypeStruct((half, columns, TS), jnp.float32),
        ],
        scratch_shapes=[
            pltpu.VMEM((half, 2, count_col, strip, columns), jnp.bfloat16),
            pltpu.SemaphoreType.DMA((len(pieces),)),
        ],
        compiler_params=pltpu.CompilerParams(vmem_limit_bytes=16 * 2**20),
        cost_estimate=pl.CostEstimate(
            flops=8 * half * strip * columns * TS, bytes_accessed=8 * half * strip * TS, transcendentals=0
        ),
        name="near_products",
    )(mask, *arrived, *pieces)


def receiver_kernel(count_col, half, mask, mixing, own, u_own, near, partial, *refs):
    arrived = refs[:count_col]
    pieces = refs[count_col : -2 * count_col - 6]
    outs = refs[-2 * count_col - 6 : -6]
    far, coefs, field, windowed, adjoint, sems = refs[-6:]
    column = lax.axis_index("col")
    group = lax.axis_index("grp")
    strip, columns = arrived[0].shape[1:]
    rows = adjoint.shape[2]
    vis = columns // 2
    copies = copy_quarters(pieces, 1 - group, lax.axis_index("rep"), far, sems)
    for s in range(half):
        stack_other(column, arrived, mask, s, coefs.at[s])
    for copy in copies:
        copy.wait()
    for s in range(half):
        field[s] = (partial[s] + other_field(coefs.at[s], 1 - group, far[:, s])).astype(jnp.bfloat16)
    for s in range(half):
        high = 64
        for lane in range(0, TS, 128):
            at = pl.ds(lane, 128)
            mix = mixing[s, :, at]
            for row in range(0, vis, high):
                inputs = []
                for source in (own, field):
                    for part in range(2):
                        inputs.append(source[s, pl.ds(part * vis + row, high), at].astype(jnp.float32))
                for p in range(4):
                    total = mix[4 * p : 4 * p + 1] * inputs[0]
                    for q in range(1, 4):
                        total = total + mix[4 * p + q : 4 * p + q + 1] * inputs[q]
                    windowed[s, p // 2, pl.ds((p % 2) * vis + row, high), at] = total.astype(jnp.bfloat16)
        for e in range(2):
            parts = [(u_own, 0)] if e == 0 else [(near, group * 2 * strip), (far, (1 - group) * 2 * strip)]
            for factors, start in parts:
                here = factors.shape[2]
                back = dot(factors[:, s].reshape(2 * here, TS), windowed[s, e], 1, 1)
                by_real, by_imag = back[:here], back[here:]
                values = jnp.concatenate(
                    [by_real[:, :vis] + by_imag[:, vis:], by_real[:, vis:] - by_imag[:, :vis]], axis=1
                )
                at = pl.ds(start if e == 0 else pl.multiple_of(start, strip), here)
                adjoint[s, e, at, :] = values.astype(jnp.bfloat16) * mask[s, at, :]
            for d in range(count_col):
                start = pl.multiple_of((column ^ d) * strip, strip)
                outs[2 * d + e][s] = adjoint[s, e, pl.ds(start, strip), :]


def receiver_products(count_col, half, mask, mixing, own, arrived, u_own, near, partial, pieces):
    strip, columns = arrived[0].shape[1:]
    rows = u_own.shape[2]
    vmem = pl.BlockSpec(memory_space=pltpu.VMEM)
    out = jax.ShapeDtypeStruct((half, strip, columns), jnp.bfloat16)
    return pl.pallas_call(
        functools.partial(receiver_kernel, count_col, half),
        in_specs=[vmem] * (6 + count_col + len(pieces)),
        out_specs=[vmem] * (2 * count_col),
        out_shape=[out] * (2 * count_col),
        scratch_shapes=[
            pltpu.VMEM((2, half, 2 * strip, TS), jnp.bfloat16),
            pltpu.VMEM((half, 2, count_col, strip, columns), jnp.bfloat16),
            pltpu.VMEM((half, columns, TS), jnp.bfloat16),
            pltpu.VMEM((half, 2, columns, TS), jnp.bfloat16),
            pltpu.VMEM((half, 2, rows, columns), jnp.bfloat16),
            pltpu.SemaphoreType.DMA((len(pieces),)),
        ],
        compiler_params=pltpu.CompilerParams(vmem_limit_bytes=24 * 2**20),
        cost_estimate=pl.CostEstimate(
            flops=12 * half * rows * columns * TS, bytes_accessed=8 * half * rows * TS, transcendentals=0
        ),
        name="receiver_products",
    )(mask, mixing, own, u_own, near, partial, *arrived, *pieces)


def update_kernel(count_col, half, owners, *refs):
    arrivals = refs[: 2 * count_col]
    focus, factors, out, out_here, gathered, adjoint, tile_of, held, sems = refs[2 * count_col :]
    column = lax.axis_index("col")
    mine = lax.axis_index("freq")
    two, vis, sources = out_here.shape
    rows = factors.shape[1]
    blocks = sources // TS
    width = 512
    capacity = 2 * half
    list_tiles(owners, tile_of, held, count_col, capacity)
    def gather(j):
        for s in range(half):
            for d in range(count_col):
                for e in range(2):
                    tile = tile_of[(column ^ d) * capacity + (mine ^ e) * half + s]
                    values = arrivals[2 * d + e][s].astype(jnp.float32)
                    gathered[j, pl.ds(pl.multiple_of(tile * R, 8), R), :] = values[j * R : (j + 1) * R]
        values = gathered[j]
        adjoint[j, :rows] = values.astype(jnp.bfloat16)
        adjoint[j, rows:] = jnp.concatenate([values[:, vis:], -values[:, :vis]], axis=1).astype(jnp.bfloat16)

    writes = []
    for n in range(sources // width):
        j = n * width // TS
        at = pl.ds(n * width, width)
        if n * width % TS == 0:
            gather(j)
        right = factors[:, :, at].reshape(2 * rows, width)
        wave = dot(adjoint[j], right, 0, 0)
        out_here[:, :, at] = focus[:, :, at] - wave.reshape(two, vis, width)
        writes.append(pltpu.make_async_copy(out_here.at[:, :, at], out.at[0, :, :, at], sems.at[n]))
        writes[n].start()
    for write in writes:
        write.wait()


def update_products(count_col, half, owners, arrivals, focusing, v_factors):
    vis, sources = focusing.shape[1:]
    rows = v_factors.shape[1]
    blocks = sources // TS
    smem = pl.BlockSpec(memory_space=pltpu.SMEM)
    vmem = pl.BlockSpec(memory_space=pltpu.VMEM)
    anywhere = pl.BlockSpec(memory_space=pl.ANY)
    return pl.pallas_call(
        functools.partial(update_kernel, count_col, half),
        in_specs=[smem] + [vmem] * (len(arrivals) + 2),
        out_specs=anywhere,
        out_shape=jax.ShapeDtypeStruct((1,) + focusing.shape, jnp.float32),
        scratch_shapes=[
            pltpu.VMEM(focusing.shape, jnp.float32),
            pltpu.VMEM((blocks, rows, 2 * vis), jnp.float32),
            pltpu.VMEM((blocks, 2 * rows, 2 * vis), jnp.bfloat16),
            pltpu.SMEM((count_col * 2 * half,), jnp.int32),
            pltpu.SMEM((count_col,), jnp.int32),
            pltpu.SemaphoreType.DMA((sources // 512,)),
        ],
        compiler_params=pltpu.CompilerParams(vmem_limit_bytes=24 * 2**20),
        cost_estimate=pl.CostEstimate(
            flops=8 * rows * vis * sources, bytes_accessed=16 * vis * sources + 4 * rows * sources, transcendentals=0
        ),
        name="update_products",
    )(owners, *arrivals, focusing, v_factors)


def swap(array, axis):
    return lax.ppermute(array, axis, [(0, 1), (1, 0)])


def exchange(arrays, count_col):
    moved = list(arrays)
    for d in range(count_col - 1, -1, -1):
        for e in (1, 0):
            offset = 2 * d + e
            if offset:
                moved[offset] = lax.ppermute(
                    arrays[offset], ("col", "freq"), [(i, i ^ offset) for i in range(2 * count_col)]
                )
    return moved


def per_device_paired(focusing, v_factors, u_factors, tile_ranks, owners, onsets):
    count_col = lax.axis_size("col")
    mine = lax.axis_index("freq")
    capacity = u_factors.shape[2]
    half = capacity // 2
    rows = u_factors.shape[3]
    place = lax.axis_index("grp") * 2 + lax.axis_index("rep")
    table = jnp.asarray(mixing_table(2))
    tile_onsets = onsets.reshape(NR // TS, 1, TS)
    quarter = rows // 4
    cuts = (quarter // 2, quarter - quarter // 2)
    first = []
    share = lax.dynamic_slice(
        u_factors, (0, 0, (1 - mine) * half, place * quarter, 0), (1, 2, half, quarter, TS)
    ).reshape(2, half, quarter, TS)
    first = [swap(share[:, :, : cuts[0]], "freq"), swap(share[:, :, cuts[0] :], "freq")]
    *outgoing, focus_here, v_here = forward_products(count_col, half, focusing, v_factors, owners)
    def move(offset, payload):
        return lax.ppermute(payload, ("col", "freq"), [(i, i ^ offset) for i in range(2 * count_col)])
    arrived = list(outgoing)
    far, _ = lax.optimization_barrier((u_factors, outgoing[0]))
    u_here, mixing, mask = prepare(
        count_col, half, outgoing[0].shape[2], owners, tile_ranks, tile_onsets, table, far
    )
    first[0], _ = lax.optimization_barrier((first[0], outgoing[0]))
    second = [swap(first[0], "grp")]
    for offset in (4, 7, 2):
        arrived[offset] = move(offset, arrived[offset])
    held = lax.optimization_barrier(tuple(arrived + first + [u_here, mixing] + second))
    arrived, (*first, u_here, mixing, head) = list(held[: 2 * count_col]), held[2 * count_col :]
    second = [head, swap(first[1], "grp")]
    for offset in (5, 6, 3, 1):
        arrived[offset] = move(offset, arrived[offset])
    first[0], _ = lax.optimization_barrier((first[0], arrived[5]))
    first[1], _ = lax.optimization_barrier((first[1], arrived[1]))
    mates = [swap(piece, "rep") for piece in first]
    own = own_field(count_col, half, mask, u_here, arrived[::2])
    held = lax.optimization_barrier(tuple(arrived + first + second + [u_here, own]))
    arrived, (*pieces, u_here, own) = list(held[: 2 * count_col]), held[2 * count_col :]
    first, second = pieces[:2], pieces[2:4]
    near, partial = near_products(
        count_col, half, mask, arrived[1::2], [first[0], mates[0], first[1], mates[1]]
    )
    pieces = []
    for piece in second:
        pieces.extend([piece, swap(piece, "rep")])
    back = receiver_products(count_col, half, mask, mixing, own, arrived[1::2], u_here, near, partial, pieces)
    returned = exchange(back, count_col)
    return update_products(count_col, half, owners, returned, focus_here, v_here)


def per_device(focusing, v_factors, u_factors, tile_ranks, owners, onsets):
    count_col = lax.axis_size("col")
    paired = (
        lax.axis_size("freq") == 2
        and lax.axis_size("grp") == 2
        and lax.axis_size("rep") == 2
        and focusing.shape[0] == 1
        and count_col == 4
        and u_factors.shape[2] % 2 == 0
        and u_factors.shape[2] * count_col == NR // TS
        and focusing.shape[2] % 128 == 0
        and focusing.shape[3] % TS == 0
        and (focusing.shape[3] // TS * R) % 16 == 0
        and u_factors.shape[3] % 64 == 0
    )
    chosen = per_device_paired if paired else per_device_general
    return chosen(focusing, v_factors, u_factors, tile_ranks, owners, onsets)


def solution(mesh):
    return jax.shard_map(
        per_device,
        mesh=mesh,
        in_specs=(
            P("freq", None, ("grp", "rep"), "col"),
            P("freq", None, None, "col"),
            P("freq", None, "col", None, None),
            P(),
            P(),
            P(),
        ),
        out_specs=P("freq", None, ("grp", "rep"), "col"),
        check_vma=False,
    )
```
